32 devices in a mesh: seq: 8 (over z, x), rep: 4 (over y, core).
Axes of the slice: x: 2, y: 2, z: 4, core: 2. Of those that a mesh axis runs over, the one named last changes fastest.
Arguments:
- start_deter: bfloat16 [64, 512], P(('seq', 'rep')), may hold values from -1 to 1
- post_cat: int32 [64, 64, 32], P(('seq', 'rep')), may hold values from 0 to 31
- embed: bfloat16 [64, 64, 4096], P(('seq', 'rep')), may hold values from -6 to 6
- camera: int32 [64], P(('seq', 'rep')), may hold values from 0 to 1
- start_order: int32 [32, 128], P(('seq', 'rep')), may hold values from 0 to 127, each once within a row
- imag_cat: int32 [2048, 14, 32], P(('seq', 'rep')), may hold values from 0 to 31
- imag_cot: bfloat16 [2048, 15, 512], P(('seq', 'rep')), may hold values from -6 to 6
- stoch_table: bfloat16 [1024, 512], replicated, may hold values from -1 to 1
- stoch_gain: float32 [512], replicated, may hold values from 0.1 to 1.9
- stoch_bias: float32 [512], replicated, may hold values from -3 to 3
- state_weight: bfloat16 [8, 64, 192], replicated, may hold values from -0.25 to 0.25
- input_weight: bfloat16 [512, 1536], replicated, may hold values from -0.25 to 0.25
- cell_gain: float32 [1536], replicated, may hold values from 0.1 to 1.9
- cell_bias: float32 [1536], replicated, may hold values from -3 to 3
- prior_hidden: bfloat16 [512, 512], replicated, may hold values from -0.25 to 0.25
- prior_gain: float32 [512], replicated, may hold values from 0.1 to 1.9
- prior_bias: float32 [512], replicated, may hold values from -3 to 3
- prior_out: bfloat16 [512, 1024], replicated, may hold values from -0.75 to 0.75
- prior_shift: float32 [1024], replicated, may hold values from -3 to 3
- post_deter: bfloat16 [512, 512], replicated, may hold values from -0.09375 to 0.09375
- post_embed: bfloat16 [4096, 512], replicated, may hold values from -0.09375 to 0.09375
- post_gain: float32 [512], replicated, may hold values from 0.1 to 1.9
- post_bias: float32 [512], replicated, may hold values from -3 to 3
- post_out: bfloat16 [512, 1024], replicated, may hold values from -0.75 to 0.75
- post_shift: float32 [1024], replicated, may hold values from -3 to 3
- camera_scale: float32 [2, 4096], replicated, may hold values from 0.1 to 1.9
Outputs:
- imag_deter: float32 [2048, 15, 512], P(('seq', 'rep'))
- embed_grad: float32 [64, 64, 4096], P(('seq', 'rep'))
- start_grad: float32 [64, 512], P(('seq', 'rep'))
- stoch_table_grad: float32 [1024, 512], P('rep')
- stoch_gain_grad: float32 [512], P('rep')
- stoch_bias_grad: float32 [512], P('rep')
- state_weight_grad: float32 [8, 64, 192], P('rep')
- input_weight_grad: float32 [512, 1536], P('rep')
- cell_gain_grad: float32 [1536], P('rep')
- cell_bias_grad: float32 [1536], P('rep')
- prior_hidden_grad: float32 [512, 512], P('rep')
- prior_gain_grad: float32 [512], P('rep')
- prior_bias_grad: float32 [512], P('rep')
- prior_out_grad: float32 [512, 1024], P('rep')
- prior_shift_grad: float32 [1024], P('rep')
- post_deter_grad: float32 [512, 512], P('rep')
- post_embed_grad: float32 [4096, 512], P('rep')
- post_gain_grad: float32 [512], P('rep')
- post_bias_grad: float32 [512], P('rep')
- post_out_grad: float32 [512, 1024], P('rep')
- post_shift_grad: float32 [1024], P('rep')
- camera_scale_grad: float32 [2, 4096], P(None, 'rep')
The draws below stay inside these ranges and needn't reach their ends.
Inputs may be any that keep to these rules, and one draw needn't show every extreme that they name: `start_order`: each row lists the frames 0 to 127 of one device once each.
All inputs are finite; a program needn't handle non-finite values.
Results may differ from the reference program's by a relative error of at most 0.0095.
Values may be sent and summed in bfloat16 or wider, within the bound.
No kernel may reach another device: no remote copies, remote signals or barrier semaphores. Data moves between devices by JAX's collectives and lax.ppermute only.
A program may use at most 320 MiB of HBM per device.

```python
import jax
import jax.numpy as jnp
from jax import lax

DETER = 512
UNITS = 512
BLOCKS = 8
GROUPS = 32
CLASSES = 32
EMB = 4096
CAMERAS = 2
HORIZON = 15
LEN = 64
SEQ_DEV = 2
BLOCK = 64
ROWS_DEV = 128
ROLL_DEV = 64
SEQS = 64
STARTS = 2048
N_SEQ = 8
N_REP = 4


def plant(drawn, rng, smallest, top_value):
    extent = drawn.shape
    index_at = [jax.random.randint(jax.random.fold_in(rng, axis), (), 0, extent[axis]) for axis in range(len(extent))]
    drawn = drawn.at[tuple(index_at)].set(smallest)
    longest = extent.index(max(extent))
    index_at[longest] = (index_at[longest] + 1) % extent[longest]
    return drawn.at[tuple(index_at)].set(top_value)


def block_scale(own_key, dims, cuts, least, top_value):
    loudness = 1.0
    for position, shards_of in cuts:
        steps = jax.random.uniform(jax.random.fold_in(jax.random.fold_in(own_key, 6), position), (shards_of,), jnp.float32, least / len(cuts), top_value / len(cuts))
        loudness = loudness * jnp.repeat(jnp.exp(steps), dims[position] // shards_of).reshape((-1,) + (1,) * (len(dims) - 1 - position))
    return loudness


def centred(own_key, shape, scale, most, cuts=(), kind=jnp.bfloat16):
    gain = block_scale(own_key, shape, cuts, -0.22, 0.18) if cuts else 1.0
    result = jax.random.normal(own_key, shape, jnp.float32) * scale * gain
    return jnp.minimum(jnp.maximum(result, -most), most).astype(kind)


def setup_inputs(seed: int = 0) -> dict:
    seeds = jax.random.split(jax.random.key(seed), 27)
    start_deter = jnp.clip(jax.random.uniform(seeds[0], (SEQS, DETER), jnp.float32, -1.0, 1.0) * block_scale(seeds[0], (SEQS, DETER), ((0, 32),), -0.4, 0.0), -1.0, 1.0).astype(jnp.bfloat16)
    post_cat = plant(jax.random.randint(seeds[1], (SEQS, LEN, GROUPS), 0, CLASSES), jax.random.fold_in(seeds[1], 1), 0, CLASSES - 1).astype(jnp.int32)
    embed = centred(seeds[2], (SEQS, LEN, EMB), 1.0, 6.0, ((0, 32),))
    camera = plant(jax.random.randint(seeds[3], (SEQS,), 0, CAMERAS), jax.random.fold_in(seeds[3], 1), 0, CAMERAS - 1).astype(jnp.int32)
    start_order = jax.vmap(lambda own: jax.random.permutation(own, ROWS_DEV))(jax.random.split(seeds[4], (N_SEQ * N_REP))).reshape((N_SEQ * N_REP, ROWS_DEV)).astype(jnp.int32)
    imag_cat = plant(jax.random.randint(seeds[5], (STARTS, HORIZON - 1, GROUPS), 0, CLASSES), jax.random.fold_in(seeds[5], 1), 0, CLASSES - 1).astype(jnp.int32)
    imag_cot = centred(seeds[6], (STARTS, HORIZON, DETER), 1.0, 6.0, ((0, 32),))
    stoch_table = centred(seeds[7], (GROUPS * CLASSES, UNITS), GROUPS ** -0.5, 1.0)
    stoch_gain = jnp.clip(1.0 + 0.18 * jax.random.normal(seeds[8], (UNITS,), jnp.float32), 0.1, 1.9)
    stoch_bias = centred(seeds[9], (UNITS,), 0.5, 3.0, (), jnp.float32)
    state_weight = centred(seeds[10], (BLOCKS, BLOCK, 3 * BLOCK), (BLOCK + UNITS) ** -0.5, 0.25)
    input_weight = centred(seeds[11], (UNITS, 3 * DETER), (BLOCK + UNITS) ** -0.5, 0.25)
    cell_gain = jnp.clip(1.0 + 0.18 * jax.random.normal(seeds[12], (3 * DETER,), jnp.float32), 0.1, 1.9)
    cell_bias = centred(seeds[13], (3 * DETER,), 0.5, 3.0, (), jnp.float32)
    prior_hidden = centred(seeds[14], (DETER, UNITS), DETER ** -0.5, 0.25)
    prior_gain = jnp.clip(1.0 + 0.18 * jax.random.normal(seeds[15], (UNITS,), jnp.float32), 0.1, 1.9)
    prior_bias = centred(seeds[16], (UNITS,), 0.5, 3.0, (), jnp.float32)
    prior_out = centred(seeds[17], (UNITS, GROUPS * CLASSES), (UNITS // 8) ** -0.5, 0.75)
    prior_shift = centred(seeds[18], (GROUPS * CLASSES,), 0.5, 3.0, (), jnp.float32)
    post_deter = centred(seeds[19], (DETER, UNITS), (DETER + EMB) ** -0.5, 0.09375)
    post_embed = centred(seeds[20], (EMB, UNITS), (DETER + EMB) ** -0.5, 0.09375)
    post_gain = jnp.clip(1.0 + 0.18 * jax.random.normal(seeds[21], (UNITS,), jnp.float32), 0.1, 1.9)
    post_bias = centred(seeds[22], (UNITS,), 0.5, 3.0, (), jnp.float32)
    post_out = centred(seeds[23], (UNITS, GROUPS * CLASSES), (UNITS // 8) ** -0.5, 0.75)
    post_shift = centred(seeds[24], (GROUPS * CLASSES,), 0.5, 3.0, (), jnp.float32)
    camera_scale = jnp.clip(1.0 + 0.18 * jax.random.normal(seeds[25], (CAMERAS, EMB), jnp.float32), 0.1, 1.9)
    return {"start_deter": start_deter, "post_cat": post_cat, "embed": embed, "camera": camera, "start_order": start_order, "imag_cat": imag_cat, "imag_cot": imag_cot, "stoch_table": stoch_table, "stoch_gain": stoch_gain, "stoch_bias": stoch_bias, "state_weight": state_weight, "input_weight": input_weight, "cell_gain": cell_gain, "cell_bias": cell_bias, "prior_hidden": prior_hidden, "prior_gain": prior_gain, "prior_bias": prior_bias, "prior_out": prior_out, "prior_shift": prior_shift, "post_deter": post_deter, "post_embed": post_embed, "post_gain": post_gain, "post_bias": post_bias, "post_out": post_out, "post_shift": post_shift, "camera_scale": camera_scale}


epsilon = 1e-05
unimix = 0.01
free_bits = 1.0
highest = lax.Precision.HIGHEST

@jax.custom_vjp
def low(v):
    return lax.optimization_barrier(v.astype(jnp.bfloat16)).astype(jnp.float32)

@jax.custom_vjp
def low_back(v):
    return v

def low_keep(v):
    return (low(v), None)

def low_pass(kept, grad):
    return (grad,)

def back_keep(v):
    return (v, None)

def back_low(kept, grad):
    return (low(grad),)
low.defvjp(low_keep, low_pass)
low_back.defvjp(back_keep, back_low)

def layer_norm(values, factor, offset):
    center = values - lax.optimization_barrier(jnp.mean(values, -1, keepdims=True))
    spread = lax.optimization_barrier(jnp.mean(center * center, -1, keepdims=True))
    return center * lax.rsqrt(spread + epsilon) * factor + offset

def norm_silu(values, factor, offset):
    return jax.nn.silu(layer_norm(values, factor, offset))

def gru_update(gate_values, previous, factor, offset):
    row_count = gate_values.shape[0]
    normed = layer_norm(gate_values, factor, offset).reshape(row_count, BLOCKS, 3, -1)
    reset_gate = jax.nn.sigmoid(normed[:, :, 0])
    candidate = jnp.tanh(reset_gate * normed[:, :, 1])
    update_gate = jax.nn.sigmoid(normed[:, :, 2] - 1.0)
    blocked = previous.reshape(row_count, BLOCKS, -1)
    return (update_gate * candidate + (1.0 - update_gate) * blocked).reshape(row_count, -1)

def mixed_probs(logits):
    row_count = logits.shape[0]
    probability = jax.nn.softmax(logits.reshape(row_count, GROUPS, -1), axis=-1)
    return (1.0 - unimix) * probability + unimix / probability.shape[-1]

def frame_losses(post_logits, prior_logits):
    posterior = mixed_probs(post_logits)
    prior_probs = mixed_probs(prior_logits)
    divergence = lax.optimization_barrier(jnp.sum(posterior * (jnp.log(posterior) - jnp.log(prior_probs)), axis=(1, 2)))
    return 1.0 + jax.nn.softplus(divergence - free_bits)

def reference(start_deter, post_cat, embed, camera, start_order, imag_cat, imag_cot, stoch_table, stoch_gain, stoch_bias, state_weight, input_weight, cell_gain, cell_bias, prior_hidden, prior_gain, prior_bias, prior_out, prior_shift, post_deter, post_embed, post_gain, post_bias, post_out, post_shift, camera_scale):

    def forward(start_f, embed_f, stoch_table, stoch_gain, stoch_bias, state_weight, input_weight, cell_gain, cell_bias, prior_hidden, prior_gain, prior_bias, prior_out, prior_shift, post_deter, post_embed, post_gain, post_bias, post_out, post_shift, camera_scale):

        def stoch_input(categories):
            lookup = stoch_table.reshape(GROUPS, CLASSES, -1)
            picked = lookup[jnp.arange(GROUPS, dtype=jnp.int32)[None, :], categories]
            return low(norm_silu(low_back(lax.optimization_barrier(jnp.sum(picked, axis=1))), stoch_gain, stoch_bias))

        def gates_of(held_state, taken_rows):
            row_count = held_state.shape[0]
            blocked = held_state.reshape(row_count, BLOCKS, -1)
            state_term = jnp.einsum('rbk,bkn->rbn', blocked, state_weight, precision=highest).reshape(row_count, -1)
            return low_back(state_term + jnp.dot(taken_rows, input_weight, precision=highest))
        scale_rows = camera_scale[camera]
        scaled = low(embed_f * scale_rows[:, None, :])

        def observe(carry, inputs):
            current, held_state, taken_rows = carry
            categories, scaled_now = inputs
            renewed = gru_update(gates_of(held_state, taken_rows), current, cell_gain, cell_bias)
            renewed_held = low(renewed)
            prior_pre = low_back(jnp.dot(renewed_held, prior_hidden, precision=highest))
            prior_act = low(norm_silu(prior_pre, prior_gain, prior_bias))
            prior_logits = low_back(jnp.dot(prior_act, prior_out, precision=highest) + prior_shift)
            post_pre = low_back(jnp.dot(renewed_held, post_deter, precision=highest) + jnp.dot(scaled_now, post_embed, precision=highest))
            post_act = low(norm_silu(post_pre, post_gain, post_bias))
            post_logits = low_back(jnp.dot(post_act, post_out, precision=highest) + post_shift)
            frame_sum = jnp.sum(frame_losses(post_logits, prior_logits))
            taken_new = stoch_input(categories)
            return ((renewed, renewed_held, taken_new), (renewed_held, taken_new, frame_sum))
        first = (start_f, low(start_f), jnp.zeros((SEQS, UNITS), jnp.float32))
        scanned = lax.scan(jax.checkpoint(observe), first, (jnp.swapaxes(post_cat, 0, 1), jnp.swapaxes(scaled, 0, 1)))
        held_all, taken_all, frame_sums = scanned[1]
        loss_total = jnp.sum(frame_sums)
        per_peer = ROLL_DEV // N_SEQ

        def arrange(frames):
            width_all = frames.shape[-1]
            per_device = jnp.swapaxes(frames, 0, 1).reshape(N_SEQ * N_REP, SEQ_DEV * LEN, width_all)
            picked = jnp.take_along_axis(per_device, start_order[:, :ROLL_DEV, None], axis=1)
            picked = picked.reshape(N_SEQ, N_REP, N_SEQ, per_peer, width_all)
            return jnp.transpose(picked, (2, 1, 0, 3, 4)).reshape(STARTS, width_all)
        first_held = low_back(arrange(held_all))
        first_taken = low_back(arrange(taken_all))
        block_rows = N_REP * ROLL_DEV
        block_count = STARTS // block_rows

        def rollout(inputs):
            held_first, taken_first, categories = inputs
            later = lax.map(stoch_input, jnp.swapaxes(categories, 0, 1))
            taken_steps = jnp.concatenate([taken_first[None], later], 0)

            def advance(current, taken_rows):
                renewed = gru_update(gates_of(low(current), taken_rows), current, cell_gain, cell_bias)
                return (renewed, renewed)
            states = lax.scan(advance, held_first, taken_steps)[1]
            return jnp.swapaxes(states, 0, 1)
        imagined = lax.map(jax.checkpoint(rollout), (first_held.reshape(block_count, block_rows, -1), first_taken.reshape(block_count, block_rows, -1), imag_cat.reshape(block_count, block_rows, HORIZON - 1, GROUPS)))
        return (imagined.reshape(STARTS, HORIZON, -1), loss_total)
    floats = (start_deter.astype(jnp.float32), embed.astype(jnp.float32), stoch_table.astype(jnp.float32), stoch_gain.astype(jnp.float32), stoch_bias.astype(jnp.float32), state_weight.astype(jnp.float32), input_weight.astype(jnp.float32), cell_gain.astype(jnp.float32), cell_bias.astype(jnp.float32), prior_hidden.astype(jnp.float32), prior_gain.astype(jnp.float32), prior_bias.astype(jnp.float32), prior_out.astype(jnp.float32), prior_shift.astype(jnp.float32), post_deter.astype(jnp.float32), post_embed.astype(jnp.float32), post_gain.astype(jnp.float32), post_bias.astype(jnp.float32), post_out.astype(jnp.float32), post_shift.astype(jnp.float32), camera_scale.astype(jnp.float32))
    outputs, pullback = jax.vjp(forward, *floats)
    grads = pullback((imag_cot.astype(jnp.float32), jnp.asarray(1.0, dtype=jnp.float32)))
    return (outputs[0], grads[1], grads[0], grads[2], grads[3], grads[4], grads[5], grads[6], grads[7], grads[8], grads[9], grads[10], grads[11], grads[12], grads[13], grads[14], grads[15], grads[16], grads[17], grads[18], grads[19], grads[20])
```

```python
import jax
import jax.numpy as jnp
from jax import lax
from jax.experimental import pallas as pl
from jax.experimental.pallas import tpu as pltpu
from jax.sharding import PartitionSpec as P

BLOCKS = 8
GROUPS = 32
CLASSES = 32
PAIRS = BLOCKS // 2
LANES = 128
GATE = 3 * LANES

epsilon = 1e-05
unimix = 0.01
free_bits = 1.0

f32 = jnp.float32
bf16 = jnp.bfloat16


def iota(shape, axis):
    return lax.broadcasted_iota(jnp.int32, shape, axis)


def mm(left, right):
    return jnp.dot(left, right, preferred_element_type=f32)


def mm_nt(left, right):
    return lax.dot_general(left, right, (((1,), (1,)), ((), ())), preferred_element_type=f32)


def mm_tn(left, right):
    return lax.dot_general(left, right, (((0,), (0,)), ((), ())), preferred_element_type=f32)


def sigmoid(values):
    return 0.5 * jnp.tanh(0.5 * values) + 0.5


def row_mean(values):
    return jnp.sum(values, -1, keepdims=True) * (1.0 / values.shape[-1])


def hot_rows(columns):
    categories = jnp.concatenate([part.astype(f32).T for part in columns], 0).astype(bf16)
    count = categories.shape[0]
    width = GROUPS * CLASSES
    spread = (iota((GROUPS, width), 1) // CLASSES == iota((GROUPS, width), 0)).astype(f32)
    wide = mm(categories, spread.astype(bf16))
    own = (iota((count, width), 1) % CLASSES).astype(f32)
    return jnp.where(wide == own, 1.0, 0.0).astype(bf16)


def normed(values):
    center = values - row_mean(values)
    scale = lax.rsqrt(row_mean(center * center) + epsilon)
    return center * scale, scale


def norm_silu(values, factor, offset):
    act = normed(values)[0] * factor + offset
    return act * sigmoid(act)


def norm_silu_back(values, factor, offset, grad):
    unit, scale = normed(values)
    act = unit * factor + offset
    gate = sigmoid(act)
    act_grad = grad * (gate + act * gate * (1.0 - gate))
    unit_grad = act_grad * factor
    pre_grad = scale * (unit_grad - row_mean(unit_grad) - unit * row_mean(unit_grad * unit))
    return (
        pre_grad,
        jnp.sum(act_grad * unit, 0, keepdims=True),
        jnp.sum(act_grad, 0, keepdims=True),
    )


def pick_columns(chosen, count):
    return jnp.where(iota((count, chosen.shape[1]), 0) == chosen, 1.0, 0.0).astype(bf16)


def column_order():
    source, target = iota((GATE, GATE), 0), iota((GATE, GATE), 1)
    half = LANES // 2
    moved = source // half % 3 * LANES + source // (3 * half) * half + source % half
    return jnp.where(moved == target, 1.0, 0.0).astype(bf16)


def pair_row(ref, pair):
    half = LANES // 2
    return jnp.concatenate(
        [
            ref[:, pair * GATE + (3 * e + p) * half : pair * GATE + (3 * e + p + 1) * half]
            for p in range(3)
            for e in range(2)
        ],
        1,
    )


def plain_row(row):
    half = LANES // 2
    return jnp.concatenate(
        [
            row[:, (2 * p + e) * half : (2 * p + e + 1) * half]
            for e in range(2)
            for p in range(3)
        ],
        1,
    )


def group_sum(values):
    values = values + pltpu.roll(values, 4, 0)
    return values + pltpu.roll(values, 2, 0)


def lanes_of(pair):
    return slice(pair * LANES, (pair + 1) * LANES)


def gates_of(pair):
    return slice(pair * GATE, (pair + 1) * GATE)


def scale_row(camera_ref, camera_scale_ref, s, columns):
    row = None
    for c in range(camera_scale_ref.shape[0]):
        part = jnp.where(camera_ref[s] == c, camera_scale_ref[c : c + 1, columns], 0.0)
        row = part if row is None else row + part
    return row


def observe_kernel(
    cat_ref,
    table_ref,
    stoch_gain_ref,
    stoch_bias_ref,
    input_ref,
    weight_ref,
    cell_gain_ref,
    cell_bias_ref,
    start_ref,
    order_ref,
    held_ref,
    taken_ref,
    pre_ref,
    gates_ref,
    states_ref,
    sent_ref,
    ordered_ref,
    state_ref,
    cell_ref,
    inputs_ref,
):
    frames, width = held_ref.shape
    length = frames // 2
    half = LANES // 2
    pre = mm(hot_rows([cat_ref[s] for s in range(2)]), table_ref[...])
    pre_ref[...] = pre
    taken = norm_silu(pre, stoch_gain_ref[...], stoch_bias_ref[...]).astype(bf16)
    taken_ref[...] = taken
    order = column_order()
    for pair in range(PAIRS):
        columns = mm(input_ref[:, gates_of(pair)], order).astype(bf16)
        ordered_ref[:, gates_of(pair)] = columns
        values = mm(taken, columns)
        for p in range(3):
            at = p * PAIRS * frames + pair * frames
            inputs_ref[at : at + frames, :] = values[:, lanes_of(p)]
    source, target = iota((3 * half, GATE), 0), iota((3 * half, GATE), 1)
    same = (source // half == target // LANES) & (source % half == target % half)
    weights = mm(weight_ref[...], jnp.where(same, 1.0, 0.0).astype(bf16))
    own = iota(weights.shape, 0) // half % 2 == iota(weights.shape, 1) // half % 2
    state_ref[...] = jnp.where(own, weights, 0.0).astype(bf16)
    gain_rows = [pair_row(cell_gain_ref, pair) for pair in range(PAIRS)]
    bias_rows = [pair_row(cell_bias_ref, pair) for pair in range(PAIRS)]
    cell_ref[...] = jnp.concatenate(
        [jnp.concatenate(gain_rows, 1), jnp.concatenate(bias_rows, 1)], 0
    )
    row_pair = iota((8, LANES), 0) // 2
    part = iota((8, GATE), 1) // LANES
    smaller = jnp.where(part == 1, 1.0, 0.5)
    gain = jnp.concatenate([row for row in gain_rows for _ in range(2)], 0) * smaller
    bias = jnp.concatenate([row for row in bias_rows for _ in range(2)], 0)
    bias = (bias - jnp.where(part == 2, 1.0, 0.0)) * smaller
    start = jnp.concatenate(
        [start_ref[:, lanes_of(pair)].astype(f32) for pair in range(PAIRS)], 0
    )
    scale = 1.0 / (PAIRS * GATE)

    def advance(step, state, first=False):
        wide = jnp.concatenate([jnp.where(row_pair == j, state, 0.0) for j in range(PAIRS)], 1)
        values = mm(wide.astype(bf16), state_ref[...])
        parts = [values[:, lanes_of(p)] for p in range(3)]
        for p in range(3):
            at = p * PAIRS * frames + step
            if not first:
                parts[p] = parts[p] + inputs_ref[pl.ds(at - 1, 8, stride=length), :]
            gates_ref[pl.ds(at, 8, stride=length), :] = parts[p]
        total = parts[0] + parts[1] + parts[2]
        square = parts[0] * parts[0] + parts[1] * parts[1] + parts[2] * parts[2]
        mean = jnp.sum(group_sum(total), 1, keepdims=True) * scale
        spread = jnp.sum(group_sum(square), 1, keepdims=True) * scale - mean * mean
        factor = lax.rsqrt(jnp.maximum(spread, 0.0) + epsilon)
        units = [
            (parts[p] - mean) * (factor * gain[:, lanes_of(p)]) + bias[:, lanes_of(p)]
            for p in range(3)
        ]
        reset = 0.5 * jnp.tanh(units[0]) + 0.5
        update = 0.5 * jnp.tanh(units[2]) + 0.5
        renewed = state + update * (jnp.tanh(reset * units[1]) - state)
        states_ref[pl.ds(step, 8, stride=length), :] = renewed
        return renewed

    for ref in (taken_ref, pre_ref, ordered_ref, state_ref, cell_ref):
        ref.flush()
    state = advance(0, start, True)
    lax.fori_loop(1, length, advance, state, unroll=7)
    gates_ref.flush()
    states_ref.flush()
    for pair in range(PAIRS):
        held_ref[:, lanes_of(pair)] = states_ref[pair * frames : (pair + 1) * frames, :].astype(
            bf16
        )
    chosen = pick_columns(order_ref[:, : sent_ref.shape[0]], frames)
    held_ref.flush()
    sent_ref[:, :width] = mm_tn(chosen, held_ref[...]).astype(bf16)
    sent_ref[:, width:] = mm_tn(chosen, taken).astype(bf16)


def mixed_probs(logits):
    shifted = jnp.exp(logits - jnp.max(logits, 1, keepdims=True))
    probability = shifted / jnp.sum(shifted, 1, keepdims=True)
    return probability, (1.0 - unimix) * probability + unimix / CLASSES


def softmax_back(probability, grad):
    grad = (1.0 - unimix) * grad
    return probability * (grad - jnp.sum(probability * grad, 1, keepdims=True))


def heads_kernel(
    core_ref,
    camera_ref,
    held_ref,
    embed_ref,
    camera_scale_ref,
    prior_hidden_ref,
    prior_gain_ref,
    prior_bias_ref,
    prior_out_ref,
    prior_shift_ref,
    post_deter_ref,
    post_embed_ref,
    post_gain_ref,
    post_bias_ref,
    post_out_ref,
    post_shift_ref,
    post_low_ref,
    prior_low_ref,
    small_ref,
    keep_ref,
    send_ref,
    post_act_ref,
    prior_act_ref,
    scaled_ref,
):
    frames, width = held_ref.shape
    features = embed_ref.shape[1]
    length = frames // 2
    held = held_ref[...]
    for s in range(2):
        rows = slice(s * length, (s + 1) * length)
        scale = scale_row(camera_ref, camera_scale_ref, s, slice(0, features))
        scaled_ref[rows, :] = (embed_ref[rows, :].astype(f32) * scale).astype(bf16)
    post_pre = mm(held, post_deter_ref[...]) + mm(scaled_ref[...], post_embed_ref[...])
    prior_pre = mm(held, prior_hidden_ref[...])
    post_act = norm_silu(post_pre, post_gain_ref[...], post_bias_ref[...]).astype(bf16)
    prior_act = norm_silu(prior_pre, prior_gain_ref[...], prior_bias_ref[...]).astype(bf16)
    post_logits = mm(post_act, post_out_ref[...]) + post_shift_ref[...]
    prior_logits = mm(prior_act, prior_out_ref[...]) + prior_shift_ref[...]
    split = (GROUPS, CLASSES, frames)
    post_prob, post_mix = mixed_probs(post_logits.T.reshape(split))
    prior_prob, prior_mix = mixed_probs(prior_logits.T.reshape(split))
    ratio = jnp.log(post_mix) - jnp.log(prior_mix)
    divergence = jnp.sum(jnp.sum(post_mix * ratio, 0, keepdims=True), 1, keepdims=True)
    slope = sigmoid(divergence - free_bits)
    post_log = softmax_back(post_prob, slope * (ratio + 1.0))
    prior_log = softmax_back(prior_prob, -slope * (post_mix / prior_mix))
    post_log = post_log.reshape(GROUPS * CLASSES, frames).T.astype(bf16)
    prior_log = prior_log.reshape(GROUPS * CLASSES, frames).T.astype(bf16)
    post_low, post_gain_grad, post_bias_grad = norm_silu_back(
        post_pre, post_gain_ref[...], post_bias_ref[...], mm_nt(post_log, post_out_ref[...])
    )
    prior_low, prior_gain_grad, prior_bias_grad = norm_silu_back(
        prior_pre, prior_gain_ref[...], prior_bias_ref[...], mm_nt(prior_log, prior_out_ref[...])
    )
    post_low, prior_low = post_low.astype(bf16), prior_low.astype(bf16)
    post_low_ref[...] = post_low
    prior_low_ref[...] = prior_low
    post_low_ref.flush()
    prior_low_ref.flush()
    small_ref[...] = jnp.concatenate(
        [
            post_gain_grad,
            post_bias_grad,
            prior_gain_grad,
            prior_bias_grad,
            jnp.sum(post_log.astype(f32), 0, keepdims=True),
            jnp.sum(prior_log.astype(f32), 0, keepdims=True),
        ],
        1,
    )
    post_act_ref[...] = post_act
    prior_act_ref[...] = prior_act
    products = (
        (held_ref, post_low),
        (held_ref, prior_low),
        (post_act_ref, post_log[:, :width]),
        (post_act_ref, post_log[:, width:]),
        (prior_act_ref, prior_log[:, :width]),
        (prior_act_ref, prior_log[:, width:]),
    )
    shares = keep_ref.shape[0] // 2
    unit_rows, embed_rows = width // shares, features // shares
    small, large = unit_rows // 4, embed_rows // 4
    for slot, ref in ((1, send_ref), (0, keep_ref)):
        parity = core_ref[0] ^ slot
        for y in range(shares // 2):
            share = 2 * y + parity
            places = [block_place(parity, y, block) for block in range(4)]
            for block in range(4):
                at = pl.multiple_of(share * embed_rows + block * large, large)
                grad = mm_tn(scaled_ref[:, pl.ds(at, large)], post_low)
                ref[places[block], :large, :] = grad.astype(bf16)
            at = pl.multiple_of(share * unit_rows, unit_rows)
            for index, (left, right) in enumerate(products):
                grad = mm_tn(left[:, pl.ds(at, unit_rows)], right).astype(bf16)
                first = large + index * small
                for block in range(4):
                    ref[places[block], first : first + small, :] = grad[
                        block * small : (block + 1) * small
                    ]
        ref.flush()


def block_place(parity, y, block):
    low_bit, next_bit = block // 2, block % 2
    return jnp.where(
        parity == 0, 4 * y + 2 * low_bit + next_bit, 4 * next_bit + 2 * y + low_bit
    )


def embed_back_kernel(
    camera_ref,
    embed_ref,
    camera_scale_ref,
    post_low_ref,
    prior_low_ref,
    post_embed_ref,
    post_deter_ref,
    prior_hidden_ref,
    held_grad_ref,
    embed_grad_ref,
    camera_grad_ref,
):
    frames, features = embed_ref.shape
    length = frames // 2
    cameras = camera_scale_ref.shape[0]
    held_grad_ref[...] = mm_nt(post_low_ref[...], post_deter_ref[...]) + mm_nt(
        prior_low_ref[...], prior_hidden_ref[...]
    )
    wide = features // 4
    for q in range(4):
        columns = slice(q * wide, (q + 1) * wide)
        scaled_grad = mm_nt(post_low_ref[...], post_embed_ref[columns, :])
        terms = [jnp.zeros((1, wide), f32) for _ in range(cameras)]
        for s in range(2):
            rows = slice(s * length, (s + 1) * length)
            part = scaled_grad[rows]
            scale = scale_row(camera_ref, camera_scale_ref, s, columns)
            embed_grad_ref[rows, columns] = part * scale
            term = jnp.sum(part * embed_ref[rows, columns].astype(f32), 0, keepdims=True)
            for c in range(cameras):
                terms[c] = terms[c] + jnp.where(camera_ref[s] == c, term, 0.0)
        camera_grad_ref[:, columns] = jnp.concatenate(terms, 0)


def cell_gates(units, cell_ref, pair):
    scaled = units * cell_ref[:1, gates_of(pair)] + cell_ref[1:, gates_of(pair)]
    reset = sigmoid(scaled[:, :LANES])
    middle = scaled[:, LANES : 2 * LANES]
    return reset, middle, jnp.tanh(reset * middle), sigmoid(scaled[:, 2 * LANES :] - 1.0)


def rollout_kernel(
    got_ref,
    cat_ref,
    table_ref,
    stoch_gain_ref,
    stoch_bias_ref,
    ordered_ref,
    state_ref,
    cell_ref,
    states_ref,
    inputs_ref,
    held_ref,
    pre_ref,
    unit_ref,
    scale_ref,
):
    horizon, count, width = states_ref.shape
    inputs_ref[:count, :] = got_ref[:, width:]
    for at in range(0, horizon - 1, 2):
        rows = slice(at * count, (at + 2) * count)
        pre = mm(hot_rows([cat_ref[at], cat_ref[at + 1]]), table_ref[...])
        pre_ref[rows, :] = pre
        inputs_ref[(at + 1) * count : (at + 3) * count, :] = norm_silu(
            pre, stoch_gain_ref[...], stoch_bias_ref[...]
        ).astype(bf16)
    chunk = 3 * count
    for at in range(0, horizon * count, chunk):
        rows = slice(at, at + chunk)
        unit_ref[rows, :] = mm(inputs_ref[rows, :], ordered_ref[...])
    norm = 1.0 / (PAIRS * GATE)

    def advance(step, state):
        rows = pl.ds(pl.multiple_of(step * count, count), count)
        held = state.astype(bf16)
        held_ref[rows, :] = held
        values = []
        total = jnp.zeros((count, LANES), f32)
        square = jnp.zeros((count, LANES), f32)
        for pair in range(PAIRS):
            value = unit_ref[rows, gates_of(pair)] + mm(
                held[:, lanes_of(pair)], state_ref[lanes_of(pair), :]
            )
            values.append(value)
            for p in range(3):
                piece = value[:, lanes_of(p)]
                total = total + piece
                square = square + piece * piece
        mean = jnp.sum(total, 1, keepdims=True) * norm
        spread = jnp.sum(square, 1, keepdims=True) * norm - mean * mean
        factor = lax.rsqrt(jnp.maximum(spread, 0.0) + epsilon)
        scale_ref[rows, :] = jnp.broadcast_to(factor, (count, LANES))
        fresh = []
        for pair in range(PAIRS):
            units = (values[pair] - mean) * factor
            unit_ref[rows, gates_of(pair)] = units
            _, _, candidate, update = cell_gates(units, cell_ref, pair)
            old = state[:, lanes_of(pair)]
            fresh.append(old + update * (candidate - old))
        renewed = jnp.concatenate(fresh, 1)
        states_ref[step] = renewed
        return renewed

    inputs_ref.flush()
    pre_ref.flush()
    ready(state_ref, cell_ref)
    lax.fori_loop(0, horizon, advance, got_ref[:, :width].astype(f32))


def rollout_back_kernel(
    got_ref,
    states_ref,
    unit_ref,
    scale_ref,
    cot_ref,
    ordered_ref,
    state_ref,
    cell_ref,
    back_ref,
    gate_grad_ref,
    cell_grad_ref,
    part_ref,
    gain_grad_ref,
    bias_grad_ref,
):
    horizon, count, width = states_ref.shape
    norm = 1.0 / (PAIRS * GATE)
    first = got_ref[:, :width].astype(f32)
    gain_grad_ref[...] = jnp.zeros_like(gain_grad_ref)
    bias_grad_ref[...] = jnp.zeros_like(bias_grad_ref)

    def retreat(index, carry):
        step = horizon - 1 - index
        rows = pl.ds(pl.multiple_of(step * count, count), count)
        before = states_ref[jnp.maximum(step - 1, 0)]
        before = jnp.where(step == 0, first, before)
        grads = cot_ref[step].astype(f32) + carry
        low = jnp.zeros((count, LANES), f32)
        high = jnp.zeros((count, LANES), f32)
        kept = []
        for pair in range(PAIRS):
            units = unit_ref[rows, gates_of(pair)]
            reset, middle, candidate, update = cell_gates(units, cell_ref, pair)
            grad = grads[:, lanes_of(pair)]
            rest = 1.0 - update
            inner = grad * update * (1.0 - candidate * candidate)
            parts = jnp.concatenate(
                [
                    inner * middle * (reset * (1.0 - reset)),
                    inner * reset,
                    grad * (candidate - before[:, lanes_of(pair)]) * (update * rest),
                ],
                1,
            )
            weighted = parts * units
            gain_grad_ref[:, gates_of(pair)] += jnp.sum(weighted.reshape(count // 8, 8, GATE), 0)
            bias_grad_ref[:, gates_of(pair)] += jnp.sum(parts.reshape(count // 8, 8, GATE), 0)
            parts = parts * cell_ref[:1, gates_of(pair)]
            weighted = parts * units
            for p in range(3):
                low = low + parts[:, lanes_of(p)]
                high = high + weighted[:, lanes_of(p)]
            part_ref[:, gates_of(pair)] = parts
            kept.append(grad * rest)
        low = jnp.sum(low, 1, keepdims=True) * norm
        high = jnp.sum(high, 1, keepdims=True) * norm
        factor = scale_ref[rows, :][:, :1]
        carried = []
        for pair in range(PAIRS):
            units = unit_ref[rows, gates_of(pair)]
            grad = (factor * (part_ref[:, gates_of(pair)] - low - units * high)).astype(bf16)
            gate_grad_ref[rows, gates_of(pair)] = grad
            carried.append(kept[pair] + mm_nt(grad, state_ref[lanes_of(pair), :]))
        return jnp.concatenate(carried, 1)

    ready(states_ref, unit_ref, scale_ref, cot_ref, state_ref, cell_ref)
    carry = lax.fori_loop(0, horizon, retreat, jnp.zeros((count, width), f32))
    back_ref[:, :width] = carry.astype(bf16)
    back_ref[:, width:] = mm_nt(gate_grad_ref[:count, :], ordered_ref[...]).astype(bf16)
    cell_grad_ref[...] = jnp.concatenate(
        [
            jnp.sum(gain_grad_ref[...], 0, keepdims=True),
            jnp.sum(bias_grad_ref[...], 0, keepdims=True),
        ],
        0,
    )


def rollout_grads_kernel(
    gate_grad_ref,
    inputs_ref,
    held_ref,
    pre_ref,
    cat_ref,
    ordered_ref,
    stoch_gain_ref,
    stoch_bias_ref,
    input_grad_ref,
    state_grad_ref,
    table_grad_ref,
    stoch_grad_ref,
):
    for pair in range(PAIRS):
        grads = gate_grad_ref[:, gates_of(pair)]
        input_grad_ref[:, gates_of(pair)] = mm_tn(inputs_ref[...], grads)
        state_grad_ref[pair] = mm_tn(held_ref[:, lanes_of(pair)], grads)
    steps, _, count = cat_ref.shape
    table_grad_ref[...] = jnp.zeros(table_grad_ref.shape, f32)
    gain_sum = jnp.zeros(stoch_gain_ref.shape, f32)
    bias_sum = jnp.zeros(stoch_bias_ref.shape, f32)
    for at in range(0, steps, 2):
        rows = slice(at * count, (at + 2) * count)
        grad = mm_nt(gate_grad_ref[(at + 1) * count : (at + 3) * count, :], ordered_ref[...])
        low, gain_grad, bias_grad = norm_silu_back(
            pre_ref[rows, :], stoch_gain_ref[...], stoch_bias_ref[...], grad
        )
        gain_sum = gain_sum + gain_grad
        bias_sum = bias_sum + bias_grad
        table_grad_ref[...] += mm_tn(
            hot_rows([cat_ref[at], cat_ref[at + 1]]), low.astype(bf16)
        )
    stoch_grad_ref[...] = jnp.concatenate([gain_sum, bias_sum], 1)


def observe_back_kernel(
    core_ref,
    held_grad_ref,
    back_ref,
    order_ref,
    cat_ref,
    taken_ref,
    pre_ref,
    gates_ref,
    states_ref,
    start_ref,
    stoch_gain_ref,
    stoch_bias_ref,
    ordered_ref,
    state_ref,
    cell_ref,
    input_part_ref,
    state_part_ref,
    table_part_ref,
    stoch_part_ref,
    cell_part_ref,
    small_ref,
    camera_grad_ref,
    start_grad_ref,
    keep_ref,
    send_ref,
    grads_ref,
    turned_ref,
    arriving_ref,
    slope_ref,
    factor_ref,
    unit_ref,
    mean_ref,
    cross_ref,
    rest_ref,
    flat_ref,
    lean_ref,
    scale_ref,
    grad_ref,
    low_ref,
    high_ref,
    previous_ref,
):
    frames, width = held_grad_ref.shape
    length = frames // 2
    norm = 1.0 / (PAIRS * GATE)
    chosen = pick_columns(order_ref[:, : back_ref.shape[0]], frames)
    held_grad = held_grad_ref[...] + mm(chosen, back_ref[:, :width])
    turned_ref[...] = state_ref[...].astype(f32).T.astype(bf16)
    start = jnp.concatenate(
        [start_ref[:, lanes_of(pair)].astype(f32) for pair in range(PAIRS)], 0
    )
    for pair in range(PAIRS):
        arriving_ref[pair * frames : (pair + 1) * frames, :] = held_grad[:, lanes_of(pair)]
    long = PAIRS * frames
    for s in range(2):
        blocks = [
            slice((2 * pair + s) * length, (2 * pair + s + 1) * length) for pair in range(PAIRS)
        ]
        total = jnp.zeros((length, LANES), f32)
        for rows in blocks:
            for p in range(3):
                total = total + gates_ref[p * long + rows.start : p * long + rows.stop, :]
        mean = jnp.sum(total, 1, keepdims=True) * norm
        square = jnp.zeros((length, LANES), f32)
        for rows in blocks:
            for p in range(3):
                center = gates_ref[p * long + rows.start : p * long + rows.stop, :] - mean
                square = square + center * center
        scale = lax.rsqrt(jnp.sum(square, 1, keepdims=True) * norm + epsilon)
        for pair, rows in enumerate(blocks):
            gain = cell_ref[:1, gates_of(pair)]
            units = jnp.concatenate(
                [gates_ref[p * long + rows.start : p * long + rows.stop, :] for p in range(3)], 1
            )
            units = (units - mean) * scale
            reset, middle, candidate, update = cell_gates(units, cell_ref, pair)
            row = 2 * pair + s
            previous = jnp.where(
                iota((length, LANES), 0) == 0,
                start[row : row + 1, :],
                pltpu.roll(states_ref[rows, :], 1, 0),
            )
            previous_ref[rows, :] = previous
            inner = update * (1.0 - candidate * candidate)
            slope = jnp.concatenate(
                [
                    inner * middle * (reset * (1.0 - reset)),
                    inner * reset,
                    (candidate - previous) * (update * (1.0 - update)),
                ],
                1,
            )
            slope_ref[rows, :] = slope
            slope = slope * gain
            weighted = slope * units
            mean_ref[rows, :] = norm * (
                slope[:, :LANES] + slope[:, LANES : 2 * LANES] + slope[:, 2 * LANES :]
            )
            cross_ref[rows, :] = norm * (
                weighted[:, :LANES] + weighted[:, LANES : 2 * LANES] + weighted[:, 2 * LANES :]
            )
            for p in range(3):
                factor_ref[p * long + rows.start : p * long + rows.stop, :] = (
                    scale * slope[:, lanes_of(p)]
                )
            unit_ref[rows, :] = scale * units
            rest_ref[rows, :] = 1.0 - update
            scale_ref[rows, :] = jnp.broadcast_to(scale, (length, LANES))
            weight = state_ref[lanes_of(pair), :]
            flat_ref[rows, :] = scale * mm_nt(jnp.ones((8, GATE), bf16), weight)[:1, :]
            lean_ref[rows, :] = mm_nt((scale * units).astype(bf16), weight)
    row_pair = iota((8, LANES), 0) // 2

    def retreat(index, carry):
        step = length - 1 - index
        rows = pl.ds(step, 8, stride=length)
        grad = arriving_ref[rows, :] + carry
        wide = jnp.concatenate(
            [grad * factor_ref[pl.ds(p * long + step, 8, stride=length), :] for p in range(3)], 1
        )
        turned = mm(wide.astype(bf16), turned_ref[...])
        low = jnp.sum(group_sum(grad * mean_ref[rows, :]), 1, keepdims=True)
        high = jnp.sum(group_sum(grad * cross_ref[rows, :]), 1, keepdims=True)
        grad_ref[rows, :] = grad
        low_ref[rows, :] = jnp.broadcast_to(low, (8, LANES))
        high_ref[rows, :] = jnp.broadcast_to(high, (8, LANES))
        kept = grad * rest_ref[rows, :] - low * flat_ref[rows, :] - high * lean_ref[rows, :]
        for pair in range(PAIRS):
            kept = kept + jnp.where(row_pair == pair, turned[:, lanes_of(pair)], 0.0)
        return kept

    carry = lax.fori_loop(0, length, retreat, jnp.zeros((8, LANES), f32), unroll=8)
    for pair in range(PAIRS):
        start_grad_ref[:, lanes_of(pair)] = carry[2 * pair : 2 * pair + 2, :]
    frame = iota((frames, width), 0) % length
    earlier = jnp.where(frame == 0, 0.0, pltpu.roll(taken_ref[...].astype(f32), 1, 0)).astype(bf16)
    input_grad = jnp.zeros((frames, width), f32)
    gains, biases, inputs = [], [], []
    order = column_order()
    shares = grads_ref.shape[0]
    unit_rows = width // shares
    for pair in range(PAIRS):
        rows = slice(pair * frames, (pair + 1) * frames)
        grad = jnp.concatenate([grad_ref[rows, :]] * 3, 1)
        gate_grad = grad * slope_ref[rows, :]
        biases.append(jnp.sum(gate_grad, 0, keepdims=True))
        scale = scale_ref[rows, :][:, :1]
        units = unit_ref[rows, :]
        gains.append(jnp.sum(gate_grad * (units / scale), 0, keepdims=True))
        low = low_ref[rows, :][:, :1]
        high = high_ref[rows, :][:, :1]
        factors = jnp.concatenate(
            [factor_ref[p * long + rows.start : p * long + rows.stop, :] for p in range(3)], 1
        )
        gate_low = (grad * factors - low * scale - high * units).astype(bf16)
        columns = ordered_ref[:, gates_of(pair)]
        input_grad = input_grad + mm_nt(gate_low, columns)
        weight_grad = mm_tn(earlier, gate_low) + input_part_ref[:, gates_of(pair)]
        inputs.append(mm_nt(weight_grad.astype(bf16), order).astype(bf16))
        state_grad = mm_tn(previous_ref[rows, :].astype(bf16), gate_low) + state_part_ref[pair]
        half = LANES // 2
        upper = iota((half, GATE), 1) % LANES < half
        folded = jnp.where(upper, state_grad[:half], state_grad[half:])
        at = 3 * unit_rows + 2 * unit_rows
        grads_ref[pair, at : at + half, :GATE] = folded.astype(bf16)
        grads_ref[pair, at : at + half, GATE:] = jnp.zeros((half, width - GATE), bf16)
    weights = jnp.concatenate(inputs, 1)
    for q in range(shares):
        for c in range(3):
            grads_ref[q, c * unit_rows : (c + 1) * unit_rows, :] = weights[
                q * unit_rows : (q + 1) * unit_rows, c * width : (c + 1) * width
            ]
    taken_grad = jnp.where(
        frame == length - 1, 0.0, pltpu.roll(input_grad, frames - 1, 0)
    ) + mm(chosen, back_ref[:, width:])
    low, gain_grad, bias_grad = norm_silu_back(
        pre_ref[...], stoch_gain_ref[...], stoch_bias_ref[...], taken_grad
    )
    stoch = jnp.concatenate([gain_grad, bias_grad], 1) + stoch_part_ref[...]
    hot = hot_rows([cat_ref[s] for s in range(2)])
    table_grad = mm_tn(hot, low.astype(bf16)) + table_part_ref[...]
    rows = table_grad.shape[0] // shares
    vector_row = 5 * unit_rows + LANES // 2
    classes = GROUPS * CLASSES
    wide = camera_grad_ref.shape[1] // shares
    for q in range(shares):
        grads_ref[q, 3 * unit_rows : 3 * unit_rows + rows, :] = table_grad[
            q * rows : (q + 1) * rows
        ].astype(bf16)
        unit = slice(q * unit_rows, (q + 1) * unit_rows)
        logit = slice(q * classes // shares, (q + 1) * classes // shares)
        units = [stoch[:, unit], stoch[:, width + unit.start : width + unit.stop]]
        units += [
            small_ref[:, k * width + unit.start : k * width + unit.stop] for k in range(4)
        ]
        logits = [
            small_ref[
                :, 4 * width + k * classes + logit.start : 4 * width + k * classes + logit.stop
            ]
            for k in range(2)
        ]
        cells = [
            plain_row(kind[q] + cell_part_ref[k : k + 1, gates_of(q)])
            for k, kind in enumerate((gains, biases))
        ]
        pad = jnp.zeros((1, width - GATE), f32)
        rows_out = [
            jnp.concatenate(units[:4], 1),
            jnp.concatenate(units[4:] + logits[:1], 1),
            jnp.concatenate(logits[1:] + [jnp.zeros((1, width - logits[1].shape[1]), f32)], 1),
        ]
        rows_out += [jnp.concatenate([cell, pad], 1) for cell in cells]
        for c in range(camera_grad_ref.shape[0]):
            for at in range(q * wide, (q + 1) * wide, width):
                rows_out.append(camera_grad_ref[c : c + 1, at : at + width])
        rows_out.append(jnp.zeros((grads_ref.shape[1] - vector_row - len(rows_out), width), f32))
        grads_ref[q, vector_row:, :] = jnp.concatenate(rows_out, 0).astype(bf16)
    block = keep_ref.shape[1]
    for slot, ref in ((0, keep_ref), (1, send_ref)):
        parity = core_ref[0] ^ slot
        for y in range(shares // 2):
            for index in range(4):
                at = index * block
                ref[block_place(parity, y, index)] = grads_ref[
                    2 * y + parity, at : at + block, :
                ]


def place_blocks(where_ref, own_ref, got_ref, full_ref):
    block = own_ref.shape[0] // 2
    parity, bit = where_ref[0], where_ref[1]
    for side in range(2):
        for inner in range(2):
            rows = slice(inner * block, (inner + 1) * block)
            piece = jnp.where(bit == side, own_ref[rows, :], got_ref[rows, :]).astype(f32)
            place = jnp.where(parity == 0, 2 * side + inner, 2 * inner + side)
            full_ref[pl.ds(pl.multiple_of(place * block, block), block), :] = piece


def finish_heads_kernel(
    where_ref,
    own_ref,
    got_ref,
    post_embed_ref,
    post_deter_ref,
    prior_hidden_ref,
    post_out_ref,
    prior_out_ref,
    full_ref,
):
    place_blocks(where_ref, own_ref, got_ref, full_ref)
    block = full_ref.shape[0] // 4
    width = own_ref.shape[1]
    large, small = post_embed_ref.shape[0] // 4, post_deter_ref.shape[0] // 4
    for index in range(4):
        at = index * block
        post_embed_ref[index * large : (index + 1) * large, :] = full_ref[at : at + large, :]
        rows = slice(index * small, (index + 1) * small)
        for member, (ref, column) in enumerate(
            (
                (post_deter_ref, 0),
                (prior_hidden_ref, 0),
                (post_out_ref, 0),
                (post_out_ref, width),
                (prior_out_ref, 0),
                (prior_out_ref, width),
            )
        ):
            first = at + large + member * small
            ref[rows, column : column + width] = full_ref[first : first + small, :]


def finish_kernel(where_ref, own_ref, got_ref, *refs):
    outs, full_ref = refs[:-1], refs[-1]
    width = own_ref.shape[1]
    place_blocks(where_ref, own_ref, got_ref, full_ref)
    input_ref, table_ref, state_ref = outs[:3]
    unit_rows = input_ref.shape[0]
    for c in range(3):
        input_ref[:, c * width : (c + 1) * width] = full_ref[c * unit_rows : (c + 1) * unit_rows, :]
    at = 3 * unit_rows
    table_ref[...] = full_ref[at : at + table_ref.shape[0], :]
    at += table_ref.shape[0]
    half = state_ref.shape[1]
    folded = full_ref[at : at + half, :]
    for e in range(2):
        state_ref[e] = jnp.concatenate(
            [folded[:, (2 * p + e) * half : (2 * p + e + 1) * half] for p in range(3)], 1
        )
    at += half
    units = outs[3:9]
    for k, ref in enumerate(units):
        ref[...] = full_ref[
            at + k // 4 : at + k // 4 + 1, k % 4 * unit_rows : (k % 4 + 1) * unit_rows
        ]
    size = outs[9].shape[1]
    outs[9][...] = full_ref[at + 1 : at + 2, size:]
    outs[10][...] = full_ref[at + 2 : at + 3, :size]
    outs[11][...] = full_ref[at + 3 : at + 4, :GATE]
    outs[12][...] = full_ref[at + 4 : at + 5, :GATE]
    row = at + 5
    camera_ref = outs[13]
    for c in range(camera_ref.shape[0]):
        for column in range(0, camera_ref.shape[1], width):
            camera_ref[c : c + 1, column : column + width] = full_ref[row : row + 1, :]
            row += 1


def struct(shape, dtype):
    return jax.ShapeDtypeStruct(shape, dtype)


class Incoming:
    def __init__(self, ref, copy):
        self.ref, self.copy, self.shape = ref, copy, ref.shape
        copy.start()

    def ready(self):
        if self.copy is not None:
            self.copy.wait()
            self.copy = None

    def __getitem__(self, index):
        self.ready()
        return self.ref[index]


class Outgoing:
    def __init__(self, ref, copy):
        self.ref, self.copy, self.shape, self.started = ref, copy, ref.shape, False

    def __getitem__(self, index):
        return self.ref[index]

    def __setitem__(self, index, value):
        self.ref[index] = value

    def flush(self):
        if not self.started:
            self.copy.start()
            self.started = True


def ready(*refs):
    for ref in refs:
        if isinstance(ref, Incoming):
            ref.ready()


def call(kernel, name, outs, ins, mib, scratch=(), scalars=0, after=(), near_in=(), near_out=()):
    count, total = len(ins), len(ins) + len(after) + len(outs)
    far_in = [k for k in range(scalars, count) if k not in near_in]
    far_out = [k for k in range(len(outs)) if k not in near_out]
    near = pl.BlockSpec(memory_space=pltpu.VMEM)
    far = pl.BlockSpec(memory_space=pltpu.HBM)

    def body(*refs):
        given, made = list(refs[:count]), list(refs[count + len(after) : total])
        places = refs[total : total + len(far_in) + len(far_out)]
        rest = refs[total + len(far_in) + len(far_out) : -1]
        marks = refs[-1]
        for at, k in enumerate(far_in):
            copy = pltpu.make_async_copy(given[k], places[at], marks.at[at])
            given[k] = Incoming(places[at], copy)
        for at, k in enumerate(far_out, len(far_in)):
            copy = pltpu.make_async_copy(places[at], made[k], marks.at[at])
            made[k] = Outgoing(places[at], copy)
        kernel(*given, *made, *rest)
        ready(*given)
        for k in far_out:
            made[k].flush()
        for k in far_out:
            made[k].copy.wait()

    return pl.pallas_call(
        body,
        out_shape=tuple(
            pltpu.HBM(out.shape, out.dtype) if k in far_out else out for k, out in enumerate(outs)
        ),
        in_specs=[pl.BlockSpec(memory_space=pltpu.SMEM)] * scalars
        + [far if k in far_in else near for k in range(scalars, count)]
        + [pl.BlockSpec(memory_space=pl.ANY)] * len(after),
        out_specs=tuple(far if k in far_out else near for k in range(len(outs))),
        scratch_shapes=[pltpu.VMEM(ins[k].shape, ins[k].dtype) for k in far_in]
        + [pltpu.VMEM(outs[k].shape, outs[k].dtype) for k in far_out]
        + list(scratch)
        + [pltpu.SemaphoreType.DMA((len(far_in) + len(far_out),))],
        compiler_params=pltpu.CompilerParams(vmem_limit_bytes=mib * 1024 * 1024),
        name=name,
    )(
        *[
            pltpu.with_memory_space_constraint(member, pltpu.HBM) if k in far_in else member
            for k, member in enumerate(ins)
        ],
        *after,
    )


def linear_bits(bits):
    own = bits[0]
    rep_count = lax.axis_size("rep")
    index = lax.axis_index("seq") * rep_count + lax.axis_index("rep")
    if bits[0] != bits[1]:
        own = jnp.where(index & 1 == 0, bits[0], bits[1])
    return (index >> own) & 1


def swap(values, bits):
    count = lax.axis_size("seq") * lax.axis_size("rep")
    return lax.ppermute(
        values, ("seq", "rep"), [(i, i ^ (1 << bits[i & 1])) for i in range(count)]
    )


def added(left, right):
    return (left.astype(f32) + right.astype(f32)).astype(bf16)


def folded(keep, got, bits):
    own = linear_bits(bits)
    half = keep.shape[0] // 2
    return [
        added(
            lax.dynamic_slice_in_dim(keep, side * half, half, 0),
            lax.dynamic_slice_in_dim(got, side * half, half, 0),
        )
        for side in (1 - own, own)
    ]


def doubled(values, bits):
    got = swap(values, bits)
    own = linear_bits(bits)
    return jnp.where(
        own == 0, jnp.concatenate([values, got], 0), jnp.concatenate([got, values], 0)
    )


def on_device(
    start_deter,
    post_cat,
    embed,
    camera,
    start_order,
    imag_cat,
    imag_cot,
    stoch_table,
    stoch_gain,
    stoch_bias,
    state_weight,
    input_weight,
    cell_gain,
    cell_bias,
    prior_hidden,
    prior_gain,
    prior_bias,
    prior_out,
    prior_shift,
    post_deter,
    post_embed,
    post_gain,
    post_bias,
    post_out,
    post_shift,
    camera_scale,
):
    seq_count, length = post_cat.shape[:2]
    frames = seq_count * length
    count, horizon, width = imag_cot.shape
    features = embed.shape[-1]
    shares = lax.axis_size("rep")
    rep_bits = shares.bit_length() - 1
    seq_bits = lax.axis_size("seq").bit_length() - 1
    half = LANES // 2
    gate_count = 3 * width
    classes = GROUPS * CLASSES
    rows = horizon * count
    long = PAIRS * frames
    unit_rows = width // shares
    core = (lax.axis_index("rep") & 1).astype(jnp.int32).reshape(1)
    row = lambda vector: vector.reshape(1, -1)
    cat = jnp.swapaxes(post_cat, 1, 2)
    later_cat = jnp.transpose(imag_cat, (1, 2, 0))
    stoch_rows = (row(stoch_gain), row(stoch_bias))
    embed_rows = embed.reshape(frames, features)

    low_bit, next_bit = rep_bits, rep_bits + 1
    deeper = [(rep_bits + bit,) * 2 for bit in range(2, seq_bits)]
    outer, inner = (low_bit, next_bit), (next_bit, low_bit)
    stages = [(1, next_bit), (low_bit, 1), inner] + deeper

    held, taken, obs_pre, obs_gates, obs_states, sent, ordered, state, cell = call(
        observe_kernel,
        "observe",
        [
            struct((frames, width), bf16),
            struct((frames, width), bf16),
            struct((frames, width), f32),
            struct((3 * long, LANES), f32),
            struct((long, LANES), f32),
            struct((count, 2 * width), bf16),
            struct((width, gate_count), bf16),
            struct((width, GATE), bf16),
            struct((2, gate_count), f32),
        ],
        (
            cat,
            stoch_table,
            *stoch_rows,
            input_weight,
            state_weight.reshape(width, 3 * half),
            row(cell_gain),
            row(cell_bias),
            start_deter,
            start_order,
        ),
        18,
        scratch=[pltpu.VMEM((3 * long, LANES), f32)],
    )
    got = lax.all_to_all(sent, "seq", split_axis=0, concat_axis=0, tiled=True)

    square = struct((frames, width), bf16)
    embed_rows_count = features // shares
    head_rows = embed_rows_count + 6 * unit_rows
    blocks = struct((2 * shares, head_rows // 4, width), bf16)
    post_low, prior_low, head_small, keep, send = call(
        heads_kernel,
        "heads",
        [square, square, struct((1, 4 * width + 2 * classes), f32), blocks, blocks],
        (
            core,
            camera,
            held,
            embed_rows,
            camera_scale,
            prior_hidden,
            row(prior_gain),
            row(prior_bias),
            prior_out,
            row(prior_shift),
            post_deter,
            post_embed,
            row(post_gain),
            row(post_bias),
            post_out,
            row(post_shift),
        ),
        34,
        scratch=[
            pltpu.VMEM((frames, width), bf16),
            pltpu.VMEM((frames, width), bf16),
            pltpu.VMEM((frames, features), bf16),
        ],
        scalars=2,
    )
    flat = (shares * head_rows // 2, width)
    arrived = swap(send.reshape(flat), (0, 0))
    send, keep = folded(keep.reshape(flat), arrived, stages[0])
    arrived = swap(send, stages[0])

    states, imag_inputs, imag_held, imag_pre, units, scales = call(
        rollout_kernel,
        "rollout",
        [
            struct((horizon, count, width), f32),
            struct((rows, width), bf16),
            struct((rows, width), bf16),
            struct((rows - count, width), f32),
            struct((rows, gate_count), f32),
            struct((rows, LANES), f32),
        ],
        (got, later_cat, stoch_table, *stoch_rows, ordered, state, cell),
        24,
        near_out=(4, 5),
        after=(send,),
    )
    imag_deter = jnp.swapaxes(states, 0, 1)
    keep, scales = lax.optimization_barrier((keep, scales))
    send, keep = folded(keep, arrived, stages[1])
    arrived = swap(send, stages[1])
    back, gate_grads, cell_part = call(
        rollout_back_kernel,
        "rollout_back",
        [
            struct((count, 2 * width), bf16),
            struct((rows, gate_count), bf16),
            struct((2, gate_count), f32),
        ],
        (got, states, units, scales, jnp.swapaxes(imag_cot, 0, 1), ordered, state, cell),
        24,
        scratch=[
            pltpu.VMEM((count, gate_count), f32),
            pltpu.VMEM((8, gate_count), f32),
            pltpu.VMEM((8, gate_count), f32),
        ],
        near_in=(2, 3),
        after=(send,),
    )
    returned = lax.all_to_all(back, "seq", split_axis=0, concat_axis=0, tiled=True)
    keep, cell_part = lax.optimization_barrier((keep, cell_part))
    send, keep = folded(keep, arrived, stages[2])
    arrived = swap(send, stages[2])

    input_part, state_part, table_part, stoch_part = call(
        rollout_grads_kernel,
        "rollout_grads",
        [
            struct((width, gate_count), f32),
            struct((PAIRS, LANES, GATE), f32),
            struct(stoch_table.shape, f32),
            struct((1, 2 * width), f32),
        ],
        (gate_grads, imag_inputs, imag_held, imag_pre, later_cat, ordered, *stoch_rows),
        22,
        after=(send,),
    )
    keep, stoch_part = lax.optimization_barrier((keep, stoch_part))
    for bits in deeper:
        send, keep = folded(keep, arrived, bits)
        arrived = swap(send, bits)
    held_grad, embed_grad, camera_grad = call(
        embed_back_kernel,
        "embed_back",
        [
            struct((frames, width), f32),
            struct((frames, features), f32),
            struct(camera_scale.shape, f32),
        ],
        (
            camera,
            embed_rows,
            camera_scale,
            post_low,
            prior_low,
            post_embed,
            post_deter,
            prior_hidden,
        ),
        18,
        scalars=1,
        after=(send,),
    )
    keep, camera_grad = lax.optimization_barrier((keep, camera_grad))
    piece = added(keep, arrived)
    for bits in reversed(deeper):
        piece = doubled(piece, bits)
    head_piece = doubled(piece, inner)
    head_other = swap(head_piece, outer)

    tail_rows = 768
    blocks = struct((2 * shares, tail_rows // 4, width), bf16)
    start_grad, tail_keep, tail_send = call(
        observe_back_kernel,
        "observe_back",
        [struct((seq_count, width), f32), blocks, blocks],
        (
            core,
            held_grad,
            returned,
            start_order,
            cat,
            taken,
            obs_pre,
            obs_gates,
            obs_states,
            start_deter,
            *stoch_rows,
            ordered,
            state,
            cell,
            input_part,
            state_part,
            table_part,
            stoch_part,
            cell_part,
            head_small,
            camera_grad,
        ),
        30,
        scratch=[
            pltpu.VMEM((shares, tail_rows, width), bf16),
            pltpu.VMEM((GATE, PAIRS * LANES), bf16),
            pltpu.VMEM((long, LANES), f32),
            pltpu.VMEM((long, GATE), f32),
            pltpu.VMEM((3 * long, LANES), f32),
            pltpu.VMEM((long, GATE), f32),
        ]
        + [pltpu.VMEM((long, LANES), f32)] * 10,
        scalars=1,
    )
    full = (2 * tail_rows, width)
    keep = tail_keep.reshape(full)
    arrived = swap(tail_send.reshape(full), (0, 0))
    for bits in stages:
        send, keep = folded(keep, arrived, bits)
        arrived = swap(send, bits)
    piece = added(keep, arrived)
    for bits in reversed([inner] + deeper):
        piece = doubled(piece, bits)
    other = swap(piece, outer)
    where = jnp.concatenate([core, linear_bits(outer).astype(jnp.int32).reshape(1)])
    unit = struct((1, unit_rows), f32)
    logit = struct((1, classes // shares), f32)
    gate = struct((1, GATE), f32)
    finished = call(
        finish_kernel,
        "finish",
        [
            struct((unit_rows, gate_count), f32),
            struct((stoch_table.shape[0] // shares, width), f32),
            struct((2, half, 3 * half), f32),
            *[unit] * 6,
            logit,
            logit,
            gate,
            gate,
            struct((camera_scale.shape[0], features // shares), f32),
        ],
        (where, piece, other),
        12,
        scratch=[pltpu.VMEM((tail_rows, width), f32)],
        scalars=1,
    )
    small_rows = struct((unit_rows, width), f32)
    wide_rows = struct((unit_rows, classes), f32)
    post_embed_grad, post_deter_grad, prior_hidden_grad, post_out_grad, prior_out_grad = call(
        finish_heads_kernel,
        "finish_heads",
        [struct((embed_rows_count, width), f32), small_rows, small_rows, wide_rows, wide_rows],
        (where, head_piece, head_other),
        16,
        scratch=[pltpu.VMEM((head_rows, width), f32)],
        scalars=1,
    )
    input_weight_grad, stoch_table_grad, state_weight_grad = finished[:3]
    (
        stoch_gain_grad,
        stoch_bias_grad,
        post_gain_grad,
        post_bias_grad,
        prior_gain_grad,
        prior_bias_grad,
        post_shift_grad,
        prior_shift_grad,
        cell_gain_grad,
        cell_bias_grad,
    ) = [member.reshape(-1) for member in finished[3:13]]
    return (
        imag_deter,
        embed_grad.reshape(embed.shape),
        start_grad,
        stoch_table_grad,
        stoch_gain_grad,
        stoch_bias_grad,
        state_weight_grad,
        input_weight_grad,
        cell_gain_grad,
        cell_bias_grad,
        prior_hidden_grad,
        prior_gain_grad,
        prior_bias_grad,
        prior_out_grad,
        prior_shift_grad,
        post_deter_grad,
        post_embed_grad,
        post_gain_grad,
        post_bias_grad,
        post_out_grad,
        post_shift_grad,
        finished[13],
    )


def solution(mesh):
    both = ("seq", "rep")
    in_specs = (
        P(both, None),
        P(both, None, None),
        P(both, None, None),
        P(both),
        P(both, None),
        P(both, None, None),
        P(both, None, None),
    ) + (P(),) * 19
    rows, flat = P("rep", None), P("rep")
    out_specs = (
        P(both, None, None),
        P(both, None, None),
        P(both, None),
        rows,
        flat,
        flat,
        P("rep", None, None),
        rows,
        flat,
        flat,
        rows,
        flat,
        flat,
        rows,
        flat,
        rows,
        rows,
        flat,
        flat,
        rows,
        flat,
        P(None, "rep"),
    )
    return jax.shard_map(
        on_device, mesh=mesh, in_specs=in_specs, out_specs=out_specs, check_vma=False
    )
```

```python
import jax
import jax.numpy as jnp
from jax import lax
from jax.experimental import pallas as pl
from jax.experimental.pallas import tpu as pltpu
from jax.sharding import PartitionSpec as P

BLOCKS = 8
GROUPS = 32
CLASSES = 32
PAIRS = BLOCKS // 2
LANES = 128
GATE = 3 * LANES

epsilon = 1e-05
unimix = 0.01
free_bits = 1.0

f32 = jnp.float32
bf16 = jnp.bfloat16


def iota(shape, axis):
    return lax.broadcasted_iota(jnp.int32, shape, axis)


def mm(left, right):
    return jnp.dot(left, right, preferred_element_type=f32)


def mm_nt(left, right):
    return lax.dot_general(left, right, (((1,), (1,)), ((), ())), preferred_element_type=f32)


def mm_tn(left, right):
    return lax.dot_general(left, right, (((0,), (0,)), ((), ())), preferred_element_type=f32)


def sigmoid(values):
    return 0.5 * jnp.tanh(0.5 * values) + 0.5


def row_mean(values):
    return jnp.sum(values, -1, keepdims=True) * (1.0 / values.shape[-1])


def hot_rows(columns):
    categories = jnp.concatenate([part.astype(f32).T for part in columns], 0).astype(bf16)
    count = categories.shape[0]
    width = GROUPS * CLASSES
    spread = (iota((GROUPS, width), 1) // CLASSES == iota((GROUPS, width), 0)).astype(f32)
    wide = mm(categories, spread.astype(bf16))
    own = (iota((count, width), 1) % CLASSES).astype(f32)
    return jnp.where(wide == own, 1.0, 0.0).astype(bf16)


def hot_columns(columns):
    categories = jnp.concatenate([part.astype(f32) for part in columns], 1).astype(bf16)
    count = categories.shape[1]
    width = GROUPS * CLASSES
    spread = (iota((width, GROUPS), 0) // CLASSES == iota((width, GROUPS), 1)).astype(f32)
    wide = mm(spread.astype(bf16), categories)
    own = (iota((width, count), 0) % CLASSES).astype(f32)
    return jnp.where(wide == own, 1.0, 0.0).astype(bf16)


def normed(values):
    center = values - row_mean(values)
    scale = lax.rsqrt(row_mean(center * center) + epsilon)
    return center * scale, scale


def norm_silu(values, factor, offset):
    act = normed(values)[0] * factor + offset
    return act * sigmoid(act)


def norm_silu_back(values, factor, offset, grad):
    unit, scale = normed(values)
    act = unit * factor + offset
    gate = sigmoid(act)
    act_grad = grad * (gate + act * gate * (1.0 - gate))
    unit_grad = act_grad * factor
    pre_grad = scale * (unit_grad - row_mean(unit_grad) - unit * row_mean(unit_grad * unit))
    return (
        pre_grad,
        jnp.sum(act_grad * unit, 0, keepdims=True),
        jnp.sum(act_grad, 0, keepdims=True),
    )


def pick_columns(chosen, count):
    return jnp.where(iota((count, chosen.shape[1]), 0) == chosen, 1.0, 0.0).astype(bf16)


def column_order():
    source, target = iota((GATE, GATE), 0), iota((GATE, GATE), 1)
    half = LANES // 2
    moved = source // half % 3 * LANES + source // (3 * half) * half + source % half
    return jnp.where(moved == target, 1.0, 0.0).astype(bf16)


def pair_row(ref, pair):
    half = LANES // 2
    pieces = []
    for p in range(3):
        for e in range(2):
            at = pair * GATE + (3 * e + p) * half
            line, lane = at // LANES, at % LANES
            pieces.append(ref[line : line + 1, lane : lane + half])
    return jnp.concatenate(pieces, 1)


def plain_row(row):
    half = LANES // 2
    return jnp.concatenate(
        [
            row[:, (2 * p + e) * half : (2 * p + e + 1) * half]
            for e in range(2)
            for p in range(3)
        ],
        1,
    )


def group_sum(values):
    values = values + pltpu.roll(values, 4, 0)
    return values + pltpu.roll(values, 2, 0)


def lanes_of(pair):
    return slice(pair * LANES, (pair + 1) * LANES)


def gates_of(pair):
    return slice(pair * GATE, (pair + 1) * GATE)


def scale_row(camera_ref, camera_scale_ref, s, columns):
    row = None
    for c in range(camera_scale_ref.shape[0]):
        part = jnp.where(camera_ref[s] == c, camera_scale_ref[c : c + 1, columns], 0.0)
        row = part if row is None else row + part
    return row


def observe_kernel(
    cat_ref,
    table_ref,
    stoch_gain_ref,
    stoch_bias_ref,
    input_ref,
    weight_ref,
    cell_gain_ref,
    cell_bias_ref,
    start_ref,
    order_ref,
    later_cat_ref,
    held_ref,
    taken_ref,
    pre_ref,
    later_ref,
    later_pre_ref,
    gates_ref,
    states_ref,
    sent_ref,
    ordered_ref,
    state_ref,
    cell_ref,
    inputs_ref,
):
    frames, width = held_ref.shape
    length = frames // 2
    half = LANES // 2
    pre = mm(hot_rows([cat_ref[s] for s in range(2)]), table_ref[...])
    pre_ref[...] = pre
    taken = norm_silu(pre, stoch_gain_ref[...], stoch_bias_ref[...]).astype(bf16)
    taken_ref[...] = taken
    order = column_order()
    for pair in range(PAIRS):
        columns = mm(input_ref[:, gates_of(pair)], order).astype(bf16)
        ordered_ref[:, gates_of(pair)] = columns
        values = mm(taken, columns)
        for p in range(3):
            at = p * PAIRS * frames + pair * frames
            inputs_ref[at : at + frames, :] = values[:, lanes_of(p)]
    source, target = iota((3 * half, GATE), 0), iota((3 * half, GATE), 1)
    same = (source // half == target // LANES) & (source % half == target % half)
    weights = mm(weight_ref[...], jnp.where(same, 1.0, 0.0).astype(bf16))
    own = iota(weights.shape, 0) // half % 2 == iota(weights.shape, 1) // half % 2
    state_ref[...] = jnp.where(own, weights, 0.0).astype(bf16)
    gain_rows = [pair_row(cell_gain_ref, pair) for pair in range(PAIRS)]
    bias_rows = [pair_row(cell_bias_ref, pair) for pair in range(PAIRS)]
    cell_ref[...] = jnp.concatenate(
        [jnp.concatenate(gain_rows, 1), jnp.concatenate(bias_rows, 1)], 0
    )
    row_pair = iota((8, LANES), 0) // 2
    part = iota((8, GATE), 1) // LANES
    smaller = jnp.where(part == 1, 1.0, 0.5)
    gain = jnp.concatenate([row for row in gain_rows for _ in range(2)], 0) * smaller
    bias = jnp.concatenate([row for row in bias_rows for _ in range(2)], 0)
    bias = (bias - jnp.where(part == 2, 1.0, 0.0)) * smaller
    start = jnp.concatenate(
        [start_ref[:, lanes_of(pair)].astype(f32) for pair in range(PAIRS)], 0
    )
    scale = 1.0 / (PAIRS * GATE)

    def advance(step, state, first=False):
        wide = jnp.concatenate([jnp.where(row_pair == j, state, 0.0) for j in range(PAIRS)], 1)
        values = mm(wide.astype(bf16), state_ref[...])
        parts = [values[:, lanes_of(p)] for p in range(3)]
        for p in range(3):
            at = p * PAIRS * frames + step
            if not first:
                parts[p] = parts[p] + inputs_ref[pl.ds(at - 1, 8, stride=length), :]
            gates_ref[pl.ds(at, 8, stride=length), :] = parts[p]
        total = parts[0] + parts[1] + parts[2]
        square = parts[0] * parts[0] + parts[1] * parts[1] + parts[2] * parts[2]
        mean = jnp.sum(group_sum(total), 1, keepdims=True) * scale
        spread = jnp.sum(group_sum(square), 1, keepdims=True) * scale - mean * mean
        factor = lax.rsqrt(jnp.maximum(spread, 0.0) + epsilon)
        units = [
            (parts[p] - mean) * (factor * gain[:, lanes_of(p)]) + bias[:, lanes_of(p)]
            for p in range(3)
        ]
        reset = 0.5 * jnp.tanh(units[0]) + 0.5
        update = 0.5 * jnp.tanh(units[2]) + 0.5
        renewed = state + update * (jnp.tanh(reset * units[1]) - state)
        states_ref[pl.ds(step, 8, stride=length), :] = renewed
        return renewed

    for ref in (taken_ref, pre_ref, ordered_ref, state_ref, cell_ref):
        ref.flush()
    state = advance(0, start, True)
    ready(later_cat_ref)
    steps, _, count = later_cat_ref.shape
    chunks = steps // 2
    share = 7

    def several(chunk, state):
        rows = pl.ds(pl.multiple_of(chunk * 2 * count, 2 * count), 2 * count)
        later_pre = mm(
            hot_rows([later_cat_ref[2 * chunk], later_cat_ref[2 * chunk + 1]]), table_ref[...]
        )
        later_pre_ref[rows, :] = later_pre
        later = norm_silu(later_pre, stoch_gain_ref[...], stoch_bias_ref[...])
        later_ref[rows, :] = later.astype(bf16)
        for step in range(share):
            state = advance(1 + chunk * share + step, state)
        return state

    state = lax.fori_loop(0, chunks, several, state)
    later_ref.flush()
    later_pre_ref.flush()
    lax.fori_loop(1 + chunks * share, length, advance, state, unroll=7)
    gates_ref.flush()
    states_ref.flush()
    for pair in range(PAIRS):
        held_ref[:, lanes_of(pair)] = states_ref[pair * frames : (pair + 1) * frames, :].astype(
            bf16
        )
    chosen = pick_columns(order_ref[:, : sent_ref.shape[0]], frames)
    held_ref.flush()
    sent_ref[:, :width] = mm_tn(chosen, held_ref[...]).astype(bf16)
    sent_ref[:, width:] = mm_tn(chosen, taken).astype(bf16)


def mixed_probs(logits):
    shifted = jnp.exp(logits - jnp.max(logits, 1, keepdims=True))
    probability = shifted / jnp.sum(shifted, 1, keepdims=True)
    return probability, (1.0 - unimix) * probability + unimix / CLASSES


def softmax_back(probability, grad):
    grad = (1.0 - unimix) * grad
    return probability * (grad - jnp.sum(probability * grad, 1, keepdims=True))


def heads_kernel(
    core_ref,
    camera_ref,
    held_ref,
    prior_hidden_ref,
    prior_gain_ref,
    prior_bias_ref,
    prior_out_ref,
    prior_shift_ref,
    embed_ref,
    camera_scale_ref,
    post_deter_ref,
    post_embed_ref,
    post_gain_ref,
    post_bias_ref,
    post_out_ref,
    post_shift_ref,
    post_low_ref,
    prior_low_ref,
    small_ref,
    keep_ref,
    send_ref,
    post_act_ref,
    prior_act_ref,
    scaled_ref,
):
    frames, width = held_ref.shape
    features = embed_ref.shape[1]
    length = frames // 2
    held = held_ref[...]
    split = (GROUPS, CLASSES, frames)
    prior_pre = mm(held, prior_hidden_ref[...])
    prior_act = norm_silu(prior_pre, prior_gain_ref[...], prior_bias_ref[...]).astype(bf16)
    prior_logits = mm(prior_act, prior_out_ref[...]) + prior_shift_ref[...]
    prior_prob, prior_mix = mixed_probs(prior_logits.T.reshape(split))
    for s in range(2):
        rows = slice(s * length, (s + 1) * length)
        scale = scale_row(camera_ref, camera_scale_ref, s, slice(0, features))
        scaled_ref[rows, :] = (embed_ref[rows, :].astype(f32) * scale).astype(bf16)
    post_pre = mm(held, post_deter_ref[...]) + mm(scaled_ref[...], post_embed_ref[...])
    post_act = norm_silu(post_pre, post_gain_ref[...], post_bias_ref[...]).astype(bf16)
    post_logits = mm(post_act, post_out_ref[...]) + post_shift_ref[...]
    post_prob, post_mix = mixed_probs(post_logits.T.reshape(split))
    ratio = jnp.log(post_mix) - jnp.log(prior_mix)
    divergence = jnp.sum(jnp.sum(post_mix * ratio, 0, keepdims=True), 1, keepdims=True)
    slope = sigmoid(divergence - free_bits)
    post_log = softmax_back(post_prob, slope * (ratio + 1.0))
    prior_log = softmax_back(prior_prob, -slope * (post_mix / prior_mix))
    post_log = post_log.reshape(GROUPS * CLASSES, frames).T.astype(bf16)
    prior_log = prior_log.reshape(GROUPS * CLASSES, frames).T.astype(bf16)
    post_low, post_gain_grad, post_bias_grad = norm_silu_back(
        post_pre, post_gain_ref[...], post_bias_ref[...], mm_nt(post_log, post_out_ref[...])
    )
    prior_low, prior_gain_grad, prior_bias_grad = norm_silu_back(
        prior_pre, prior_gain_ref[...], prior_bias_ref[...], mm_nt(prior_log, prior_out_ref[...])
    )
    post_low, prior_low = post_low.astype(bf16), prior_low.astype(bf16)
    post_low_ref[...] = post_low
    prior_low_ref[...] = prior_low
    post_low_ref.flush()
    prior_low_ref.flush()
    small_ref[...] = jnp.concatenate(
        [
            post_gain_grad,
            post_bias_grad,
            prior_gain_grad,
            prior_bias_grad,
            jnp.sum(post_log.astype(f32), 0, keepdims=True),
            jnp.sum(prior_log.astype(f32), 0, keepdims=True),
        ],
        1,
    )
    post_act_ref[...] = post_act
    prior_act_ref[...] = prior_act
    products = (
        (held_ref, post_low),
        (held_ref, prior_low),
        (post_act_ref, post_log[:, :width]),
        (post_act_ref, post_log[:, width:]),
        (prior_act_ref, prior_log[:, :width]),
        (prior_act_ref, prior_log[:, width:]),
    )
    shares = keep_ref.shape[0] // 2
    unit_rows, embed_rows = width // shares, features // shares
    small, large = unit_rows // 4, embed_rows // 4
    for slot, ref in ((1, send_ref), (0, keep_ref)):
        parity = core_ref[0] ^ slot
        for y in range(shares // 2):
            share = 2 * y + parity
            places = [block_place(parity, y, block) for block in range(4)]
            for block in range(4):
                at = pl.multiple_of(share * embed_rows + block * large, large)
                grad = mm_tn(scaled_ref[:, pl.ds(at, large)], post_low)
                ref[places[block], :large, :] = grad.astype(bf16)
            at = pl.multiple_of(share * unit_rows, unit_rows)
            for index, (left, right) in enumerate(products):
                grad = mm_tn(left[:, pl.ds(at, unit_rows)], right).astype(bf16)
                first = large + index * small
                for block in range(4):
                    ref[places[block], first : first + small, :] = grad[
                        block * small : (block + 1) * small
                    ]
        ref.flush()


def block_place(parity, y, block):
    low_bit, next_bit = block // 2, block % 2
    return jnp.where(
        parity == 0, 4 * y + 2 * low_bit + next_bit, 4 * next_bit + 2 * y + low_bit
    )


def embed_back_kernel(
    camera_ref,
    embed_ref,
    camera_scale_ref,
    post_low_ref,
    prior_low_ref,
    post_embed_ref,
    post_deter_ref,
    prior_hidden_ref,
    held_grad_ref,
    embed_grad_ref,
    camera_grad_ref,
):
    frames, features = embed_ref.shape
    length = frames // 2
    cameras = camera_scale_ref.shape[0]
    held_grad_ref[...] = mm_nt(post_low_ref[...], post_deter_ref[...]) + mm_nt(
        prior_low_ref[...], prior_hidden_ref[...]
    )
    wide = features // 4
    for q in range(4):
        columns = slice(q * wide, (q + 1) * wide)
        scaled_grad = mm_nt(post_low_ref[...], post_embed_ref[columns, :])
        terms = [jnp.zeros((1, wide), f32) for _ in range(cameras)]
        for s in range(2):
            rows = slice(s * length, (s + 1) * length)
            part = scaled_grad[rows]
            scale = scale_row(camera_ref, camera_scale_ref, s, columns)
            embed_grad_ref[rows, columns] = part * scale
            term = jnp.sum(part * embed_ref[rows, columns].astype(f32), 0, keepdims=True)
            for c in range(cameras):
                terms[c] = terms[c] + jnp.where(camera_ref[s] == c, term, 0.0)
        camera_grad_ref[:, columns] = jnp.concatenate(terms, 0)


def cell_gates(units, cell_ref, pair):
    scaled = units * cell_ref[:1, gates_of(pair)] + cell_ref[1:, gates_of(pair)]
    reset = sigmoid(scaled[:, :LANES])
    middle = scaled[:, LANES : 2 * LANES]
    return reset, middle, jnp.tanh(reset * middle), sigmoid(scaled[:, 2 * LANES :] - 1.0)


def rollout_kernel(
    got_ref,
    inputs_ref,
    ordered_ref,
    state_ref,
    cell_ref,
    cot_ref,
    states_ref,
    held_ref,
    back_ref,
    gate_grad_ref,
    cell_grad_ref,
    unit_ref,
    scale_ref,
    part_ref,
    gain_grad_ref,
    bias_grad_ref,
    turned_ref,
):
    horizon, count, width = states_ref.shape
    unit_ref[:count, :] = mm(got_ref[:, width:], ordered_ref[...])
    chunk = (horizon - 1) * count // 2
    for at in range(0, (horizon - 1) * count, chunk):
        rows = slice(count + at, count + at + chunk)
        unit_ref[rows, :] = mm(inputs_ref[at : at + chunk, :], ordered_ref[...])
    norm = 1.0 / (PAIRS * GATE)

    def advance(step, state):
        rows = pl.ds(pl.multiple_of(step * count, count), count)
        held = state.astype(bf16)
        held_ref[rows, :] = held
        values = []
        total = jnp.zeros((count, LANES), f32)
        square = jnp.zeros((count, LANES), f32)
        for pair in range(PAIRS):
            value = unit_ref[rows, gates_of(pair)] + mm(
                held[:, lanes_of(pair)], state_ref[lanes_of(pair), :]
            )
            values.append(value)
            for p in range(3):
                piece = value[:, lanes_of(p)]
                total = total + piece
                square = square + piece * piece
        mean = jnp.sum(total, 1, keepdims=True) * norm
        spread = jnp.sum(square, 1, keepdims=True) * norm - mean * mean
        factor = lax.rsqrt(jnp.maximum(spread, 0.0) + epsilon)
        scale_ref[rows, :] = jnp.broadcast_to(factor, (count, LANES))
        fresh = []
        for pair in range(PAIRS):
            units = (values[pair] - mean) * factor
            unit_ref[rows, gates_of(pair)] = units
            _, _, candidate, update = cell_gates(units, cell_ref, pair)
            old = state[:, lanes_of(pair)]
            fresh.append(old + update * (candidate - old))
        renewed = jnp.concatenate(fresh, 1)
        states_ref[step] = renewed
        return renewed

    ready(state_ref, cell_ref)
    first = got_ref[:, :width].astype(f32)
    lax.fori_loop(0, horizon, advance, first, unroll=5)
    held_ref.flush()
    states_ref.flush()
    turned_ref[...] = state_ref[...].astype(f32).T.astype(bf16)
    ready(cot_ref)
    gain_grad_ref[...] = jnp.zeros_like(gain_grad_ref)
    bias_grad_ref[...] = jnp.zeros_like(bias_grad_ref)

    def retreat(index, carry):
        step = horizon - 1 - index
        rows = pl.ds(pl.multiple_of(step * count, count), count)
        before = states_ref[jnp.maximum(step - 1, 0)]
        before = jnp.where(step == 0, first, before)
        grads = cot_ref[step].astype(f32) + carry
        low = jnp.zeros((count, LANES), f32)
        high = jnp.zeros((count, LANES), f32)
        kept = []
        for pair in range(PAIRS):
            units = unit_ref[rows, gates_of(pair)]
            reset, middle, candidate, update = cell_gates(units, cell_ref, pair)
            grad = grads[:, lanes_of(pair)]
            rest = 1.0 - update
            inner = grad * update * (1.0 - candidate * candidate)
            parts = jnp.concatenate(
                [
                    inner * middle * (reset * (1.0 - reset)),
                    inner * reset,
                    grad * (candidate - before[:, lanes_of(pair)]) * (update * rest),
                ],
                1,
            )
            weighted = parts * units
            gain_grad_ref[:, gates_of(pair)] += jnp.sum(weighted.reshape(count // 8, 8, GATE), 0)
            bias_grad_ref[:, gates_of(pair)] += jnp.sum(parts.reshape(count // 8, 8, GATE), 0)
            parts = parts * cell_ref[:1, gates_of(pair)]
            weighted = parts * units
            for p in range(3):
                low = low + parts[:, lanes_of(p)]
                high = high + weighted[:, lanes_of(p)]
            part_ref[:, gates_of(pair)] = parts
            kept.append(grad * rest)
        low = jnp.sum(low, 1, keepdims=True) * norm
        high = jnp.sum(high, 1, keepdims=True) * norm
        factor = scale_ref[rows, :][:, :1]
        carried = []
        for pair in range(PAIRS):
            units = unit_ref[rows, gates_of(pair)]
            grad = (factor * (part_ref[:, gates_of(pair)] - low - units * high)).astype(bf16)
            gate_grad_ref[rows, gates_of(pair)] = grad
            carried.append(kept[pair] + mm(grad, turned_ref[:, lanes_of(pair)]))
        return jnp.concatenate(carried, 1)

    carry = lax.fori_loop(0, horizon, retreat, jnp.zeros((count, width), f32), unroll=5)
    back_ref[:, :width] = carry.astype(bf16)
    back_ref[:, width:] = mm_nt(gate_grad_ref[:count, :], ordered_ref[...]).astype(bf16)
    cell_grad_ref[...] = jnp.concatenate(
        [
            jnp.sum(gain_grad_ref[...], 0, keepdims=True),
            jnp.sum(bias_grad_ref[...], 0, keepdims=True),
        ],
        0,
    )


def rollout_grads_kernel(
    gate_grad_ref,
    got_ref,
    inputs_ref,
    held_ref,
    pre_ref,
    cat_ref,
    ordered_ref,
    stoch_gain_ref,
    stoch_bias_ref,
    input_grad_ref,
    state_grad_ref,
    table_grad_ref,
    stoch_grad_ref,
    hot_ref,
    low_ref,
    taken_ref,
):
    steps, _, count = cat_ref.shape
    width = inputs_ref.shape[1]
    taken_ref[:count, :] = got_ref[:, width:]
    taken_ref[count:, :] = inputs_ref[...]
    input_grad_ref[...] = mm_tn(taken_ref[...], gate_grad_ref[...])
    input_grad_ref.flush()
    for pair in range(PAIRS):
        state_grad_ref[pair] = mm_tn(held_ref[:, lanes_of(pair)], gate_grad_ref[:, gates_of(pair)])
    state_grad_ref.flush()
    gain_sum = jnp.zeros(stoch_gain_ref.shape, f32)
    bias_sum = jnp.zeros(stoch_bias_ref.shape, f32)
    grads = mm_nt(gate_grad_ref[count:, :], ordered_ref[...])
    for at in range(0, steps, 2):
        rows = slice(at * count, (at + 2) * count)
        low, gain_grad, bias_grad = norm_silu_back(
            pre_ref[rows, :], stoch_gain_ref[...], stoch_bias_ref[...], grads[rows]
        )
        gain_sum = gain_sum + gain_grad
        bias_sum = bias_sum + bias_grad
        low_ref[rows, :] = low.astype(bf16)
        hot_ref[:, rows] = hot_columns([cat_ref[at], cat_ref[at + 1]])
    table_grad_ref[...] = mm(hot_ref[...], low_ref[...])
    stoch_grad_ref[...] = jnp.concatenate([gain_sum, bias_sum], 1)


def observe_back_kernel(
    core_ref,
    held_grad_ref,
    back_ref,
    order_ref,
    cat_ref,
    taken_ref,
    pre_ref,
    gates_ref,
    states_ref,
    start_ref,
    stoch_gain_ref,
    stoch_bias_ref,
    ordered_ref,
    state_ref,
    cell_ref,
    input_part_ref,
    state_part_ref,
    table_part_ref,
    stoch_part_ref,
    cell_part_ref,
    small_ref,
    camera_grad_ref,
    start_grad_ref,
    keep_ref,
    send_ref,
    grads_ref,
    turned_ref,
    arriving_ref,
    slope_ref,
    factor_ref,
    unit_ref,
    mean_ref,
    cross_ref,
    rest_ref,
    flat_ref,
    lean_ref,
    scale_ref,
    grad_ref,
    low_ref,
    high_ref,
    previous_ref,
):
    frames, width = held_grad_ref.shape
    length = frames // 2
    norm = 1.0 / (PAIRS * GATE)
    chosen = pick_columns(order_ref[:, : back_ref.shape[0]], frames)
    held_grad = held_grad_ref[...] + mm(chosen, back_ref[:, :width])
    turned_ref[...] = state_ref[...].astype(f32).T.astype(bf16)
    start = jnp.concatenate(
        [start_ref[:, lanes_of(pair)].astype(f32) for pair in range(PAIRS)], 0
    )
    for pair in range(PAIRS):
        arriving_ref[pair * frames : (pair + 1) * frames, :] = held_grad[:, lanes_of(pair)]
    long = PAIRS * frames
    for s in range(2):
        blocks = [
            slice((2 * pair + s) * length, (2 * pair + s + 1) * length) for pair in range(PAIRS)
        ]
        total = jnp.zeros((length, LANES), f32)
        for rows in blocks:
            for p in range(3):
                total = total + gates_ref[p * long + rows.start : p * long + rows.stop, :]
        mean = jnp.sum(total, 1, keepdims=True) * norm
        square = jnp.zeros((length, LANES), f32)
        for rows in blocks:
            for p in range(3):
                center = gates_ref[p * long + rows.start : p * long + rows.stop, :] - mean
                square = square + center * center
        scale = lax.rsqrt(jnp.sum(square, 1, keepdims=True) * norm + epsilon)
        for pair, rows in enumerate(blocks):
            gain = cell_ref[:1, gates_of(pair)]
            units = jnp.concatenate(
                [gates_ref[p * long + rows.start : p * long + rows.stop, :] for p in range(3)], 1
            )
            units = (units - mean) * scale
            reset, middle, candidate, update = cell_gates(units, cell_ref, pair)
            row = 2 * pair + s
            previous = jnp.where(
                iota((length, LANES), 0) == 0,
                start[row : row + 1, :],
                pltpu.roll(states_ref[rows, :], 1, 0),
            )
            previous_ref[rows, :] = previous
            inner = update * (1.0 - candidate * candidate)
            slope = jnp.concatenate(
                [
                    inner * middle * (reset * (1.0 - reset)),
                    inner * reset,
                    (candidate - previous) * (update * (1.0 - update)),
                ],
                1,
            )
            slope_ref[rows, :] = slope
            slope = slope * gain
            weighted = slope * units
            mean_ref[rows, :] = norm * (
                slope[:, :LANES] + slope[:, LANES : 2 * LANES] + slope[:, 2 * LANES :]
            )
            cross_ref[rows, :] = norm * (
                weighted[:, :LANES] + weighted[:, LANES : 2 * LANES] + weighted[:, 2 * LANES :]
            )
            for p in range(3):
                factor_ref[p * long + rows.start : p * long + rows.stop, :] = (
                    scale * slope[:, lanes_of(p)]
                )
            unit_ref[rows, :] = scale * units
            rest_ref[rows, :] = 1.0 - update
            scale_ref[rows, :] = jnp.broadcast_to(scale, (length, LANES))
            weight = state_ref[lanes_of(pair), :]
            flat_ref[rows, :] = scale * mm_nt(jnp.ones((8, GATE), bf16), weight)[:1, :]
            lean_ref[rows, :] = mm_nt((scale * units).astype(bf16), weight)
    row_pair = iota((8, LANES), 0) // 2

    def retreat(index, carry):
        step = length - 1 - index
        rows = pl.ds(step, 8, stride=length)
        grad = arriving_ref[rows, :] + carry
        wide = jnp.concatenate(
            [grad * factor_ref[pl.ds(p * long + step, 8, stride=length), :] for p in range(3)], 1
        )
        turned = mm(wide.astype(bf16), turned_ref[...])
        low = jnp.sum(group_sum(grad * mean_ref[rows, :]), 1, keepdims=True)
        high = jnp.sum(group_sum(grad * cross_ref[rows, :]), 1, keepdims=True)
        grad_ref[rows, :] = grad
        low_ref[rows, :] = jnp.broadcast_to(low, (8, LANES))
        high_ref[rows, :] = jnp.broadcast_to(high, (8, LANES))
        kept = grad * rest_ref[rows, :] - low * flat_ref[rows, :] - high * lean_ref[rows, :]
        for pair in range(PAIRS):
            kept = kept + jnp.where(row_pair == pair, turned[:, lanes_of(pair)], 0.0)
        return kept

    carry = lax.fori_loop(0, length, retreat, jnp.zeros((8, LANES), f32), unroll=8)
    for pair in range(PAIRS):
        start_grad_ref[:, lanes_of(pair)] = carry[2 * pair : 2 * pair + 2, :]
    frame = iota((frames, width), 0) % length
    earlier = jnp.where(frame == 0, 0.0, pltpu.roll(taken_ref[...].astype(f32), 1, 0)).astype(bf16)
    input_grad = jnp.zeros((frames, width), f32)
    gains, biases, inputs = [], [], []
    shares = grads_ref.shape[0]
    unit_rows = width // shares
    for pair in range(PAIRS):
        rows = slice(pair * frames, (pair + 1) * frames)
        grad = jnp.concatenate([grad_ref[rows, :]] * 3, 1)
        gate_grad = grad * slope_ref[rows, :]
        biases.append(jnp.sum(gate_grad, 0, keepdims=True))
        scale = scale_ref[rows, :][:, :1]
        units = unit_ref[rows, :]
        gains.append(jnp.sum(gate_grad * (units / scale), 0, keepdims=True))
        low = low_ref[rows, :][:, :1]
        high = high_ref[rows, :][:, :1]
        factors = jnp.concatenate(
            [factor_ref[p * long + rows.start : p * long + rows.stop, :] for p in range(3)], 1
        )
        gate_low = (grad * factors - low * scale - high * units).astype(bf16)
        columns = ordered_ref[:, gates_of(pair)]
        input_grad = input_grad + mm_nt(gate_low, columns)
        weight_grad = mm_tn(earlier, gate_low) + input_part_ref[:, gates_of(pair)]
        inputs.append(weight_grad.astype(bf16))
        state_grad = mm_tn(previous_ref[rows, :].astype(bf16), gate_low) + state_part_ref[pair]
        half = LANES // 2
        upper = iota((half, GATE), 1) % LANES < half
        folded = jnp.where(upper, state_grad[:half], state_grad[half:])
        at = 3 * unit_rows + 2 * unit_rows
        grads_ref[pair, at : at + half, :GATE] = folded.astype(bf16)
    weights = jnp.concatenate(inputs, 1)
    for q in range(shares):
        for c in range(3):
            grads_ref[q, c * unit_rows : (c + 1) * unit_rows, :] = weights[
                q * unit_rows : (q + 1) * unit_rows, c * width : (c + 1) * width
            ]
    taken_grad = jnp.where(
        frame == length - 1, 0.0, pltpu.roll(input_grad, frames - 1, 0)
    ) + mm(chosen, back_ref[:, width:])
    low, gain_grad, bias_grad = norm_silu_back(
        pre_ref[...], stoch_gain_ref[...], stoch_bias_ref[...], taken_grad
    )
    stoch = jnp.concatenate([gain_grad, bias_grad], 1) + stoch_part_ref[...]
    hot = hot_columns([cat_ref[s] for s in range(2)])
    table_grad = mm(hot, low.astype(bf16)) + table_part_ref[...]
    rows = table_grad.shape[0] // shares
    vector_row = 5 * unit_rows
    classes = GROUPS * CLASSES
    wide = camera_grad_ref.shape[1] // shares
    for q in range(shares):
        grads_ref[q, 3 * unit_rows : 3 * unit_rows + rows, :] = table_grad[
            q * rows : (q + 1) * rows
        ].astype(bf16)
        unit = slice(q * unit_rows, (q + 1) * unit_rows)
        logit = slice(q * classes // shares, (q + 1) * classes // shares)
        units = [stoch[:, unit], stoch[:, width + unit.start : width + unit.stop]]
        units += [
            small_ref[:, k * width + unit.start : k * width + unit.stop] for k in range(4)
        ]
        logits = [
            small_ref[
                :, 4 * width + k * classes + logit.start : 4 * width + k * classes + logit.stop
            ]
            for k in range(2)
        ]
        cells = [
            plain_row(kind[q] + cell_part_ref[k : k + 1, gates_of(q)])
            for k, kind in enumerate((gains, biases))
        ]
        cameras = [
            camera_grad_ref[c : c + 1, q * wide : (q + 1) * wide]
            for c in range(camera_grad_ref.shape[0])
        ]
        lines = []
        for vector in units + logits + cells + cameras:
            lines += [vector[:, at : at + LANES] for at in range(0, vector.shape[1], LANES)]
        lines.append(jnp.zeros((LANES // 2 - len(lines), LANES), f32))
        grads_ref[q, vector_row:, GATE:] = jnp.concatenate(lines, 0).astype(bf16)
    block = keep_ref.shape[1]
    for slot, ref in ((0, keep_ref), (1, send_ref)):
        parity = core_ref[0] ^ slot
        for y in range(shares // 2):
            for index in range(4):
                at = index * block
                ref[block_place(parity, y, index)] = grads_ref[
                    2 * y + parity, at : at + block, :
                ]


def place_blocks(where_ref, own_ref, got_ref, full_ref):
    block = own_ref.shape[0] // 2
    parity, bit = where_ref[0], where_ref[1]
    for side in range(2):
        for inner in range(2):
            rows = slice(inner * block, (inner + 1) * block)
            piece = jnp.where(bit == side, own_ref[rows, :], got_ref[rows, :]).astype(f32)
            place = jnp.where(parity == 0, 2 * side + inner, 2 * inner + side)
            full_ref[pl.ds(pl.multiple_of(place * block, block), block), :] = piece


def finish_heads_kernel(
    where_ref,
    own_ref,
    got_ref,
    post_embed_ref,
    post_deter_ref,
    prior_hidden_ref,
    post_out_ref,
    prior_out_ref,
    full_ref,
):
    place_blocks(where_ref, own_ref, got_ref, full_ref)
    block = full_ref.shape[0] // 4
    width = own_ref.shape[1]
    large, small = post_embed_ref.shape[0] // 4, post_deter_ref.shape[0] // 4
    for index in range(4):
        at = index * block
        post_embed_ref[index * large : (index + 1) * large, :] = full_ref[at : at + large, :]
        rows = slice(index * small, (index + 1) * small)
        for member, (ref, column) in enumerate(
            (
                (post_deter_ref, 0),
                (prior_hidden_ref, 0),
                (post_out_ref, 0),
                (post_out_ref, width),
                (prior_out_ref, 0),
                (prior_out_ref, width),
            )
        ):
            first = at + large + member * small
            ref[rows, column : column + width] = full_ref[first : first + small, :]


def finish_kernel(where_ref, own_ref, got_ref, *refs):
    outs, full_ref = refs[:-1], refs[-1]
    width = own_ref.shape[1]
    place_blocks(where_ref, own_ref, got_ref, full_ref)
    input_ref, table_ref, state_ref = outs[:3]
    unit_rows = input_ref.shape[0]
    for pair in range(PAIRS):
        parts = []
        for p in range(3):
            at = pair * GATE + p * LANES
            line, column = at // width * unit_rows, at % width
            parts.append(full_ref[line : line + unit_rows, column : column + LANES])
        input_ref[:, gates_of(pair)] = plain_row(jnp.concatenate(parts, 1))
    at = 3 * unit_rows
    table_ref[...] = full_ref[at : at + table_ref.shape[0], :]
    at += table_ref.shape[0]
    half = state_ref.shape[1]
    folded = full_ref[at : at + half, :]
    for e in range(2):
        state_ref[e] = jnp.concatenate(
            [folded[:, (2 * p + e) * half : (2 * p + e + 1) * half] for p in range(3)], 1
        )
    for ref in outs[3:14]:
        for line in range(ref.shape[0]):
            for column in range(0, ref.shape[1], LANES):
                ref[line : line + 1, column : column + LANES] = full_ref[at : at + 1, GATE:]
                at += 1


def struct(shape, dtype):
    return jax.ShapeDtypeStruct(shape, dtype)


class Incoming:
    def __init__(self, ref, copy):
        self.ref, self.copy, self.shape = ref, copy, ref.shape
        copy.start()

    def ready(self):
        if self.copy is not None:
            self.copy.wait()
            self.copy = None

    def __getitem__(self, index):
        self.ready()
        return self.ref[index]


class Outgoing:
    def __init__(self, ref, copy):
        self.ref, self.copy, self.shape, self.started = ref, copy, ref.shape, False

    def __getitem__(self, index):
        return self.ref[index]

    def __setitem__(self, index, value):
        self.ref[index] = value

    def flush(self):
        if not self.started:
            self.copy.start()
            self.started = True


def ready(*refs):
    for ref in refs:
        if isinstance(ref, Incoming):
            ref.ready()


def call(kernel, name, outs, ins, mib, scratch=(), scalars=0, after=(), near_in=(), near_out=()):
    count, total = len(ins), len(ins) + len(after) + len(outs)
    far_in = [k for k in range(scalars, count) if k not in near_in]
    far_out = [k for k in range(len(outs)) if k not in near_out]
    near = pl.BlockSpec(memory_space=pltpu.VMEM)
    far = pl.BlockSpec(memory_space=pltpu.HBM)

    def body(*refs):
        given, made = list(refs[:count]), list(refs[count + len(after) : total])
        places = refs[total : total + len(far_in) + len(far_out)]
        rest = refs[total + len(far_in) + len(far_out) : -1]
        marks = refs[-1]
        for at, k in enumerate(far_in):
            copy = pltpu.make_async_copy(given[k], places[at], marks.at[at])
            given[k] = Incoming(places[at], copy)
        for at, k in enumerate(far_out, len(far_in)):
            copy = pltpu.make_async_copy(places[at], made[k], marks.at[at])
            made[k] = Outgoing(places[at], copy)
        kernel(*given, *made, *rest)
        ready(*given)
        for k in far_out:
            made[k].flush()
        for k in far_out:
            made[k].copy.wait()

    return pl.pallas_call(
        body,
        out_shape=tuple(
            pltpu.HBM(out.shape, out.dtype) if k in far_out else out for k, out in enumerate(outs)
        ),
        in_specs=[pl.BlockSpec(memory_space=pltpu.SMEM)] * scalars
        + [far if k in far_in else near for k in range(scalars, count)]
        + [far] * len(after),
        out_specs=tuple(far if k in far_out else near for k in range(len(outs))),
        scratch_shapes=[pltpu.VMEM(ins[k].shape, ins[k].dtype) for k in far_in]
        + [pltpu.VMEM(outs[k].shape, outs[k].dtype) for k in far_out]
        + list(scratch)
        + [pltpu.SemaphoreType.DMA((len(far_in) + len(far_out),))],
        compiler_params=pltpu.CompilerParams(vmem_limit_bytes=mib * 1024 * 1024),
        name=name,
    )(
        *[
            pltpu.with_memory_space_constraint(member, pltpu.HBM) if k in far_in else member
            for k, member in enumerate(ins)
        ],
        *[pltpu.with_memory_space_constraint(member, pltpu.HBM) for member in after],
    )


def linear_bits(bits):
    own = bits[0]
    rep_count = lax.axis_size("rep")
    index = lax.axis_index("seq") * rep_count + lax.axis_index("rep")
    if bits[0] != bits[1]:
        own = jnp.where(index & 1 == 0, bits[0], bits[1])
    return (index >> own) & 1


def swap(values, bits):
    count = lax.axis_size("seq") * lax.axis_size("rep")
    return lax.ppermute(
        values, ("seq", "rep"), [(i, i ^ (1 << bits[i & 1])) for i in range(count)]
    )


class Terms:
    def __init__(self, member):
        self.members = [(member, [])]

    def add(self, member):
        self.members.append((member, []))

    def part(self, *sides):
        total = 0.0
        for member, path in self.members:
            path = path + list(sides)
            rows = member.shape[0] >> len(path)
            split = member.reshape((2,) * len(path) + (rows, member.shape[1]))
            one = (1,) * len(path) + split.shape[-2:]
            chosen = lax.dynamic_slice(split, path + [0, 0], one)
            total = total + chosen.reshape(split.shape[-2:]).astype(f32)
        return total.astype(bf16)

    def fold(self, arrived, bits):
        self.add(arrived)
        own = linear_bits(bits).astype(jnp.int32)
        send = self.part(1 - own)
        self.members = [(member, path + [own]) for member, path in self.members]
        return send


def added(left, right):
    return (left.astype(f32) + right.astype(f32)).astype(bf16)


def joined(values, got, bits):
    own = linear_bits(bits)
    return jnp.where(
        own == 0, jnp.concatenate([values, got], 0), jnp.concatenate([got, values], 0)
    )


class Chain:
    def __init__(self, keep, send, stages, merged):
        self.terms, self.piece = Terms(keep), None
        self.merged = merged
        self.folds, self.middle = list(stages), stages[-1]
        if merged:
            self.folds.pop()
        self.joins = list(reversed(stages[2:-1])) + [(stages[1][0], stages[0][1])]
        self.begin(send, (0, 0))

    def begin(self, send, bits):
        self.sent, self.last = send, bits
        self.arrived = swap(send, bits)

    def advance(self, *after):
        if after:
            self.arrived = lax.optimization_barrier((self.arrived, *after))[0]
        if self.folds:
            bits = self.folds.pop(0)
            self.begin(self.terms.fold(self.arrived, bits), bits)
            return
        if self.piece is None:
            bits = self.middle
            self.terms.add(self.arrived)
            self.piece = self.terms.part()
        else:
            bits = self.joins.pop(0)
            if self.merged and self.last == self.middle:
                self.piece = added(self.piece, self.arrived)
            else:
                self.piece = joined(self.piece, self.arrived, self.last)
        self.begin(self.piece, bits)


def on_device(
    start_deter,
    post_cat,
    embed,
    camera,
    start_order,
    imag_cat,
    imag_cot,
    stoch_table,
    stoch_gain,
    stoch_bias,
    state_weight,
    input_weight,
    cell_gain,
    cell_bias,
    prior_hidden,
    prior_gain,
    prior_bias,
    prior_out,
    prior_shift,
    post_deter,
    post_embed,
    post_gain,
    post_bias,
    post_out,
    post_shift,
    camera_scale,
):
    seq_count, length = post_cat.shape[:2]
    frames = seq_count * length
    count, horizon, width = imag_cot.shape
    features = embed.shape[-1]
    shares = lax.axis_size("rep")
    rep_bits = shares.bit_length() - 1
    seq_bits = lax.axis_size("seq").bit_length() - 1
    half = LANES // 2
    gate_count = 3 * width
    classes = GROUPS * CLASSES
    rows = horizon * count
    long = PAIRS * frames
    unit_rows = width // shares
    core = (lax.axis_index("rep") & 1).astype(jnp.int32).reshape(1)
    row = lambda vector: vector.reshape(1, -1)
    cat = jnp.swapaxes(post_cat, 1, 2)
    later_cat = jnp.transpose(imag_cat, (1, 2, 0))
    stoch_rows = (row(stoch_gain), row(stoch_bias))
    embed_rows = embed.reshape(frames, features)

    low_bit, next_bit = rep_bits, rep_bits + 1
    deeper = [rep_bits + bit for bit in range(2, seq_bits)]
    outer = (low_bit, next_bit)
    stages = list(
        zip([1, low_bit, next_bit] + deeper, [next_bit, 1] + deeper + [low_bit], strict=True)
    )

    (
        held,
        taken,
        obs_pre,
        imag_inputs,
        imag_pre,
        obs_gates,
        obs_states,
        sent,
        ordered,
        state,
        cell,
    ) = call(
        observe_kernel,
        "observe",
        [
            struct((frames, width), bf16),
            struct((frames, width), bf16),
            struct((frames, width), f32),
            struct((rows - count, width), bf16),
            struct((rows - count, width), f32),
            struct((3 * long, LANES), f32),
            struct((long, LANES), f32),
            struct((count, 2 * width), bf16),
            struct((width, gate_count), bf16),
            struct((width, GATE), bf16),
            struct((2, gate_count), f32),
        ],
        (
            cat,
            stoch_table,
            *stoch_rows,
            input_weight,
            state_weight.reshape(width, 3 * half),
            cell_gain.reshape(-1, LANES),
            cell_bias.reshape(-1, LANES),
            start_deter,
            start_order,
            later_cat,
        ),
        26,
        scratch=[pltpu.VMEM((3 * long, LANES), f32)],
    )
    got = lax.all_to_all(sent, "seq", split_axis=0, concat_axis=0, tiled=True)

    square = struct((frames, width), bf16)
    embed_rows_count = features // shares
    head_rows = embed_rows_count + 6 * unit_rows
    blocks = struct((2 * shares, head_rows // 4, width), bf16)
    post_low, prior_low, head_small, keep, send = call(
        heads_kernel,
        "heads",
        [square, square, struct((1, 4 * width + 2 * classes), f32), blocks, blocks],
        (
            core,
            camera,
            held,
            prior_hidden,
            row(prior_gain),
            row(prior_bias),
            prior_out,
            row(prior_shift),
            embed_rows,
            camera_scale,
            post_deter,
            post_embed,
            row(post_gain),
            row(post_bias),
            post_out,
            row(post_shift),
        ),
        34,
        scratch=[
            pltpu.VMEM((frames, width), bf16),
            pltpu.VMEM((frames, width), bf16),
            pltpu.VMEM((frames, features), bf16),
        ],
        scalars=2,
    )
    flat = (shares * head_rows // 2, width)
    send, got = lax.optimization_barrier((send, got))
    tail_stages = list(
        zip([1, low_bit, next_bit] + deeper, [next_bit, 1, low_bit] + deeper, strict=True)
    )
    head = Chain(keep.reshape(flat), send.reshape(flat), stages, True)
    held_grad, embed_grad, camera_grad = call(
        embed_back_kernel,
        "embed_back",
        [
            struct((frames, width), f32),
            struct((frames, features), f32),
            struct(camera_scale.shape, f32),
        ],
        (
            camera,
            embed_rows,
            camera_scale,
            post_low,
            prior_low,
            post_embed,
            post_deter,
            prior_hidden,
        ),
        18,
        scalars=1,
        after=(head.sent,),
    )
    head.advance(camera_grad)

    states, imag_held, back, gate_grads, cell_part = call(
        rollout_kernel,
        "rollout",
        [
            struct((horizon, count, width), f32),
            struct((rows, width), bf16),
            struct((count, 2 * width), bf16),
            struct((rows, gate_count), bf16),
            struct((2, gate_count), f32),
        ],
        (
            got,
            imag_inputs,
            ordered,
            state,
            cell,
            jnp.swapaxes(imag_cot, 0, 1),
        ),
        36,
        scratch=[
            pltpu.VMEM((rows, gate_count), f32),
            pltpu.VMEM((rows, LANES), f32),
            pltpu.VMEM((count, gate_count), f32),
            pltpu.VMEM((8, gate_count), f32),
            pltpu.VMEM((8, gate_count), f32),
            pltpu.VMEM((GATE, PAIRS * LANES), bf16),
        ],
        after=(head.sent,),
    )
    imag_deter = jnp.swapaxes(states, 0, 1)
    returned = lax.all_to_all(back, "seq", split_axis=0, concat_axis=0, tiled=True)
    head.advance(cell_part)

    input_part, state_part, table_part, stoch_part = call(
        rollout_grads_kernel,
        "rollout_grads",
        [
            struct((width, gate_count), f32),
            struct((PAIRS, LANES, GATE), f32),
            struct(stoch_table.shape, f32),
            struct((1, 2 * width), f32),
        ],
        (gate_grads, got, imag_inputs, imag_held, imag_pre, later_cat, ordered, *stoch_rows),
        30,
        scratch=[
            pltpu.VMEM((stoch_table.shape[0], rows - count), bf16),
            pltpu.VMEM((rows - count, width), bf16),
            pltpu.VMEM((rows, width), bf16),
        ],
        after=(head.sent,),
    )
    head.advance(stoch_part, returned)
    tail_rows = 5 * unit_rows + half
    blocks = struct((2 * shares, tail_rows // 4, width), bf16)
    start_grad, tail_keep, tail_send = call(
        observe_back_kernel,
        "observe_back",
        [struct((seq_count, width), f32), blocks, blocks],
        (
            core,
            held_grad,
            returned,
            start_order,
            cat,
            taken,
            obs_pre,
            obs_gates,
            obs_states,
            start_deter,
            *stoch_rows,
            ordered,
            state,
            cell,
            input_part,
            state_part,
            table_part,
            stoch_part,
            cell_part,
            head_small,
            camera_grad,
        ),
        30,
        after=(head.sent,),
        scratch=[
            pltpu.VMEM((shares, tail_rows, width), bf16),
            pltpu.VMEM((GATE, PAIRS * LANES), bf16),
            pltpu.VMEM((long, LANES), f32),
            pltpu.VMEM((long, GATE), f32),
            pltpu.VMEM((3 * long, LANES), f32),
            pltpu.VMEM((long, GATE), f32),
        ]
        + [pltpu.VMEM((long, LANES), f32)] * 10,
        scalars=1,
    )
    full = (2 * tail_rows, width)
    tail_send, head.arrived = lax.optimization_barrier((tail_send, head.arrived))
    for _ in deeper:
        head.advance()
    tail = Chain(tail_keep.reshape(full), tail_send.reshape(full), tail_stages, True)
    for step in range(2 * len(stages) - 2):
        if step in (0, 2):
            head.advance(tail.sent)
        tail.advance()
    while head.joins:
        head.advance(tail.sent)
    piece, other = tail.piece, tail.arrived
    head_piece, head_other = head.piece, head.arrived
    where = jnp.concatenate([core, linear_bits(outer).astype(jnp.int32).reshape(1)])
    unit = struct((1, unit_rows), f32)
    logit = struct((1, classes // shares), f32)
    gate = struct((3, LANES), f32)
    small_rows = struct((unit_rows, width), f32)
    wide_rows = struct((unit_rows, classes), f32)
    post_embed_grad, post_deter_grad, prior_hidden_grad, post_out_grad, prior_out_grad = call(
        finish_heads_kernel,
        "finish_heads",
        [
            struct((embed_rows_count, width), f32),
            small_rows,
            small_rows,
            wide_rows,
            wide_rows,
        ],
        (where, head_piece, head_other),
        18,
        scratch=[pltpu.VMEM((head_rows, width), f32)],
        scalars=1,
        near_in=(1, 2),
    )
    finished = call(
        finish_kernel,
        "finish",
        [
            struct((unit_rows, gate_count), f32),
            struct((stoch_table.shape[0] // shares, width), f32),
            struct((2, half, 3 * half), f32),
            *[unit] * 6,
            logit,
            logit,
            gate,
            gate,
            struct((camera_scale.shape[0], features // shares), f32),
        ],
        (where, piece, other),
        12,
        scratch=[pltpu.VMEM((tail_rows, width), f32)],
        scalars=1,
        near_in=(1, 2),
        after=(post_embed_grad,),
    )
    input_weight_grad, stoch_table_grad, state_weight_grad = finished[:3]
    (
        stoch_gain_grad,
        stoch_bias_grad,
        post_gain_grad,
        post_bias_grad,
        prior_gain_grad,
        prior_bias_grad,
        post_shift_grad,
        prior_shift_grad,
        cell_gain_grad,
        cell_bias_grad,
    ) = [member.reshape(-1) for member in finished[3:13]]
    return (
        imag_deter,
        embed_grad.reshape(embed.shape),
        start_grad,
        stoch_table_grad,
        stoch_gain_grad,
        stoch_bias_grad,
        state_weight_grad,
        input_weight_grad,
        cell_gain_grad,
        cell_bias_grad,
        prior_hidden_grad,
        prior_gain_grad,
        prior_bias_grad,
        prior_out_grad,
        prior_shift_grad,
        post_deter_grad,
        post_embed_grad,
        post_gain_grad,
        post_bias_grad,
        post_out_grad,
        post_shift_grad,
        finished[13],
    )


def solution(mesh):
    both = ("seq", "rep")
    in_specs = (
        P(both, None),
        P(both, None, None),
        P(both, None, None),
        P(both),
        P(both, None),
        P(both, None, None),
        P(both, None, None),
    ) + (P(),) * 19
    rows, flat = P("rep", None), P("rep")
    out_specs = (
        P(both, None, None),
        P(both, None, None),
        P(both, None),
        rows,
        flat,
        flat,
        P("rep", None, None),
        rows,
        flat,
        flat,
        rows,
        flat,
        flat,
        rows,
        flat,
        rows,
        rows,
        flat,
        flat,
        rows,
        flat,
        P(None, "rep"),
    )
    return jax.shard_map(
        on_device, mesh=mesh, in_specs=in_specs, out_specs=out_specs, check_vma=False
    )
```

```python
import jax
import jax.numpy as jnp
from jax import lax
from jax.experimental import pallas as pl
from jax.experimental.pallas import tpu as pltpu
from jax.sharding import PartitionSpec as P

BLOCKS = 8
GROUPS = 32
CLASSES = 32
PAIRS = BLOCKS // 2
LANES = 128
GATE = 3 * LANES

epsilon = 1e-05
unimix = 0.01
free_bits = 1.0

f32 = jnp.float32
bf16 = jnp.bfloat16


def iota(shape, axis):
    return lax.broadcasted_iota(jnp.int32, shape, axis)


def mm(left, right):
    return jnp.dot(left, right, preferred_element_type=f32)


def mm_nt(left, right):
    return lax.dot_general(left, right, (((1,), (1,)), ((), ())), preferred_element_type=f32)


def mm_tn(left, right):
    return lax.dot_general(left, right, (((0,), (0,)), ((), ())), preferred_element_type=f32)


def sigmoid(values):
    return 0.5 * jnp.tanh(0.5 * values) + 0.5


def row_mean(values):
    return jnp.sum(values, -1, keepdims=True) * (1.0 / values.shape[-1])


def hot_rows(columns):
    categories = jnp.concatenate([part.astype(f32).T for part in columns], 0).astype(bf16)
    count = categories.shape[0]
    width = GROUPS * CLASSES
    spread = (iota((GROUPS, width), 1) // CLASSES == iota((GROUPS, width), 0)).astype(f32)
    wide = mm(categories, spread.astype(bf16))
    own = (iota((count, width), 1) % CLASSES).astype(f32)
    return jnp.where(wide == own, 1.0, 0.0).astype(bf16)


def hot_columns(columns):
    categories = jnp.concatenate([part.astype(f32) for part in columns], 1).astype(bf16)
    count = categories.shape[1]
    width = GROUPS * CLASSES
    spread = (iota((width, GROUPS), 0) // CLASSES == iota((width, GROUPS), 1)).astype(f32)
    wide = mm(spread.astype(bf16), categories)
    own = (iota((width, count), 0) % CLASSES).astype(f32)
    return jnp.where(wide == own, 1.0, 0.0).astype(bf16)


def normed(values):
    center = values - row_mean(values)
    scale = lax.rsqrt(row_mean(center * center) + epsilon)
    return center * scale, scale


def norm_silu(values, factor, offset):
    act = normed(values)[0] * factor + offset
    return act * sigmoid(act)


def norm_silu_back(values, factor, offset, grad):
    unit, scale = normed(values)
    act = unit * factor + offset
    gate = sigmoid(act)
    act_grad = grad * (gate + act * gate * (1.0 - gate))
    unit_grad = act_grad * factor
    pre_grad = scale * (unit_grad - row_mean(unit_grad) - unit * row_mean(unit_grad * unit))
    return (
        pre_grad,
        jnp.sum(act_grad * unit, 0, keepdims=True),
        jnp.sum(act_grad, 0, keepdims=True),
    )


def pick_columns(chosen, count):
    return jnp.where(iota((count, chosen.shape[1]), 0) == chosen, 1.0, 0.0).astype(bf16)


def column_order():
    source, target = iota((GATE, GATE), 0), iota((GATE, GATE), 1)
    half = LANES // 2
    moved = source // half % 3 * LANES + source // (3 * half) * half + source % half
    return jnp.where(moved == target, 1.0, 0.0).astype(bf16)


def pair_row(ref, pair):
    half = LANES // 2
    pieces = []
    for p in range(3):
        for e in range(2):
            at = pair * GATE + (3 * e + p) * half
            line, lane = at // LANES, at % LANES
            pieces.append(ref[line : line + 1, lane : lane + half])
    return jnp.concatenate(pieces, 1)


def plain_row(row):
    half = LANES // 2
    return jnp.concatenate(
        [
            row[:, (2 * p + e) * half : (2 * p + e + 1) * half]
            for e in range(2)
            for p in range(3)
        ],
        1,
    )


def group_sum(values):
    values = values + pltpu.roll(values, 4, 0)
    return values + pltpu.roll(values, 2, 0)


def lanes_of(pair):
    return slice(pair * LANES, (pair + 1) * LANES)


def gates_of(pair):
    return slice(pair * GATE, (pair + 1) * GATE)


def scale_row(camera_ref, camera_scale_ref, s, columns):
    row = None
    for c in range(camera_scale_ref.shape[0]):
        part = jnp.where(camera_ref[s] == c, camera_scale_ref[c : c + 1, columns], 0.0)
        row = part if row is None else row + part
    return row


def observe_kernel(
    camera_ref,
    cat_ref,
    table_ref,
    stoch_gain_ref,
    stoch_bias_ref,
    input_ref,
    weight_ref,
    cell_gain_ref,
    cell_bias_ref,
    start_ref,
    order_ref,
    later_cat_ref,
    embed_ref,
    camera_scale_ref,
    post_embed_ref,
    held_ref,
    taken_ref,
    pre_ref,
    later_ref,
    later_pre_ref,
    gates_ref,
    states_ref,
    sent_ref,
    ordered_ref,
    state_ref,
    cell_ref,
    scaled_ref,
    embed_part_ref,
    inputs_ref,
):
    frames, width = held_ref.shape
    length = frames // 2
    half = LANES // 2
    pre = mm(hot_rows([cat_ref[s] for s in range(2)]), table_ref[...])
    pre_ref[...] = pre
    taken = norm_silu(pre, stoch_gain_ref[...], stoch_bias_ref[...]).astype(bf16)
    taken_ref[...] = taken
    order = column_order()
    for pair in range(PAIRS):
        columns = mm(input_ref[:, gates_of(pair)], order).astype(bf16)
        ordered_ref[:, gates_of(pair)] = columns
        values = mm(taken, columns)
        for p in range(3):
            at = p * PAIRS * frames + pair * frames
            inputs_ref[at : at + frames, :] = values[:, lanes_of(p)]
    source, target = iota((3 * half, GATE), 0), iota((3 * half, GATE), 1)
    same = (source // half == target // LANES) & (source % half == target % half)
    weights = mm(weight_ref[...], jnp.where(same, 1.0, 0.0).astype(bf16))
    own = iota(weights.shape, 0) // half % 2 == iota(weights.shape, 1) // half % 2
    state_ref[...] = jnp.where(own, weights, 0.0).astype(bf16)
    gain_rows = [pair_row(cell_gain_ref, pair) for pair in range(PAIRS)]
    bias_rows = [pair_row(cell_bias_ref, pair) for pair in range(PAIRS)]
    cell_ref[...] = jnp.concatenate(
        [jnp.concatenate(gain_rows, 1), jnp.concatenate(bias_rows, 1)], 0
    )
    row_pair = iota((8, LANES), 0) // 2
    part = iota((8, GATE), 1) // LANES
    smaller = jnp.where(part == 1, 1.0, 0.5)
    gain = jnp.concatenate([row for row in gain_rows for _ in range(2)], 0) * smaller
    bias = jnp.concatenate([row for row in bias_rows for _ in range(2)], 0)
    bias = (bias - jnp.where(part == 2, 1.0, 0.0)) * smaller
    start = jnp.concatenate(
        [start_ref[:, lanes_of(pair)].astype(f32) for pair in range(PAIRS)], 0
    )
    scale = 1.0 / (PAIRS * GATE)

    def advance(step, state, first=False):
        wide = jnp.concatenate([jnp.where(row_pair == j, state, 0.0) for j in range(PAIRS)], 1)
        values = mm(wide.astype(bf16), state_ref[...])
        parts = [values[:, lanes_of(p)] for p in range(3)]
        for p in range(3):
            at = p * PAIRS * frames + step
            if not first:
                parts[p] = parts[p] + inputs_ref[pl.ds(at - 1, 8, stride=length), :]
            gates_ref[pl.ds(at, 8, stride=length), :] = parts[p]
        total = parts[0] + parts[1] + parts[2]
        square = parts[0] * parts[0] + parts[1] * parts[1] + parts[2] * parts[2]
        mean = jnp.sum(group_sum(total), 1, keepdims=True) * scale
        spread = jnp.sum(group_sum(square), 1, keepdims=True) * scale - mean * mean
        factor = lax.rsqrt(jnp.maximum(spread, 0.0) + epsilon)
        units = [
            (parts[p] - mean) * (factor * gain[:, lanes_of(p)]) + bias[:, lanes_of(p)]
            for p in range(3)
        ]
        reset = 0.5 * jnp.tanh(units[0]) + 0.5
        update = 0.5 * jnp.tanh(units[2]) + 0.5
        renewed = state + update * (jnp.tanh(reset * units[1]) - state)
        states_ref[pl.ds(step, 8, stride=length), :] = renewed
        return renewed

    for ref in (taken_ref, pre_ref, ordered_ref, state_ref, cell_ref):
        ref.flush()
    state = advance(0, start, True)
    ready(later_cat_ref, embed_ref, camera_scale_ref, post_embed_ref)
    steps, _, count = later_cat_ref.shape
    chunks = steps // 2
    share = 7
    features = embed_ref.shape[1] // (chunks + 1)

    def scale_block(chunk):
        columns = pl.ds(pl.multiple_of(chunk * features, features), features)
        for s in range(2):
            rows = slice(s * length, (s + 1) * length)
            factor = scale_row(camera_ref, camera_scale_ref, s, columns)
            scaled_ref[rows, columns] = (embed_ref[rows, columns].astype(f32) * factor).astype(
                bf16
            )

    def embed_block(chunk, side):
        block = features // 2
        columns = pl.ds(pl.multiple_of(chunk * features + side * block, block), block)
        return mm(scaled_ref[:, columns], post_embed_ref[columns, :])

    scale_block(chunks)
    embed_part_ref[...] = embed_block(chunks, 0) + embed_block(chunks, 1)

    def several(chunk, state):
        rows = pl.ds(pl.multiple_of(chunk * 2 * count, 2 * count), 2 * count)
        hot = hot_rows([later_cat_ref[2 * chunk], later_cat_ref[2 * chunk + 1]])
        later_pre = None
        block = hot.shape[1] // 4
        for step in range(share):
            state = advance(1 + chunk * share + step, state)
            if step < 4:
                columns = slice(step * block, (step + 1) * block)
                part = mm(hot[:, columns], table_ref[columns, :])
                later_pre = part if later_pre is None else later_pre + part
            if step == 3:
                scale_block(chunk)
            if step >= 5:
                embed_part_ref[...] += embed_block(chunk, step - 5)
            if step == 4:
                later_pre_ref[rows, :] = later_pre
                later = norm_silu(later_pre, stoch_gain_ref[...], stoch_bias_ref[...])
                later_ref[rows, :] = later.astype(bf16)
        return state

    state = lax.fori_loop(0, chunks, several, state)
    for ref in (later_ref, later_pre_ref, scaled_ref, embed_part_ref):
        ref.flush()
    lax.fori_loop(1 + chunks * share, length, advance, state, unroll=7)
    gates_ref.flush()
    states_ref.flush()
    for pair in range(PAIRS):
        held_ref[:, lanes_of(pair)] = states_ref[pair * frames : (pair + 1) * frames, :].astype(
            bf16
        )
    chosen = pick_columns(order_ref[:, : sent_ref.shape[0]], frames)
    held_ref.flush()
    sent_ref[:, :width] = mm_tn(chosen, held_ref[...]).astype(bf16)
    sent_ref[:, width:] = mm_tn(chosen, taken).astype(bf16)


def mixed_probs(logits):
    shifted = jnp.exp(logits - jnp.max(logits, 1, keepdims=True))
    probability = shifted / jnp.sum(shifted, 1, keepdims=True)
    return probability, (1.0 - unimix) * probability + unimix / CLASSES


def softmax_back(probability, grad):
    grad = (1.0 - unimix) * grad
    return probability * (grad - jnp.sum(probability * grad, 1, keepdims=True))


def heads_kernel(
    core_ref,
    held_ref,
    prior_hidden_ref,
    prior_gain_ref,
    prior_bias_ref,
    prior_out_ref,
    prior_shift_ref,
    post_deter_ref,
    embed_part_ref,
    post_gain_ref,
    post_bias_ref,
    post_out_ref,
    post_shift_ref,
    scaled_ref,
    post_low_ref,
    prior_low_ref,
    small_ref,
    keep_ref,
    send_ref,
    post_act_ref,
    prior_act_ref,
):
    frames, width = held_ref.shape
    features = scaled_ref.shape[1]
    held = held_ref[...]
    split = (GROUPS, CLASSES, frames)
    prior_pre = mm(held, prior_hidden_ref[...])
    prior_act = norm_silu(prior_pre, prior_gain_ref[...], prior_bias_ref[...]).astype(bf16)
    prior_logits = mm(prior_act, prior_out_ref[...]) + prior_shift_ref[...]
    prior_prob, prior_mix = mixed_probs(prior_logits.T.reshape(split))
    post_pre = mm(held, post_deter_ref[...]) + embed_part_ref[...]
    post_act = norm_silu(post_pre, post_gain_ref[...], post_bias_ref[...]).astype(bf16)
    post_logits = mm(post_act, post_out_ref[...]) + post_shift_ref[...]
    post_prob, post_mix = mixed_probs(post_logits.T.reshape(split))
    ratio = jnp.log(post_mix) - jnp.log(prior_mix)
    divergence = jnp.sum(jnp.sum(post_mix * ratio, 0, keepdims=True), 1, keepdims=True)
    slope = sigmoid(divergence - free_bits)
    post_log = softmax_back(post_prob, slope * (ratio + 1.0))
    prior_log = softmax_back(prior_prob, -slope * (post_mix / prior_mix))
    post_log = post_log.reshape(GROUPS * CLASSES, frames).T.astype(bf16)
    prior_log = prior_log.reshape(GROUPS * CLASSES, frames).T.astype(bf16)
    post_low, post_gain_grad, post_bias_grad = norm_silu_back(
        post_pre, post_gain_ref[...], post_bias_ref[...], mm_nt(post_log, post_out_ref[...])
    )
    prior_low, prior_gain_grad, prior_bias_grad = norm_silu_back(
        prior_pre, prior_gain_ref[...], prior_bias_ref[...], mm_nt(prior_log, prior_out_ref[...])
    )
    post_low, prior_low = post_low.astype(bf16), prior_low.astype(bf16)
    post_low_ref[...] = post_low
    prior_low_ref[...] = prior_low
    post_low_ref.flush()
    prior_low_ref.flush()
    small_ref[...] = jnp.concatenate(
        [
            post_gain_grad,
            post_bias_grad,
            prior_gain_grad,
            prior_bias_grad,
            jnp.sum(post_log.astype(f32), 0, keepdims=True),
            jnp.sum(prior_log.astype(f32), 0, keepdims=True),
        ],
        1,
    )
    post_act_ref[...] = post_act
    prior_act_ref[...] = prior_act
    products = (
        (held_ref, post_low),
        (held_ref, prior_low),
        (post_act_ref, post_log[:, :width]),
        (post_act_ref, post_log[:, width:]),
        (prior_act_ref, prior_log[:, :width]),
        (prior_act_ref, prior_log[:, width:]),
    )
    shares = keep_ref.shape[0] // 2
    unit_rows, embed_rows = width // shares, features // shares
    small, large = unit_rows // 4, embed_rows // 4
    for slot, ref in ((1, send_ref), (0, keep_ref)):
        parity = core_ref[0] ^ slot
        for y in range(shares // 2):
            share = 2 * y + parity
            places = [block_place(parity, y, block) for block in range(4)]
            at = pl.multiple_of(share * unit_rows, unit_rows)
            for index, (left, right) in enumerate(products):
                grad = mm_tn(left[:, pl.ds(at, unit_rows)], right).astype(bf16)
                first = large + index * small
                for block in range(4):
                    ref[places[block], first : first + small, :] = grad[
                        block * small : (block + 1) * small
                    ]
            for block in range(4):
                at = pl.multiple_of(share * embed_rows + block * large, large)
                grad = mm_tn(scaled_ref[:, pl.ds(at, large)], post_low)
                ref[places[block], :large, :] = grad.astype(bf16)
                ref.flush(places[block])


def other_place(parity, y, block):
    low_bit, next_bit = block // 2, block % 2
    return jnp.where(
        parity == 0, 4 * low_bit + 2 * y + next_bit, 4 * y + 2 * low_bit + next_bit
    )


def block_place(parity, y, block):
    low_bit, next_bit = block // 2, block % 2
    return jnp.where(
        parity == 0, 4 * y + 2 * low_bit + next_bit, 4 * next_bit + 2 * y + low_bit
    )


def embed_back_kernel(
    camera_ref,
    embed_ref,
    camera_scale_ref,
    post_low_ref,
    prior_low_ref,
    post_embed_ref,
    post_deter_ref,
    prior_hidden_ref,
    held_grad_ref,
    embed_grad_ref,
    camera_grad_ref,
):
    frames, features = embed_ref.shape
    length = frames // 2
    cameras = camera_scale_ref.shape[0]
    held_grad_ref[...] = mm_nt(post_low_ref[...], post_deter_ref[...]) + mm_nt(
        prior_low_ref[...], prior_hidden_ref[...]
    )
    wide = features // 4
    for q in range(4):
        columns = slice(q * wide, (q + 1) * wide)
        scaled_grad = mm_nt(post_low_ref[...], post_embed_ref[columns, :])
        terms = [jnp.zeros((1, wide), f32) for _ in range(cameras)]
        for s in range(2):
            rows = slice(s * length, (s + 1) * length)
            part = scaled_grad[rows]
            scale = scale_row(camera_ref, camera_scale_ref, s, columns)
            embed_grad_ref[rows, columns] = part * scale
            term = jnp.sum(part * embed_ref[rows, columns].astype(f32), 0, keepdims=True)
            for c in range(cameras):
                terms[c] = terms[c] + jnp.where(camera_ref[s] == c, term, 0.0)
        camera_grad_ref[:, columns] = jnp.concatenate(terms, 0)


def cell_gates(units, cell_ref, pair):
    scaled = units * cell_ref[:1, gates_of(pair)] + cell_ref[1:, gates_of(pair)]
    reset = sigmoid(scaled[:, :LANES])
    middle = scaled[:, LANES : 2 * LANES]
    return reset, middle, jnp.tanh(reset * middle), sigmoid(scaled[:, 2 * LANES :] - 1.0)


def rollout_kernel(
    got_ref,
    inputs_ref,
    ordered_ref,
    state_ref,
    cell_ref,
    cot_ref,
    states_ref,
    back_ref,
    gate_grad_ref,
    cell_grad_ref,
    state_grad_ref,
    held_ref,
    unit_ref,
    scale_ref,
    part_ref,
    gain_grad_ref,
    bias_grad_ref,
    turned_ref,
):
    horizon, count, width = states_ref.shape
    unit_ref[:count, :] = mm(got_ref[:, width:], ordered_ref[...])
    chunk = (horizon - 1) * count // 2
    for at in range(0, (horizon - 1) * count, chunk):
        rows = slice(count + at, count + at + chunk)
        unit_ref[rows, :] = mm(inputs_ref[at : at + chunk, :], ordered_ref[...])
    norm = 1.0 / (PAIRS * GATE)

    def advance(step, state):
        rows = pl.ds(pl.multiple_of(step * count, count), count)
        held = state.astype(bf16)
        held_ref[rows, :] = held
        values = []
        total = jnp.zeros((count, LANES), f32)
        square = jnp.zeros((count, LANES), f32)
        for pair in range(PAIRS):
            value = unit_ref[rows, gates_of(pair)] + mm(
                held[:, lanes_of(pair)], state_ref[lanes_of(pair), :]
            )
            values.append(value)
            for p in range(3):
                piece = value[:, lanes_of(p)]
                total = total + piece
                square = square + piece * piece
        mean = jnp.sum(total, 1, keepdims=True) * norm
        spread = jnp.sum(square, 1, keepdims=True) * norm - mean * mean
        factor = lax.rsqrt(jnp.maximum(spread, 0.0) + epsilon)
        scale_ref[rows, :] = jnp.broadcast_to(factor, (count, LANES))
        fresh = []
        for pair in range(PAIRS):
            units = (values[pair] - mean) * factor
            unit_ref[rows, gates_of(pair)] = units
            _, _, candidate, update = cell_gates(units, cell_ref, pair)
            old = state[:, lanes_of(pair)]
            fresh.append(old + update * (candidate - old))
        renewed = jnp.concatenate(fresh, 1)
        states_ref[step] = renewed
        return renewed

    ready(state_ref, cell_ref)
    first = got_ref[:, :width].astype(f32)
    lax.fori_loop(0, horizon, advance, first, unroll=5)
    states_ref.flush()
    turned_ref[...] = state_ref[...].astype(f32).T.astype(bf16)
    ready(cot_ref)
    gain_grad_ref[...] = jnp.zeros_like(gain_grad_ref)
    bias_grad_ref[...] = jnp.zeros_like(bias_grad_ref)

    def retreat(index, carry):
        step = horizon - 1 - index
        rows = pl.ds(pl.multiple_of(step * count, count), count)
        before = states_ref[jnp.maximum(step - 1, 0)]
        before = jnp.where(step == 0, first, before)
        grads = cot_ref[step].astype(f32) + carry
        low = jnp.zeros((count, LANES), f32)
        high = jnp.zeros((count, LANES), f32)
        kept = []
        for pair in range(PAIRS):
            units = unit_ref[rows, gates_of(pair)]
            reset, middle, candidate, update = cell_gates(units, cell_ref, pair)
            grad = grads[:, lanes_of(pair)]
            rest = 1.0 - update
            inner = grad * update * (1.0 - candidate * candidate)
            parts = jnp.concatenate(
                [
                    inner * middle * (reset * (1.0 - reset)),
                    inner * reset,
                    grad * (candidate - before[:, lanes_of(pair)]) * (update * rest),
                ],
                1,
            )
            weighted = parts * units
            gain_grad_ref[:, gates_of(pair)] += jnp.sum(weighted.reshape(count // 8, 8, GATE), 0)
            bias_grad_ref[:, gates_of(pair)] += jnp.sum(parts.reshape(count // 8, 8, GATE), 0)
            parts = parts * cell_ref[:1, gates_of(pair)]
            weighted = parts * units
            for p in range(3):
                low = low + parts[:, lanes_of(p)]
                high = high + weighted[:, lanes_of(p)]
            part_ref[:, gates_of(pair)] = parts
            kept.append(grad * rest)
        low = jnp.sum(low, 1, keepdims=True) * norm
        high = jnp.sum(high, 1, keepdims=True) * norm
        factor = scale_ref[rows, :][:, :1]
        carried = []
        for pair in range(PAIRS):
            units = unit_ref[rows, gates_of(pair)]
            grad = (factor * (part_ref[:, gates_of(pair)] - low - units * high)).astype(bf16)
            gate_grad_ref[rows, gates_of(pair)] = grad
            carried.append(kept[pair] + mm(grad, turned_ref[:, lanes_of(pair)]))
        return jnp.concatenate(carried, 1)

    carry = lax.fori_loop(0, horizon, retreat, jnp.zeros((count, width), f32), unroll=5)
    back_ref[:, :width] = carry.astype(bf16)
    back_ref[:, width:] = mm_nt(gate_grad_ref[:count, :], ordered_ref[...]).astype(bf16)
    back_ref.flush()
    gate_grad_ref.flush()
    for pair in range(PAIRS):
        state_grad_ref[pair] = mm_tn(held_ref[:, lanes_of(pair)], gate_grad_ref[:, gates_of(pair)])
    cell_grad_ref[...] = jnp.concatenate(
        [
            jnp.sum(gain_grad_ref[...], 0, keepdims=True),
            jnp.sum(bias_grad_ref[...], 0, keepdims=True),
        ],
        0,
    )


def rollout_grads_kernel(
    gate_grad_ref,
    got_ref,
    inputs_ref,
    pre_ref,
    cat_ref,
    ordered_ref,
    stoch_gain_ref,
    stoch_bias_ref,
    input_grad_ref,
    table_grad_ref,
    stoch_grad_ref,
    hot_ref,
    low_ref,
    taken_ref,
):
    steps, _, count = cat_ref.shape
    width = inputs_ref.shape[1]
    taken_ref[:count, :] = got_ref[:, width:]
    taken_ref[count:, :] = inputs_ref[...]
    input_grad_ref[...] = mm_tn(taken_ref[...], gate_grad_ref[...])
    input_grad_ref.flush()
    gain_sum = jnp.zeros(stoch_gain_ref.shape, f32)
    bias_sum = jnp.zeros(stoch_bias_ref.shape, f32)
    grads = mm_nt(gate_grad_ref[count:, :], ordered_ref[...])
    for at in range(0, steps, 2):
        rows = slice(at * count, (at + 2) * count)
        low, gain_grad, bias_grad = norm_silu_back(
            pre_ref[rows, :], stoch_gain_ref[...], stoch_bias_ref[...], grads[rows]
        )
        gain_sum = gain_sum + gain_grad
        bias_sum = bias_sum + bias_grad
        low_ref[rows, :] = low.astype(bf16)
        hot_ref[:, rows] = hot_columns([cat_ref[at], cat_ref[at + 1]])
    table_grad_ref[...] = mm(hot_ref[...], low_ref[...])
    stoch_grad_ref[...] = jnp.concatenate([gain_sum, bias_sum], 1)


def observe_back_kernel(
    core_ref,
    held_grad_ref,
    back_ref,
    order_ref,
    cat_ref,
    taken_ref,
    pre_ref,
    gates_ref,
    states_ref,
    start_ref,
    stoch_gain_ref,
    stoch_bias_ref,
    ordered_ref,
    state_ref,
    cell_ref,
    input_part_ref,
    state_part_ref,
    table_part_ref,
    stoch_part_ref,
    cell_part_ref,
    small_ref,
    camera_grad_ref,
    start_grad_ref,
    keep_ref,
    send_ref,
    keep_more_ref,
    send_more_ref,
    grads_ref,
    turned_ref,
    arriving_ref,
    slope_ref,
    factor_ref,
    unit_ref,
    mean_ref,
    cross_ref,
    rest_ref,
    flat_ref,
    lean_ref,
    scale_ref,
    grad_ref,
    low_ref,
    high_ref,
    previous_ref,
):
    frames, width = held_grad_ref.shape
    length = frames // 2
    norm = 1.0 / (PAIRS * GATE)
    chosen = pick_columns(order_ref[:, : back_ref.shape[0]], frames)
    held_grad = held_grad_ref[...] + mm(chosen, back_ref[:, :width])
    turned_ref[...] = state_ref[...].astype(f32).T.astype(bf16)
    start = jnp.concatenate(
        [start_ref[:, lanes_of(pair)].astype(f32) for pair in range(PAIRS)], 0
    )
    for pair in range(PAIRS):
        arriving_ref[pair * frames : (pair + 1) * frames, :] = held_grad[:, lanes_of(pair)]
    long = PAIRS * frames
    for s in range(2):
        blocks = [
            slice((2 * pair + s) * length, (2 * pair + s + 1) * length) for pair in range(PAIRS)
        ]
        total = jnp.zeros((length, LANES), f32)
        for rows in blocks:
            for p in range(3):
                total = total + gates_ref[p * long + rows.start : p * long + rows.stop, :]
        mean = jnp.sum(total, 1, keepdims=True) * norm
        square = jnp.zeros((length, LANES), f32)
        for rows in blocks:
            for p in range(3):
                center = gates_ref[p * long + rows.start : p * long + rows.stop, :] - mean
                square = square + center * center
        scale = lax.rsqrt(jnp.sum(square, 1, keepdims=True) * norm + epsilon)
        for pair, rows in enumerate(blocks):
            gain = cell_ref[:1, gates_of(pair)]
            units = jnp.concatenate(
                [gates_ref[p * long + rows.start : p * long + rows.stop, :] for p in range(3)], 1
            )
            units = (units - mean) * scale
            reset, middle, candidate, update = cell_gates(units, cell_ref, pair)
            row = 2 * pair + s
            previous = jnp.where(
                iota((length, LANES), 0) == 0,
                start[row : row + 1, :],
                pltpu.roll(states_ref[rows, :], 1, 0),
            )
            previous_ref[rows, :] = previous
            inner = update * (1.0 - candidate * candidate)
            slope = jnp.concatenate(
                [
                    inner * middle * (reset * (1.0 - reset)),
                    inner * reset,
                    (candidate - previous) * (update * (1.0 - update)),
                ],
                1,
            )
            slope_ref[rows, :] = slope
            slope = slope * gain
            weighted = slope * units
            mean_ref[rows, :] = norm * (
                slope[:, :LANES] + slope[:, LANES : 2 * LANES] + slope[:, 2 * LANES :]
            )
            cross_ref[rows, :] = norm * (
                weighted[:, :LANES] + weighted[:, LANES : 2 * LANES] + weighted[:, 2 * LANES :]
            )
            for p in range(3):
                factor_ref[p * long + rows.start : p * long + rows.stop, :] = (
                    scale * slope[:, lanes_of(p)]
                )
            unit_ref[rows, :] = scale * units
            rest_ref[rows, :] = 1.0 - update
            scale_ref[rows, :] = jnp.broadcast_to(scale, (length, LANES))
            weight = state_ref[lanes_of(pair), :]
            flat_ref[rows, :] = scale * mm_nt(jnp.ones((8, GATE), bf16), weight)[:1, :]
            lean_ref[rows, :] = mm_nt((scale * units).astype(bf16), weight)
    row_pair = iota((8, LANES), 0) // 2

    def retreat(index, carry):
        step = length - 1 - index
        rows = pl.ds(step, 8, stride=length)
        grad = arriving_ref[rows, :] + carry
        wide = jnp.concatenate(
            [grad * factor_ref[pl.ds(p * long + step, 8, stride=length), :] for p in range(3)], 1
        )
        turned = mm(wide.astype(bf16), turned_ref[...])
        low = jnp.sum(group_sum(grad * mean_ref[rows, :]), 1, keepdims=True)
        high = jnp.sum(group_sum(grad * cross_ref[rows, :]), 1, keepdims=True)
        grad_ref[rows, :] = grad
        low_ref[rows, :] = jnp.broadcast_to(low, (8, LANES))
        high_ref[rows, :] = jnp.broadcast_to(high, (8, LANES))
        kept = grad * rest_ref[rows, :] - low * flat_ref[rows, :] - high * lean_ref[rows, :]
        for pair in range(PAIRS):
            kept = kept + jnp.where(row_pair == pair, turned[:, lanes_of(pair)], 0.0)
        return kept

    carry = lax.fori_loop(0, length, retreat, jnp.zeros((8, LANES), f32), unroll=8)
    for pair in range(PAIRS):
        start_grad_ref[:, lanes_of(pair)] = carry[2 * pair : 2 * pair + 2, :]
    frame = iota((frames, width), 0) % length
    earlier = jnp.where(frame == 0, 0.0, pltpu.roll(taken_ref[...].astype(f32), 1, 0)).astype(bf16)
    input_grad = jnp.zeros((frames, width), f32)
    gains, biases, inputs = [], [], []
    shares = grads_ref.shape[0]
    unit_rows = width // shares
    for pair in range(PAIRS):
        rows = slice(pair * frames, (pair + 1) * frames)
        grad = jnp.concatenate([grad_ref[rows, :]] * 3, 1)
        gate_grad = grad * slope_ref[rows, :]
        biases.append(jnp.sum(gate_grad, 0, keepdims=True))
        scale = scale_ref[rows, :][:, :1]
        units = unit_ref[rows, :]
        gains.append(jnp.sum(gate_grad * (units / scale), 0, keepdims=True))
        low = low_ref[rows, :][:, :1]
        high = high_ref[rows, :][:, :1]
        factors = jnp.concatenate(
            [factor_ref[p * long + rows.start : p * long + rows.stop, :] for p in range(3)], 1
        )
        gate_low = (grad * factors - low * scale - high * units).astype(bf16)
        columns = ordered_ref[:, gates_of(pair)]
        input_grad = input_grad + mm_nt(gate_low, columns)
        weight_grad = mm_tn(earlier, gate_low) + input_part_ref[:, gates_of(pair)]
        inputs.append(weight_grad.astype(bf16))
        state_grad = mm_tn(previous_ref[rows, :].astype(bf16), gate_low) + state_part_ref[pair]
        half = LANES // 2
        upper = iota((half, GATE), 1) % LANES < half
        folded = jnp.where(upper, state_grad[:half], state_grad[half:])
        at = 3 * unit_rows + 2 * unit_rows
        grads_ref[pair, at : at + half, :GATE] = folded.astype(bf16)
    weights = jnp.concatenate(inputs, 1)
    for q in range(shares):
        for c in range(3):
            grads_ref[q, c * unit_rows : (c + 1) * unit_rows, :] = weights[
                q * unit_rows : (q + 1) * unit_rows, c * width : (c + 1) * width
            ]
    taken_grad = jnp.where(
        frame == length - 1, 0.0, pltpu.roll(input_grad, frames - 1, 0)
    ) + mm(chosen, back_ref[:, width:])
    low, gain_grad, bias_grad = norm_silu_back(
        pre_ref[...], stoch_gain_ref[...], stoch_bias_ref[...], taken_grad
    )
    stoch = jnp.concatenate([gain_grad, bias_grad], 1) + stoch_part_ref[...]
    hot = hot_columns([cat_ref[s] for s in range(2)])
    table_grad = mm(hot, low.astype(bf16)) + table_part_ref[...]
    rows = table_grad.shape[0] // shares
    vector_row = 5 * unit_rows
    classes = GROUPS * CLASSES
    wide = camera_grad_ref.shape[1] // shares
    for q in range(shares):
        grads_ref[q, 3 * unit_rows : 3 * unit_rows + rows, :] = table_grad[
            q * rows : (q + 1) * rows
        ].astype(bf16)
        unit = slice(q * unit_rows, (q + 1) * unit_rows)
        logit = slice(q * classes // shares, (q + 1) * classes // shares)
        units = [stoch[:, unit], stoch[:, width + unit.start : width + unit.stop]]
        units += [
            small_ref[:, k * width + unit.start : k * width + unit.stop] for k in range(4)
        ]
        logits = [
            small_ref[
                :, 4 * width + k * classes + logit.start : 4 * width + k * classes + logit.stop
            ]
            for k in range(2)
        ]
        cells = [
            plain_row(kind[q] + cell_part_ref[k : k + 1, gates_of(q)])
            for k, kind in enumerate((gains, biases))
        ]
        cameras = [
            camera_grad_ref[c : c + 1, q * wide : (q + 1) * wide]
            for c in range(camera_grad_ref.shape[0])
        ]
        lines = []
        for vector in units + logits + cells + cameras:
            lines += [vector[:, at : at + LANES] for at in range(0, vector.shape[1], LANES)]
        lines.append(jnp.zeros((LANES // 2 - len(lines), LANES), f32))
        grads_ref[q, vector_row:, GATE:] = jnp.concatenate(lines, 0).astype(bf16)
    block, more = keep_ref.shape[1], keep_more_ref.shape[1]
    for slot, ref, more_ref in ((1, send_ref, send_more_ref), (0, keep_ref, keep_more_ref)):
        parity = core_ref[0] ^ slot
        for y in range(shares // 2):
            for index in range(4):
                at = index * (block + more)
                place = block_place(parity, y, index)
                ref[place] = grads_ref[2 * y + parity, at : at + block, :]
                place = other_place(parity, y, index)
                more_ref[place] = grads_ref[2 * y + parity, at + block : at + block + more, :]


def place_blocks(where_ref, own_ref, got_ref, full_ref, at=0):
    block, whole = own_ref.shape[0] // 2, full_ref.shape[0] // 4
    parity, bit = where_ref[0], where_ref[1]
    for side in range(2):
        for inner in range(2):
            rows = slice(inner * block, (inner + 1) * block)
            piece = jnp.where(bit == side, own_ref[rows, :], got_ref[rows, :]).astype(f32)
            place = jnp.where(parity == 0, 2 * side + inner, 2 * inner + side)
            full_ref[pl.ds(pl.multiple_of(place * whole + at, 16), block), :] = piece


def finish_heads_kernel(
    where_ref,
    own_ref,
    got_ref,
    post_embed_ref,
    post_deter_ref,
    prior_hidden_ref,
    post_out_ref,
    prior_out_ref,
    full_ref,
):
    place_blocks(where_ref, own_ref, got_ref, full_ref)
    block = full_ref.shape[0] // 4
    width = own_ref.shape[1]
    large, small = post_embed_ref.shape[0] // 4, post_deter_ref.shape[0] // 4
    for index in range(4):
        at = index * block
        post_embed_ref[index * large : (index + 1) * large, :] = full_ref[at : at + large, :]
        rows = slice(index * small, (index + 1) * small)
        for member, (ref, column) in enumerate(
            (
                (post_deter_ref, 0),
                (prior_hidden_ref, 0),
                (post_out_ref, 0),
                (post_out_ref, width),
                (prior_out_ref, 0),
                (prior_out_ref, width),
            )
        ):
            first = at + large + member * small
            ref[rows, column : column + width] = full_ref[first : first + small, :]


def finish_kernel(
    where_ref, flat_where_ref, own_ref, got_ref, own_more_ref, got_more_ref, *refs
):
    outs, full_ref = refs[:-1], refs[-1]
    width = own_ref.shape[1]
    place_blocks(where_ref, own_ref, got_ref, full_ref)
    place_blocks(flat_where_ref, own_more_ref, got_more_ref, full_ref, own_ref.shape[0] // 2)
    input_ref, table_ref, state_ref = outs[:3]
    unit_rows = input_ref.shape[0]
    for pair in range(PAIRS):
        parts = []
        for p in range(3):
            at = pair * GATE + p * LANES
            line, column = at // width * unit_rows, at % width
            parts.append(full_ref[line : line + unit_rows, column : column + LANES])
        input_ref[:, gates_of(pair)] = plain_row(jnp.concatenate(parts, 1))
    at = 3 * unit_rows
    table_ref[...] = full_ref[at : at + table_ref.shape[0], :]
    at += table_ref.shape[0]
    half = state_ref.shape[1]
    folded = full_ref[at : at + half, :]
    for e in range(2):
        state_ref[e] = jnp.concatenate(
            [folded[:, (2 * p + e) * half : (2 * p + e + 1) * half] for p in range(3)], 1
        )
    for ref in outs[3:14]:
        for line in range(ref.shape[0]):
            for column in range(0, ref.shape[1], LANES):
                ref[line : line + 1, column : column + LANES] = full_ref[at : at + 1, GATE:]
                at += 1


def struct(shape, dtype):
    return jax.ShapeDtypeStruct(shape, dtype)


class Incoming:
    def __init__(self, ref, copy):
        self.ref, self.copy, self.shape = ref, copy, ref.shape
        copy.start()

    def ready(self):
        if self.copy is not None:
            self.copy.wait()
            self.copy = None

    def __getitem__(self, index):
        self.ready()
        return self.ref[index]


class Near:
    def __init__(self, ref):
        self.ref, self.shape = ref, ref.shape

    def __getitem__(self, index):
        return self.ref[index]

    def __setitem__(self, index, value):
        self.ref[index] = value

    def flush(self):
        pass


class Outgoing:
    def __init__(self, ref, target, marks):
        self.ref, self.target, self.marks = ref, target, marks
        self.shape, self.copies = ref.shape, []

    def __getitem__(self, index):
        return self.ref[index]

    def __setitem__(self, index, value):
        self.ref[index] = value

    def flush(self, part=None):
        source, target = self.ref, self.target
        if part is not None:
            source, target = source.at[part], target.at[part]
        elif self.copies:
            return
        copy = pltpu.make_async_copy(source, target, self.marks[len(self.copies)])
        copy.start()
        self.copies.append(copy)

    def finish(self):
        self.flush()
        for copy in self.copies:
            copy.wait()


def ready(*refs):
    for ref in refs:
        if isinstance(ref, Incoming):
            ref.ready()


def call(
    kernel,
    name,
    outs,
    ins,
    mib,
    scratch=(),
    scalars=0,
    after=(),
    near_in=(),
    near_out=(),
    parts=(),
):
    count, total = len(ins), len(ins) + len(after) + len(outs)
    far_in = [k for k in range(scalars, count) if k not in near_in]
    far_out = [k for k in range(len(outs)) if k not in near_out]
    pieces = {k: outs[k].shape[0] if k in parts else 1 for k in far_out}
    near = pl.BlockSpec(memory_space=pltpu.VMEM)
    far = pl.BlockSpec(memory_space=pltpu.HBM)

    def body(*refs):
        given, made = list(refs[:count]), list(refs[count + len(after) : total])
        places = refs[total : total + len(far_in) + len(far_out)]
        rest = refs[total + len(far_in) + len(far_out) : -1]
        marks = refs[-1]
        for at, k in enumerate(far_in):
            copy = pltpu.make_async_copy(given[k], places[at], marks.at[at])
            given[k] = Incoming(places[at], copy)
        at = len(far_in)
        for place, k in zip(places[at:], far_out, strict=True):
            own = [marks.at[at + part] for part in range(pieces[k])]
            made[k] = Outgoing(place, made[k], own)
            at += pieces[k]
        for k in near_out:
            made[k] = Near(made[k])
        kernel(*given, *made, *rest)
        ready(*given)
        for k in far_out:
            made[k].flush()
        for k in far_out:
            made[k].finish()

    return pl.pallas_call(
        body,
        out_shape=tuple(
            pltpu.HBM(out.shape, out.dtype) if k in far_out else out for k, out in enumerate(outs)
        ),
        in_specs=[pl.BlockSpec(memory_space=pltpu.SMEM)] * scalars
        + [far if k in far_in else near for k in range(scalars, count)]
        + [far] * len(after),
        out_specs=tuple(far if k in far_out else near for k in range(len(outs))),
        scratch_shapes=[pltpu.VMEM(ins[k].shape, ins[k].dtype) for k in far_in]
        + [pltpu.VMEM(outs[k].shape, outs[k].dtype) for k in far_out]
        + list(scratch)
        + [pltpu.SemaphoreType.DMA((len(far_in) + sum(pieces.values()),))],
        compiler_params=pltpu.CompilerParams(vmem_limit_bytes=mib * 1024 * 1024),
        name=name,
    )(
        *[
            pltpu.with_memory_space_constraint(member, pltpu.HBM) if k in far_in else member
            for k, member in enumerate(ins)
        ],
        *[pltpu.with_memory_space_constraint(member, pltpu.HBM) for member in after],
    )


def linear_bits(bits):
    own = bits[0]
    rep_count = lax.axis_size("rep")
    index = lax.axis_index("seq") * rep_count + lax.axis_index("rep")
    if bits[0] != bits[1]:
        own = jnp.where(index & 1 == 0, bits[0], bits[1])
    return (index >> own) & 1


def swap(values, bits):
    count = lax.axis_size("seq") * lax.axis_size("rep")
    return lax.ppermute(
        values, ("seq", "rep"), [(i, i ^ (1 << bits[i & 1])) for i in range(count)]
    )


class Terms:
    def __init__(self, member):
        self.members = [(member, [])]

    def add(self, member):
        self.members.append((member, []))

    def part(self, *sides):
        total = 0.0
        for member, path in self.members:
            path = path + list(sides)
            rows = member.shape[0] >> len(path)
            split = member.reshape((2,) * len(path) + (rows, member.shape[1]))
            one = (1,) * len(path) + split.shape[-2:]
            chosen = lax.dynamic_slice(split, path + [0, 0], one)
            total = total + chosen.reshape(split.shape[-2:]).astype(f32)
        return total.astype(bf16)

    def fold(self, arrived, bits):
        self.add(arrived)
        own = linear_bits(bits).astype(jnp.int32)
        send = self.part(1 - own)
        self.members = [(member, path + [own]) for member, path in self.members]
        return send


def added(left, right):
    return (left.astype(f32) + right.astype(f32)).astype(bf16)


def joined(values, got, bits):
    own = linear_bits(bits)
    return jnp.where(
        own == 0, jnp.concatenate([values, got], 0), jnp.concatenate([got, values], 0)
    )


class Chain:
    def __init__(self, keep, send, stages, last):
        self.terms, self.piece = Terms(keep), None
        self.folds, self.middle = list(stages[:-1]), stages[-1]
        self.joins = list(reversed(stages[2:-1])) + [last]
        self.begin(send, (0, 0))

    def begin(self, send, bits):
        self.sent, self.last = send, bits
        self.arrived = swap(send, bits)

    def advance(self, *after):
        if after:
            self.arrived = lax.optimization_barrier((self.arrived, *after))[0]
        if self.folds:
            bits = self.folds.pop(0)
            self.begin(self.terms.fold(self.arrived, bits), bits)
            return
        if self.piece is None:
            bits = self.middle
            self.terms.add(self.arrived)
            self.piece = self.terms.part()
        else:
            bits = self.joins.pop(0)
            if self.last == self.middle:
                self.piece = added(self.piece, self.arrived)
            else:
                self.piece = joined(self.piece, self.arrived, self.last)
        self.begin(self.piece, bits)


def on_device(
    start_deter,
    post_cat,
    embed,
    camera,
    start_order,
    imag_cat,
    imag_cot,
    stoch_table,
    stoch_gain,
    stoch_bias,
    state_weight,
    input_weight,
    cell_gain,
    cell_bias,
    prior_hidden,
    prior_gain,
    prior_bias,
    prior_out,
    prior_shift,
    post_deter,
    post_embed,
    post_gain,
    post_bias,
    post_out,
    post_shift,
    camera_scale,
):
    seq_count, length = post_cat.shape[:2]
    frames = seq_count * length
    count, horizon, width = imag_cot.shape
    features = embed.shape[-1]
    shares = lax.axis_size("rep")
    rep_bits = shares.bit_length() - 1
    seq_bits = lax.axis_size("seq").bit_length() - 1
    half = LANES // 2
    gate_count = 3 * width
    classes = GROUPS * CLASSES
    rows = horizon * count
    long = PAIRS * frames
    unit_rows = width // shares
    core = (lax.axis_index("rep") & 1).astype(jnp.int32).reshape(1)
    row = lambda vector: vector.reshape(1, -1)
    cat = jnp.swapaxes(post_cat, 1, 2)
    later_cat = jnp.transpose(imag_cat, (1, 2, 0))
    stoch_rows = (row(stoch_gain), row(stoch_bias))
    embed_rows = embed.reshape(frames, features)

    low_bit, next_bit = rep_bits, rep_bits + 1
    deeper = [rep_bits + bit for bit in range(2, seq_bits)]
    outer = (low_bit, next_bit)
    stages = list(
        zip([1, low_bit, next_bit] + deeper, [next_bit, 1] + deeper + [low_bit], strict=True)
    )

    (
        held,
        taken,
        obs_pre,
        imag_inputs,
        imag_pre,
        obs_gates,
        obs_states,
        sent,
        ordered,
        state,
        cell,
        scaled,
        embed_part,
    ) = call(
        observe_kernel,
        "observe",
        [
            struct((frames, width), bf16),
            struct((frames, width), bf16),
            struct((frames, width), f32),
            struct((rows - count, width), bf16),
            struct((rows - count, width), f32),
            struct((3 * long, LANES), f32),
            struct((long, LANES), f32),
            struct((count, 2 * width), bf16),
            struct((width, gate_count), bf16),
            struct((width, GATE), bf16),
            struct((2, gate_count), f32),
            struct((frames, features), bf16),
            struct((frames, width), f32),
        ],
        (
            camera,
            cat,
            stoch_table,
            *stoch_rows,
            input_weight,
            state_weight.reshape(width, 3 * half),
            cell_gain.reshape(-1, LANES),
            cell_bias.reshape(-1, LANES),
            start_deter,
            start_order,
            later_cat,
            embed_rows,
            camera_scale,
            post_embed,
        ),
        36,
        scratch=[pltpu.VMEM((3 * long, LANES), f32)],
        scalars=1,
    )
    got = lax.all_to_all(sent, "seq", split_axis=0, concat_axis=0, tiled=True)

    square = struct((frames, width), bf16)
    embed_rows_count = features // shares
    head_rows = embed_rows_count + 6 * unit_rows
    blocks = struct((2 * shares, head_rows // 4, width), bf16)
    post_low, prior_low, head_small, keep, send = call(
        heads_kernel,
        "heads",
        [square, square, struct((1, 4 * width + 2 * classes), f32), blocks, blocks],
        (
            core,
            held,
            prior_hidden,
            row(prior_gain),
            row(prior_bias),
            prior_out,
            row(prior_shift),
            post_deter,
            embed_part,
            row(post_gain),
            row(post_bias),
            post_out,
            row(post_shift),
            scaled,
        ),
        34,
        scratch=[pltpu.VMEM((frames, width), bf16), pltpu.VMEM((frames, width), bf16)],
        scalars=1,
        parts=(3, 4),
    )
    flat = (shares * head_rows // 2, width)
    send, got = lax.optimization_barrier((send, got))
    tail_stages = list(
        zip([1, low_bit, next_bit] + deeper, [next_bit, 1, low_bit] + deeper, strict=True)
    )
    more_stages = list(
        zip([low_bit, 1, next_bit] + deeper, [1, low_bit, next_bit] + deeper, strict=True)
    )
    head = Chain(keep.reshape(flat), send.reshape(flat), stages, outer)
    held_grad, embed_grad, camera_grad = call(
        embed_back_kernel,
        "embed_back",
        [
            struct((frames, width), f32),
            struct((frames, features), f32),
            struct(camera_scale.shape, f32),
        ],
        (
            camera,
            embed_rows,
            camera_scale,
            post_low,
            prior_low,
            post_embed,
            post_deter,
            prior_hidden,
        ),
        18,
        scalars=1,
        after=(head.sent,),
    )
    head.advance(camera_grad)

    states, back, gate_grads, cell_part, state_part = call(
        rollout_kernel,
        "rollout",
        [
            struct((horizon, count, width), f32),
            struct((count, 2 * width), bf16),
            struct((rows, gate_count), bf16),
            struct((2, gate_count), f32),
            struct((PAIRS, LANES, GATE), f32),
        ],
        (
            got,
            imag_inputs,
            ordered,
            state,
            cell,
            jnp.swapaxes(imag_cot, 0, 1),
        ),
        36,
        scratch=[
            pltpu.VMEM((rows, width), bf16),
            pltpu.VMEM((rows, gate_count), f32),
            pltpu.VMEM((rows, LANES), f32),
            pltpu.VMEM((count, gate_count), f32),
            pltpu.VMEM((8, gate_count), f32),
            pltpu.VMEM((8, gate_count), f32),
            pltpu.VMEM((GATE, PAIRS * LANES), bf16),
        ],
        after=(head.sent,),
    )
    imag_deter = jnp.swapaxes(states, 0, 1)
    returned = lax.all_to_all(back, "seq", split_axis=0, concat_axis=0, tiled=True)
    head.advance(cell_part)

    input_part, table_part, stoch_part = call(
        rollout_grads_kernel,
        "rollout_grads",
        [
            struct((width, gate_count), f32),
            struct(stoch_table.shape, f32),
            struct((1, 2 * width), f32),
        ],
        (gate_grads, got, imag_inputs, imag_pre, later_cat, ordered, *stoch_rows),
        30,
        scratch=[
            pltpu.VMEM((stoch_table.shape[0], rows - count), bf16),
            pltpu.VMEM((rows - count, width), bf16),
            pltpu.VMEM((rows, width), bf16),
        ],
        after=(head.sent,),
    )
    head.advance(stoch_part, returned)
    tail_rows = 5 * unit_rows + half
    less = tail_rows // 8 // 16 * 16
    blocks = struct((2 * shares, tail_rows // 4 - less, width), bf16)
    more = struct((2 * shares, less, width), bf16)
    start_grad, tail_keep, tail_send, more_keep, more_send = call(
        observe_back_kernel,
        "observe_back",
        [struct((seq_count, width), f32), blocks, blocks, more, more],
        (
            core,
            held_grad,
            returned,
            start_order,
            cat,
            taken,
            obs_pre,
            obs_gates,
            obs_states,
            start_deter,
            *stoch_rows,
            ordered,
            state,
            cell,
            input_part,
            state_part,
            table_part,
            stoch_part,
            cell_part,
            head_small,
            camera_grad,
        ),
        30,
        after=(head.sent,),
        scratch=[
            pltpu.VMEM((shares, tail_rows, width), bf16),
            pltpu.VMEM((GATE, PAIRS * LANES), bf16),
            pltpu.VMEM((long, LANES), f32),
            pltpu.VMEM((long, GATE), f32),
            pltpu.VMEM((3 * long, LANES), f32),
            pltpu.VMEM((long, GATE), f32),
        ]
        + [pltpu.VMEM((long, LANES), f32)] * 10,
        scalars=1,
        near_out=(1, 3),
    )
    tail_send, head.arrived = lax.optimization_barrier((tail_send, head.arrived))
    for _ in deeper:
        head.advance()
    tails = [
        Chain(keep.reshape(-1, width), send.reshape(-1, width), order, last)
        for keep, send, order, last in (
            (tail_keep, tail_send, tail_stages, outer),
            (more_keep, more_send, more_stages, (low_bit, low_bit)),
        )
    ]
    for step in range(2 * len(stages) - 2):
        if step in (1,4):
            head.advance(tails[0].sent)
        for tail in tails:
            tail.advance()
    while head.joins:
        head.advance(tails[0].sent)
    head_piece, head_other = head.piece, head.arrived
    where = jnp.concatenate([core, linear_bits(outer).astype(jnp.int32).reshape(1)])
    flat_where = jnp.stack([0, linear_bits((low_bit, low_bit)).astype(jnp.int32)])
    unit = struct((1, unit_rows), f32)
    logit = struct((1, classes // shares), f32)
    gate = struct((3, LANES), f32)
    small_rows = struct((unit_rows, width), f32)
    wide_rows = struct((unit_rows, classes), f32)
    post_embed_grad, post_deter_grad, prior_hidden_grad, post_out_grad, prior_out_grad = call(
        finish_heads_kernel,
        "finish_heads",
        [
            struct((embed_rows_count, width), f32),
            small_rows,
            small_rows,
            wide_rows,
            wide_rows,
        ],
        (where, head_piece, head_other),
        18,
        scratch=[pltpu.VMEM((head_rows, width), f32)],
        scalars=1,
        near_in=(1, 2),
    )
    finished = call(
        finish_kernel,
        "finish",
        [
            struct((unit_rows, gate_count), f32),
            struct((stoch_table.shape[0] // shares, width), f32),
            struct((2, half, 3 * half), f32),
            *[unit] * 6,
            logit,
            logit,
            gate,
            gate,
            struct((camera_scale.shape[0], features // shares), f32),
        ],
        (where, flat_where, *[member for tail in tails for member in (tail.piece, tail.arrived)]),
        12,
        scratch=[pltpu.VMEM((tail_rows, width), f32)],
        scalars=2,
        near_in=(2, 3, 4, 5),
        after=(post_embed_grad,),
    )
    input_weight_grad, stoch_table_grad, state_weight_grad = finished[:3]
    (
        stoch_gain_grad,
        stoch_bias_grad,
        post_gain_grad,
        post_bias_grad,
        prior_gain_grad,
        prior_bias_grad,
        post_shift_grad,
        prior_shift_grad,
        cell_gain_grad,
        cell_bias_grad,
    ) = [member.reshape(-1) for member in finished[3:13]]
    return (
        imag_deter,
        embed_grad.reshape(embed.shape),
        start_grad,
        stoch_table_grad,
        stoch_gain_grad,
        stoch_bias_grad,
        state_weight_grad,
        input_weight_grad,
        cell_gain_grad,
        cell_bias_grad,
        prior_hidden_grad,
        prior_gain_grad,
        prior_bias_grad,
        prior_out_grad,
        prior_shift_grad,
        post_deter_grad,
        post_embed_grad,
        post_gain_grad,
        post_bias_grad,
        post_out_grad,
        post_shift_grad,
        finished[13],
    )


def solution(mesh):
    both = ("seq", "rep")
    in_specs = (
        P(both, None),
        P(both, None, None),
        P(both, None, None),
        P(both),
        P(both, None),
        P(both, None, None),
        P(both, None, None),
    ) + (P(),) * 19
    rows, flat = P("rep", None), P("rep")
    out_specs = (
        P(both, None, None),
        P(both, None, None),
        P(both, None),
        rows,
        flat,
        flat,
        P("rep", None, None),
        rows,
        flat,
        flat,
        rows,
        flat,
        flat,
        rows,
        flat,
        rows,
        rows,
        flat,
        flat,
        rows,
        flat,
        P(None, "rep"),
    )
    return jax.shard_map(
        on_device, mesh=mesh, in_specs=in_specs, out_specs=out_specs, check_vma=False
    )
```

```python
import jax
import jax.numpy as jnp
from jax import lax
from jax.experimental import pallas as pl
from jax.experimental.pallas import tpu as pltpu
from jax.sharding import PartitionSpec as P

BLOCKS = 8
GROUPS = 32
CLASSES = 32
PAIRS = BLOCKS // 2
LANES = 128
GATE = 3 * LANES

epsilon = 1e-05
unimix = 0.01
free_bits = 1.0

f32 = jnp.float32
bf16 = jnp.bfloat16


def iota(shape, axis):
    return lax.broadcasted_iota(jnp.int32, shape, axis)


def mm(left, right):
    return jnp.dot(left, right, preferred_element_type=f32)


def mm_nt(left, right):
    return lax.dot_general(left, right, (((1,), (1,)), ((), ())), preferred_element_type=f32)


def mm_tn(left, right):
    return lax.dot_general(left, right, (((0,), (0,)), ((), ())), preferred_element_type=f32)


def sigmoid(values):
    return 0.5 * jnp.tanh(0.5 * values) + 0.5


def row_mean(values):
    return jnp.sum(values, -1, keepdims=True) * (1.0 / values.shape[-1])


def hot_rows(columns):
    categories = jnp.concatenate([part.astype(f32).T for part in columns], 0).astype(bf16)
    count = categories.shape[0]
    width = GROUPS * CLASSES
    spread = (iota((GROUPS, width), 1) // CLASSES == iota((GROUPS, width), 0)).astype(f32)
    wide = mm(categories, spread.astype(bf16))
    own = (iota((count, width), 1) % CLASSES).astype(f32)
    return jnp.where(wide == own, 1.0, 0.0).astype(bf16)


def hot_columns(columns):
    categories = jnp.concatenate([part.astype(f32) for part in columns], 1).astype(bf16)
    count = categories.shape[1]
    width = GROUPS * CLASSES
    spread = (iota((width, GROUPS), 0) // CLASSES == iota((width, GROUPS), 1)).astype(f32)
    wide = mm(spread.astype(bf16), categories)
    own = (iota((width, count), 0) % CLASSES).astype(f32)
    return jnp.where(wide == own, 1.0, 0.0).astype(bf16)


def normed(values):
    center = values - row_mean(values)
    scale = lax.rsqrt(row_mean(center * center) + epsilon)
    return center * scale, scale


def norm_silu(values, factor, offset):
    act = normed(values)[0] * factor + offset
    return act * sigmoid(act)


def norm_silu_back(values, factor, offset, grad):
    unit, scale = normed(values)
    act = unit * factor + offset
    gate = sigmoid(act)
    act_grad = grad * (gate + act * gate * (1.0 - gate))
    unit_grad = act_grad * factor
    pre_grad = scale * (unit_grad - row_mean(unit_grad) - unit * row_mean(unit_grad * unit))
    return (
        pre_grad,
        jnp.sum(act_grad * unit, 0, keepdims=True),
        jnp.sum(act_grad, 0, keepdims=True),
    )


def pick_columns(chosen, count):
    return jnp.where(iota((count, chosen.shape[1]), 0) == chosen, 1.0, 0.0).astype(bf16)


def column_order():
    source, target = iota((GATE, GATE), 0), iota((GATE, GATE), 1)
    half = LANES // 2
    moved = source // half % 3 * LANES + source // (3 * half) * half + source % half
    return jnp.where(moved == target, 1.0, 0.0).astype(bf16)


def pair_row(ref, pair):
    half = LANES // 2
    pieces = []
    for p in range(3):
        for e in range(2):
            at = pair * GATE + (3 * e + p) * half
            line, lane = at // LANES, at % LANES
            pieces.append(ref[line : line + 1, lane : lane + half])
    return jnp.concatenate(pieces, 1)


def plain_row(row):
    half = LANES // 2
    return jnp.concatenate(
        [
            row[:, (2 * p + e) * half : (2 * p + e + 1) * half]
            for e in range(2)
            for p in range(3)
        ],
        1,
    )


def group_sum(values):
    values = values + pltpu.roll(values, 4, 0)
    return values + pltpu.roll(values, 2, 0)


def lanes_of(pair):
    return slice(pair * LANES, (pair + 1) * LANES)


def gates_of(pair):
    return slice(pair * GATE, (pair + 1) * GATE)


def camera_of(camera_ref, s):
    return camera_ref[s] if len(camera_ref.shape) == 1 else camera_ref[:, s : s + 1]


def scale_row(camera_ref, camera_scale_ref, s, columns):
    row = None
    for c in range(camera_scale_ref.shape[0]):
        part = jnp.where(camera_of(camera_ref, s) == c, camera_scale_ref[c : c + 1, columns], 0.0)
        row = part if row is None else row + part
    return row


def observe_kernel(
    camera_ref,
    cat_ref,
    table_ref,
    stoch_gain_ref,
    stoch_bias_ref,
    input_ref,
    weight_ref,
    cell_gain_ref,
    cell_bias_ref,
    start_ref,
    order_ref,
    later_cat_ref,
    embed_ref,
    camera_scale_ref,
    post_embed_ref,
    held_ref,
    taken_ref,
    pre_ref,
    later_ref,
    later_pre_ref,
    gates_ref,
    states_ref,
    sent_ref,
    ordered_ref,
    state_ref,
    cell_ref,
    scaled_ref,
    embed_part_ref,
    inputs_ref,
):
    frames, width = held_ref.shape
    length = frames // 2
    half = LANES // 2
    ready(table_ref)
    begin(embed_ref, post_embed_ref)
    pre = mm(hot_rows([cat_ref[s] for s in range(2)]), table_ref[...])
    pre_ref[...] = pre
    taken = norm_silu(pre, stoch_gain_ref[...], stoch_bias_ref[...]).astype(bf16)
    taken_ref[...] = taken
    order = column_order()
    values = []
    for pair in range(PAIRS):
        columns = mm(input_ref[:, gates_of(pair)], order).astype(bf16)
        ordered_ref[:, gates_of(pair)] = columns
        values.append(mm(taken, columns))
    middle = jnp.sum(values[0] + values[1] + values[2] + values[3], 1, keepdims=True)
    middle = middle * (1.0 / (PAIRS * GATE))
    for pair in range(PAIRS):
        for p in range(3):
            at = p * PAIRS * frames + pair * frames
            inputs_ref[at : at + frames, :] = values[pair][:, lanes_of(p)] - middle
    source, target = iota((3 * half, GATE), 0), iota((3 * half, GATE), 1)
    same = (source // half == target // LANES) & (source % half == target % half)
    weights = mm(weight_ref[...], jnp.where(same, 1.0, 0.0).astype(bf16))
    own = iota(weights.shape, 0) // half % 2 == iota(weights.shape, 1) // half % 2
    state_ref[...] = jnp.where(own, weights, 0.0).astype(bf16)
    gain_rows = [pair_row(cell_gain_ref, pair) for pair in range(PAIRS)]
    bias_rows = [pair_row(cell_bias_ref, pair) for pair in range(PAIRS)]
    cell_ref[...] = jnp.concatenate(
        [jnp.concatenate(gain_rows, 1), jnp.concatenate(bias_rows, 1)], 0
    )
    row_pair = iota((8, LANES), 0) // 2
    part = iota((8, GATE), 1) // LANES
    gain = jnp.concatenate([row for row in gain_rows for _ in range(2)], 0) * 0.5
    bias = jnp.concatenate([row for row in bias_rows for _ in range(2)], 0)
    bias = (bias - jnp.where(part == 2, 1.0, 0.0)) * 0.5
    start = jnp.concatenate(
        [start_ref[:, lanes_of(pair)].astype(f32) for pair in range(PAIRS)], 0
    )
    scale = 1.0 / (PAIRS * GATE)

    def advance(step, state, first=False):
        wide = jnp.concatenate([jnp.where(row_pair == j, state, 0.0) for j in range(PAIRS)], 1)
        values = mm(wide.astype(bf16), state_ref[...])
        parts = [values[:, lanes_of(p)] for p in range(3)]
        for p in range(3):
            at = p * PAIRS * frames + step
            if not first:
                parts[p] = parts[p] + inputs_ref[pl.ds(at - 1, 8, stride=length), :]
            gates_ref[pl.ds(at, 8, stride=length), :] = parts[p]
        total = parts[0] + parts[1] + parts[2]
        square = parts[0] * parts[0] + parts[1] * parts[1] + parts[2] * parts[2]
        mean = jnp.sum(group_sum(total), 1, keepdims=True) * scale
        spread = jnp.sum(group_sum(square), 1, keepdims=True) * scale - mean * mean
        factor = lax.rsqrt(jnp.maximum(spread, 0.0) + epsilon)
        units = [
            (parts[p] - mean) * (factor * gain[:, lanes_of(p)]) + bias[:, lanes_of(p)]
            for p in range(3)
        ]
        update = 0.5 * jnp.tanh(units[2]) + 0.5
        candidate = jnp.tanh(jnp.tanh(units[0]) * units[1] + units[1])
        renewed = state + update * (candidate - state)
        states_ref[pl.ds(step, 8, stride=length), :] = renewed
        return renewed

    for ref in (taken_ref, pre_ref, ordered_ref, state_ref, cell_ref):
        ref.flush()
    state = advance(0, start, True)
    ready(camera_ref, later_cat_ref, embed_ref, camera_scale_ref, post_embed_ref)
    steps, _, count = later_cat_ref.shape
    chunks = steps // 2
    share = 8
    features = embed_ref.shape[1] // (chunks + 1)

    def scale_block(chunk):
        columns = pl.ds(pl.multiple_of(chunk * features, features), features)
        for s in range(2):
            rows = slice(s * length, (s + 1) * length)
            factor = scale_row(camera_ref, camera_scale_ref, s, columns)
            scaled_ref[rows, columns] = (embed_ref[rows, columns].astype(f32) * factor).astype(
                bf16
            )

    def embed_block(chunk, side):
        block = features // 2
        columns = pl.ds(pl.multiple_of(chunk * features + side * block, block), block)
        return mm(scaled_ref[:, columns], post_embed_ref[columns, :])

    scale_block(chunks)
    embed_part_ref[...] = embed_block(chunks, 0) + embed_block(chunks, 1)

    def several(chunk, state):
        rows = pl.ds(pl.multiple_of(chunk * 2 * count, 2 * count), 2 * count)
        hot = hot_rows([later_cat_ref[2 * chunk], later_cat_ref[2 * chunk + 1]])
        later_pre = None
        block = hot.shape[1] // 4
        for step in range(share):
            state = advance(1 + chunk * share + step, state)
            if step < 4:
                columns = slice(step * block, (step + 1) * block)
                part = mm(hot[:, columns], table_ref[columns, :])
                later_pre = part if later_pre is None else later_pre + part
            if step == 3:
                scale_block(chunk)
            if step in (5, 6):
                embed_part_ref[...] += embed_block(chunk, step - 5)
            if step == 4:
                later_pre_ref[rows, :] = later_pre
                later = norm_silu(later_pre, stoch_gain_ref[...], stoch_bias_ref[...])
                later_ref[rows, :] = later.astype(bf16)
        return state

    state = lax.fori_loop(0, chunks, several, state)
    for ref in (later_ref, later_pre_ref, scaled_ref, embed_part_ref):
        ref.flush()
    lax.fori_loop(1 + chunks * share, length, advance, state, unroll=7)
    gates_ref.flush()
    states_ref.flush()
    for pair in range(PAIRS):
        held_ref[:, lanes_of(pair)] = states_ref[pair * frames : (pair + 1) * frames, :].astype(
            bf16
        )
    chosen = pick_columns(order_ref[:, : sent_ref.shape[0]], frames)
    held_ref.flush()
    sent_ref[:, :width] = mm_tn(chosen, held_ref[...]).astype(bf16)
    sent_ref[:, width:] = mm_tn(chosen, taken).astype(bf16)


def mixed_probs(logits):
    shifted = jnp.exp(logits - jnp.max(logits, 1, keepdims=True))
    probability = shifted / jnp.sum(shifted, 1, keepdims=True)
    return probability, (1.0 - unimix) * probability + unimix / CLASSES


def softmax_back(probability, grad):
    grad = (1.0 - unimix) * grad
    return probability * (grad - jnp.sum(probability * grad, 1, keepdims=True))


def heads_kernel(
    core_ref,
    held_ref,
    prior_hidden_ref,
    prior_gain_ref,
    prior_bias_ref,
    prior_out_ref,
    prior_shift_ref,
    post_deter_ref,
    embed_part_ref,
    post_gain_ref,
    post_bias_ref,
    post_out_ref,
    post_shift_ref,
    scaled_ref,
    post_low_ref,
    prior_low_ref,
    small_ref,
    keep_ref,
    send_ref,
    post_act_ref,
    prior_act_ref,
):
    frames, width = held_ref.shape
    features = scaled_ref.shape[1]
    held = held_ref[...]
    split = (GROUPS, CLASSES, frames)
    ready(prior_hidden_ref)
    begin(post_out_ref, scaled_ref)
    prior_pre = mm(held, prior_hidden_ref[...])
    prior_act = norm_silu(prior_pre, prior_gain_ref[...], prior_bias_ref[...]).astype(bf16)
    prior_logits = mm(prior_act, prior_out_ref[...]) + prior_shift_ref[...]
    prior_prob, prior_mix = mixed_probs(prior_logits.T.reshape(split))
    post_pre = mm(held, post_deter_ref[...]) + embed_part_ref[...]
    post_act = norm_silu(post_pre, post_gain_ref[...], post_bias_ref[...]).astype(bf16)
    post_logits = mm(post_act, post_out_ref[...]) + post_shift_ref[...]
    post_prob, post_mix = mixed_probs(post_logits.T.reshape(split))
    ratio = jnp.log(post_mix) - jnp.log(prior_mix)
    divergence = jnp.sum(jnp.sum(post_mix * ratio, 0, keepdims=True), 1, keepdims=True)
    slope = sigmoid(divergence - free_bits)
    post_log = softmax_back(post_prob, slope * (ratio + 1.0))
    prior_log = softmax_back(prior_prob, -slope * (post_mix / prior_mix))
    post_log = post_log.reshape(GROUPS * CLASSES, frames).T.astype(bf16)
    prior_log = prior_log.reshape(GROUPS * CLASSES, frames).T.astype(bf16)
    post_low, post_gain_grad, post_bias_grad = norm_silu_back(
        post_pre, post_gain_ref[...], post_bias_ref[...], mm_nt(post_log, post_out_ref[...])
    )
    prior_low, prior_gain_grad, prior_bias_grad = norm_silu_back(
        prior_pre, prior_gain_ref[...], prior_bias_ref[...], mm_nt(prior_log, prior_out_ref[...])
    )
    post_low, prior_low = post_low.astype(bf16), prior_low.astype(bf16)
    post_low_ref[...] = post_low
    prior_low_ref[...] = prior_low
    post_low_ref.flush()
    prior_low_ref.flush()
    small_ref[...] = jnp.concatenate(
        [
            post_gain_grad,
            post_bias_grad,
            prior_gain_grad,
            prior_bias_grad,
            jnp.sum(post_log.astype(f32), 0, keepdims=True),
            jnp.sum(prior_log.astype(f32), 0, keepdims=True),
        ],
        1,
    )
    post_act_ref[...] = post_act
    prior_act_ref[...] = prior_act
    products = (
        (held_ref, post_low),
        (held_ref, prior_low),
        (post_act_ref, post_log[:, :width]),
        (post_act_ref, post_log[:, width:]),
        (prior_act_ref, prior_log[:, :width]),
        (prior_act_ref, prior_log[:, width:]),
    )
    shares = keep_ref.shape[0] // 2
    unit_rows, embed_rows = width // shares, features // shares
    small, large = unit_rows // 4, embed_rows // 4
    for slot, ref in ((1, send_ref), (0, keep_ref)):
        parity = core_ref[0] ^ slot
        for y in range(shares // 2):
            share = 2 * y + parity
            places = [block_place(parity, y, block) for block in range(4)]
            at = pl.multiple_of(share * unit_rows, unit_rows)
            for index, (left, right) in enumerate(products):
                grad = mm_tn(left[:, pl.ds(at, unit_rows)], right).astype(bf16)
                first = large + index * small
                for block in range(4):
                    ref[places[block], first : first + small, :] = grad[
                        block * small : (block + 1) * small
                    ]
            for block in range(4):
                at = pl.multiple_of(share * embed_rows + block * large, large)
                grad = mm_tn(scaled_ref[:, pl.ds(at, large)], post_low)
                ref[places[block], :large, :] = grad.astype(bf16)
                ref.flush(places[block])


def other_place(parity, y, block):
    low_bit, next_bit = block // 2, block % 2
    return jnp.where(
        parity == 0, 4 * low_bit + 2 * y + next_bit, 4 * y + 2 * low_bit + next_bit
    )


def block_place(parity, y, block):
    low_bit, next_bit = block // 2, block % 2
    return jnp.where(
        parity == 0, 4 * y + 2 * low_bit + next_bit, 4 * next_bit + 2 * y + low_bit
    )


def embed_back_kernel(
    camera_ref,
    embed_ref,
    camera_scale_ref,
    post_low_ref,
    prior_low_ref,
    post_embed_ref,
    post_deter_ref,
    prior_hidden_ref,
    held_grad_ref,
    embed_grad_ref,
    camera_grad_ref,
):
    frames, features = embed_ref.shape
    length = frames // 2
    cameras = camera_scale_ref.shape[0]
    held_grad_ref[...] = mm_nt(post_low_ref[...], post_deter_ref[...]) + mm_nt(
        prior_low_ref[...], prior_hidden_ref[...]
    )
    wide = features // 4
    for q in range(4):
        columns = slice(q * wide, (q + 1) * wide)
        scaled_grad = mm_nt(post_low_ref[...], post_embed_ref[columns, :])
        terms = [jnp.zeros((1, wide), f32) for _ in range(cameras)]
        for s in range(2):
            rows = slice(s * length, (s + 1) * length)
            part = scaled_grad[rows]
            scale = scale_row(camera_ref, camera_scale_ref, s, columns)
            embed_grad_ref[rows, columns] = part * scale
            term = jnp.sum(part * embed_ref[rows, columns].astype(f32), 0, keepdims=True)
            for c in range(cameras):
                terms[c] = terms[c] + jnp.where(camera_ref[s] == c, term, 0.0)
        camera_grad_ref[:, columns] = jnp.concatenate(terms, 0)


def cell_gates(units, cell_ref, pair):
    scaled = units * cell_ref[:1, gates_of(pair)] + cell_ref[1:, gates_of(pair)]
    reset = sigmoid(scaled[:, :LANES])
    middle = scaled[:, LANES : 2 * LANES]
    return reset, middle, jnp.tanh(reset * middle), sigmoid(scaled[:, 2 * LANES :] - 1.0)


def rollout_kernel(
    got_ref,
    inputs_ref,
    ordered_ref,
    state_ref,
    cell_ref,
    cot_ref,
    states_ref,
    back_ref,
    gate_grad_ref,
    cell_grad_ref,
    state_grad_ref,
    held_ref,
    unit_ref,
    scale_ref,
    part_ref,
    gain_grad_ref,
    bias_grad_ref,
    turned_ref,
):
    horizon, count, width = states_ref.shape
    unit_ref[:count, :] = mm(got_ref[:, width:], ordered_ref[...])
    chunk = (horizon - 1) * count // 2
    for at in range(0, (horizon - 1) * count, chunk):
        rows = slice(count + at, count + at + chunk)
        unit_ref[rows, :] = mm(inputs_ref[at : at + chunk, :], ordered_ref[...])
    norm = 1.0 / (PAIRS * GATE)

    def advance(step, state):
        rows = pl.ds(pl.multiple_of(step * count, count), count)
        held = state.astype(bf16)
        held_ref[rows, :] = held
        values = []
        total = jnp.zeros((count, LANES), f32)
        for pair in range(PAIRS):
            value = unit_ref[rows, gates_of(pair)] + mm(
                held[:, lanes_of(pair)], state_ref[lanes_of(pair), :]
            )
            values.append(value)
            for p in range(3):
                total = total + value[:, lanes_of(p)]
        mean = jnp.sum(total, 1, keepdims=True) * norm
        values = [value - mean for value in values]
        square = jnp.zeros((count, LANES), f32)
        for value in values:
            for p in range(3):
                square = square + value[:, lanes_of(p)] * value[:, lanes_of(p)]
        factor = lax.rsqrt(jnp.sum(square, 1, keepdims=True) * norm + epsilon)
        scale_ref[rows, :] = jnp.broadcast_to(factor, (count, LANES))
        fresh = []
        for pair in range(PAIRS):
            units = values[pair] * factor
            unit_ref[rows, gates_of(pair)] = units
            _, _, candidate, update = cell_gates(units, cell_ref, pair)
            old = state[:, lanes_of(pair)]
            fresh.append(old + update * (candidate - old))
        renewed = jnp.concatenate(fresh, 1)
        states_ref[step] = renewed
        return renewed

    ready(state_ref, cell_ref)
    first = got_ref[:, :width].astype(f32)
    lax.fori_loop(0, horizon, advance, first, unroll=5)
    states_ref.flush()
    turned_ref[...] = state_ref[...].astype(f32).T.astype(bf16)
    ready(cot_ref)
    gain_grad_ref[...] = jnp.zeros_like(gain_grad_ref)
    bias_grad_ref[...] = jnp.zeros_like(bias_grad_ref)

    def retreat(index, carry):
        step = horizon - 1 - index
        rows = pl.ds(pl.multiple_of(step * count, count), count)
        before = states_ref[jnp.maximum(step - 1, 0)]
        before = jnp.where(step == 0, first, before)
        grads = cot_ref[step].astype(f32) + carry
        low = jnp.zeros((count, LANES), f32)
        high = jnp.zeros((count, LANES), f32)
        kept = []
        for pair in range(PAIRS):
            units = unit_ref[rows, gates_of(pair)]
            reset, middle, candidate, update = cell_gates(units, cell_ref, pair)
            grad = grads[:, lanes_of(pair)]
            rest = 1.0 - update
            inner = grad * update * (1.0 - candidate * candidate)
            parts = jnp.concatenate(
                [
                    inner * middle * (reset * (1.0 - reset)),
                    inner * reset,
                    grad * (candidate - before[:, lanes_of(pair)]) * (update * rest),
                ],
                1,
            )
            weighted = parts * units
            gain_grad_ref[:, gates_of(pair)] += jnp.sum(weighted.reshape(count // 8, 8, GATE), 0)
            bias_grad_ref[:, gates_of(pair)] += jnp.sum(parts.reshape(count // 8, 8, GATE), 0)
            parts = parts * cell_ref[:1, gates_of(pair)]
            weighted = parts * units
            for p in range(3):
                low = low + parts[:, lanes_of(p)]
                high = high + weighted[:, lanes_of(p)]
            part_ref[:, gates_of(pair)] = parts
            kept.append(grad * rest)
        low = jnp.sum(low, 1, keepdims=True) * norm
        high = jnp.sum(high, 1, keepdims=True) * norm
        factor = scale_ref[rows, :][:, :1]
        carried = []
        for pair in range(PAIRS):
            units = unit_ref[rows, gates_of(pair)]
            grad = (factor * (part_ref[:, gates_of(pair)] - low - units * high)).astype(bf16)
            gate_grad_ref[rows, gates_of(pair)] = grad
            carried.append(kept[pair] + mm(grad, turned_ref[:, lanes_of(pair)]))
        return jnp.concatenate(carried, 1)

    carry = lax.fori_loop(0, horizon, retreat, jnp.zeros((count, width), f32), unroll=5)
    back_ref[:, :width] = carry.astype(bf16)
    back_ref[:, width:] = mm_nt(gate_grad_ref[:count, :], ordered_ref[...]).astype(bf16)
    back_ref.flush()
    gate_grad_ref.flush()
    for pair in range(PAIRS):
        state_grad_ref[pair] = mm_tn(held_ref[:, lanes_of(pair)], gate_grad_ref[:, gates_of(pair)])
    cell_grad_ref[...] = jnp.concatenate(
        [
            jnp.sum(gain_grad_ref[...], 0, keepdims=True),
            jnp.sum(bias_grad_ref[...], 0, keepdims=True),
        ],
        0,
    )


def rollout_grads_kernel(
    gate_grad_ref,
    got_ref,
    inputs_ref,
    pre_ref,
    cat_ref,
    ordered_ref,
    stoch_gain_ref,
    stoch_bias_ref,
    input_grad_ref,
    table_grad_ref,
    stoch_grad_ref,
    hot_ref,
    low_ref,
    taken_ref,
):
    steps, _, count = cat_ref.shape
    width = inputs_ref.shape[1]
    taken_ref[:count, :] = got_ref[:, width:]
    taken_ref[count:, :] = inputs_ref[...]
    ready(gate_grad_ref)
    begin(pre_ref, ordered_ref)
    input_grad_ref[...] = mm_tn(taken_ref[...], gate_grad_ref[...])
    input_grad_ref.flush()
    gain_sum = jnp.zeros(stoch_gain_ref.shape, f32)
    bias_sum = jnp.zeros(stoch_bias_ref.shape, f32)
    grads = mm_nt(gate_grad_ref[count:, :], ordered_ref[...])
    for at in range(0, steps, 2):
        rows = slice(at * count, (at + 2) * count)
        low, gain_grad, bias_grad = norm_silu_back(
            pre_ref[rows, :], stoch_gain_ref[...], stoch_bias_ref[...], grads[rows]
        )
        gain_sum = gain_sum + gain_grad
        bias_sum = bias_sum + bias_grad
        low_ref[rows, :] = low.astype(bf16)
        hot_ref[:, rows] = hot_columns([cat_ref[at], cat_ref[at + 1]])
    table_grad_ref[...] = mm(hot_ref[...], low_ref[...])
    stoch_grad_ref[...] = jnp.concatenate([gain_sum, bias_sum], 1)


def observe_back_kernel(
    core_ref,
    held_grad_ref,
    back_ref,
    order_ref,
    cat_ref,
    taken_ref,
    pre_ref,
    gates_ref,
    states_ref,
    start_ref,
    stoch_gain_ref,
    stoch_bias_ref,
    ordered_ref,
    state_ref,
    cell_ref,
    input_part_ref,
    state_part_ref,
    table_part_ref,
    stoch_part_ref,
    cell_part_ref,
    small_ref,
    camera_grad_ref,
    start_grad_ref,
    keep_ref,
    send_ref,
    keep_more_ref,
    send_more_ref,
    grads_ref,
    turned_ref,
    arriving_ref,
    slope_ref,
    factor_ref,
    unit_ref,
    mean_ref,
    cross_ref,
    rest_ref,
    flat_ref,
    lean_ref,
    scale_ref,
    grad_ref,
    low_ref,
    high_ref,
    previous_ref,
):
    frames, width = held_grad_ref.shape
    length = frames // 2
    norm = 1.0 / (PAIRS * GATE)
    chosen = pick_columns(order_ref[:, : back_ref.shape[0]], frames)
    held_grad = held_grad_ref[...] + mm(chosen, back_ref[:, :width])
    turned_ref[...] = state_ref[...].astype(f32).T.astype(bf16)
    start = jnp.concatenate(
        [start_ref[:, lanes_of(pair)].astype(f32) for pair in range(PAIRS)], 0
    )
    for pair in range(PAIRS):
        arriving_ref[pair * frames : (pair + 1) * frames, :] = held_grad[:, lanes_of(pair)]
    long = PAIRS * frames
    for s in range(2):
        blocks = [
            slice((2 * pair + s) * length, (2 * pair + s + 1) * length) for pair in range(PAIRS)
        ]
        total = jnp.zeros((length, LANES), f32)
        for rows in blocks:
            for p in range(3):
                total = total + gates_ref[p * long + rows.start : p * long + rows.stop, :]
        mean = jnp.sum(total, 1, keepdims=True) * norm
        square = jnp.zeros((length, LANES), f32)
        for rows in blocks:
            for p in range(3):
                center = gates_ref[p * long + rows.start : p * long + rows.stop, :] - mean
                square = square + center * center
        scale = lax.rsqrt(jnp.sum(square, 1, keepdims=True) * norm + epsilon)
        for pair, rows in enumerate(blocks):
            gain = cell_ref[:1, gates_of(pair)]
            units = jnp.concatenate(
                [gates_ref[p * long + rows.start : p * long + rows.stop, :] for p in range(3)], 1
            )
            units = (units - mean) * scale
            reset, middle, candidate, update = cell_gates(units, cell_ref, pair)
            row = 2 * pair + s
            previous = jnp.where(
                iota((length, LANES), 0) == 0,
                start[row : row + 1, :],
                pltpu.roll(states_ref[rows, :], 1, 0),
            )
            previous_ref[rows, :] = previous
            inner = update * (1.0 - candidate * candidate)
            slope = jnp.concatenate(
                [
                    inner * middle * (reset * (1.0 - reset)),
                    inner * reset,
                    (candidate - previous) * (update * (1.0 - update)),
                ],
                1,
            )
            slope_ref[rows, :] = slope
            slope = slope * gain
            weighted = slope * units
            mean_ref[rows, :] = norm * (
                slope[:, :LANES] + slope[:, LANES : 2 * LANES] + slope[:, 2 * LANES :]
            )
            cross_ref[rows, :] = norm * (
                weighted[:, :LANES] + weighted[:, LANES : 2 * LANES] + weighted[:, 2 * LANES :]
            )
            for p in range(3):
                factor_ref[p * long + rows.start : p * long + rows.stop, :] = (
                    scale * slope[:, lanes_of(p)]
                )
            unit_ref[rows, :] = scale * units
            rest_ref[rows, :] = 1.0 - update
            scale_ref[rows, :] = jnp.broadcast_to(scale, (length, LANES))
            weight = state_ref[lanes_of(pair), :]
            flat_ref[rows, :] = scale * mm_nt(jnp.ones((8, GATE), bf16), weight)[:1, :]
            lean_ref[rows, :] = mm_nt((scale * units).astype(bf16), weight)
    row_pair = iota((8, LANES), 0) // 2

    def retreat(index, carry):
        step = length - 1 - index
        rows = pl.ds(step, 8, stride=length)
        grad = arriving_ref[rows, :] + carry
        wide = jnp.concatenate(
            [grad * factor_ref[pl.ds(p * long + step, 8, stride=length), :] for p in range(3)], 1
        )
        turned = mm(wide.astype(bf16), turned_ref[...])
        low = jnp.sum(group_sum(grad * mean_ref[rows, :]), 1, keepdims=True)
        high = jnp.sum(group_sum(grad * cross_ref[rows, :]), 1, keepdims=True)
        grad_ref[rows, :] = grad
        low_ref[rows, :] = jnp.broadcast_to(low, (8, LANES))
        high_ref[rows, :] = jnp.broadcast_to(high, (8, LANES))
        kept = grad * rest_ref[rows, :] - low * flat_ref[rows, :] - high * lean_ref[rows, :]
        near = jnp.where(row_pair == 0, turned[:, lanes_of(0)], turned[:, lanes_of(1)])
        far = jnp.where(row_pair == 2, turned[:, lanes_of(2)], turned[:, lanes_of(3)])
        return kept + jnp.where(row_pair < 2, near, far)

    begin(ordered_ref, input_part_ref, state_part_ref, table_part_ref)
    carry = lax.fori_loop(0, length, retreat, jnp.zeros((8, LANES), f32), unroll=8)
    for pair in range(PAIRS):
        start_grad_ref[:, lanes_of(pair)] = carry[2 * pair : 2 * pair + 2, :]
    frame = iota((frames, width), 0) % length
    earlier = jnp.where(frame == 0, 0.0, pltpu.roll(taken_ref[...].astype(f32), 1, 0)).astype(bf16)
    input_grad = jnp.zeros((frames, width), f32)
    gains, biases, inputs = [], [], []
    shares = grads_ref.shape[0]
    unit_rows = width // shares
    for pair in range(PAIRS):
        rows = slice(pair * frames, (pair + 1) * frames)
        grad = jnp.concatenate([grad_ref[rows, :]] * 3, 1)
        gate_grad = grad * slope_ref[rows, :]
        biases.append(jnp.sum(gate_grad, 0, keepdims=True))
        scale = scale_ref[rows, :][:, :1]
        units = unit_ref[rows, :]
        gains.append(jnp.sum(gate_grad * (units / scale), 0, keepdims=True))
        low = low_ref[rows, :][:, :1]
        high = high_ref[rows, :][:, :1]
        factors = jnp.concatenate(
            [factor_ref[p * long + rows.start : p * long + rows.stop, :] for p in range(3)], 1
        )
        gate_low = (grad * factors - low * scale - high * units).astype(bf16)
        columns = ordered_ref[:, gates_of(pair)]
        input_grad = input_grad + mm_nt(gate_low, columns)
        weight_grad = mm_tn(earlier, gate_low) + input_part_ref[:, gates_of(pair)]
        inputs.append(weight_grad.astype(bf16))
        state_grad = mm_tn(previous_ref[rows, :].astype(bf16), gate_low) + state_part_ref[pair]
        half = LANES // 2
        upper = iota((half, GATE), 1) % LANES < half
        folded = jnp.where(upper, state_grad[:half], state_grad[half:])
        at = 3 * unit_rows + 2 * unit_rows
        grads_ref[pair, at : at + half, :GATE] = folded.astype(bf16)
    weights = jnp.concatenate(inputs, 1)
    for q in range(shares):
        for c in range(3):
            grads_ref[q, c * unit_rows : (c + 1) * unit_rows, :] = weights[
                q * unit_rows : (q + 1) * unit_rows, c * width : (c + 1) * width
            ]
    taken_grad = jnp.where(
        frame == length - 1, 0.0, pltpu.roll(input_grad, frames - 1, 0)
    ) + mm(chosen, back_ref[:, width:])
    low, gain_grad, bias_grad = norm_silu_back(
        pre_ref[...], stoch_gain_ref[...], stoch_bias_ref[...], taken_grad
    )
    stoch = jnp.concatenate([gain_grad, bias_grad], 1) + stoch_part_ref[...]
    hot = hot_columns([cat_ref[s] for s in range(2)])
    table_grad = mm(hot, low.astype(bf16)) + table_part_ref[...]
    rows = table_grad.shape[0] // shares
    vector_row = 5 * unit_rows
    classes = GROUPS * CLASSES
    wide = camera_grad_ref.shape[1] // shares
    for q in range(shares):
        grads_ref[q, 3 * unit_rows : 3 * unit_rows + rows, :] = table_grad[
            q * rows : (q + 1) * rows
        ].astype(bf16)
        unit = slice(q * unit_rows, (q + 1) * unit_rows)
        logit = slice(q * classes // shares, (q + 1) * classes // shares)
        units = [stoch[:, unit], stoch[:, width + unit.start : width + unit.stop]]
        units += [
            small_ref[:, k * width + unit.start : k * width + unit.stop] for k in range(4)
        ]
        logits = [
            small_ref[
                :, 4 * width + k * classes + logit.start : 4 * width + k * classes + logit.stop
            ]
            for k in range(2)
        ]
        cells = [
            plain_row(kind[q] + cell_part_ref[k : k + 1, gates_of(q)])
            for k, kind in enumerate((gains, biases))
        ]
        cameras = [
            camera_grad_ref[c : c + 1, q * wide : (q + 1) * wide]
            for c in range(camera_grad_ref.shape[0])
        ]
        lines = []
        for vector in units + logits + cells + cameras:
            lines += [vector[:, at : at + LANES] for at in range(0, vector.shape[1], LANES)]
        lines.append(jnp.zeros((LANES // 2 - len(lines), LANES), f32))
        grads_ref[q, vector_row:, GATE:] = jnp.concatenate(lines, 0).astype(bf16)
    block, more = keep_ref.shape[1], keep_more_ref.shape[1]
    for slot, ref, more_ref in ((1, send_ref, send_more_ref), (0, keep_ref, keep_more_ref)):
        parity = core_ref[0] ^ slot
        for y in range(shares // 2):
            for index in range(4):
                at = index * (block + more)
                place = block_place(parity, y, index)
                ref[place] = grads_ref[2 * y + parity, at : at + block, :]
                place = other_place(parity, y, index)
                more_ref[place] = grads_ref[2 * y + parity, at + block : at + block + more, :]
        ref.flush()
        more_ref.flush()


def place_blocks(where_ref, own_ref, got_ref, full_ref, at=0):
    block, whole = own_ref.shape[0] // 2, full_ref.shape[0] // 4
    parity, bit = where_ref[0], where_ref[1]
    for side in range(2):
        for inner in range(2):
            rows = slice(inner * block, (inner + 1) * block)
            piece = jnp.where(bit == side, own_ref[rows, :], got_ref[rows, :]).astype(f32)
            place = jnp.where(parity == 0, 2 * side + inner, 2 * inner + side)
            full_ref[pl.ds(pl.multiple_of(place * whole + at, 16), block), :] = piece


def finish_heads_kernel(
    where_ref,
    own_ref,
    got_ref,
    post_embed_ref,
    post_deter_ref,
    prior_hidden_ref,
    post_out_ref,
    prior_out_ref,
    full_ref,
):
    place_blocks(where_ref, own_ref, got_ref, full_ref)
    block = full_ref.shape[0] // 4
    width = own_ref.shape[1]
    large, small = post_embed_ref.shape[0] // 4, post_deter_ref.shape[0] // 4
    for index in range(4):
        at = index * block
        post_embed_ref[index * large : (index + 1) * large, :] = full_ref[at : at + large, :]
        rows = slice(index * small, (index + 1) * small)
        for member, (ref, column) in enumerate(
            (
                (post_deter_ref, 0),
                (prior_hidden_ref, 0),
                (post_out_ref, 0),
                (post_out_ref, width),
                (prior_out_ref, 0),
                (prior_out_ref, width),
            )
        ):
            first = at + large + member * small
            ref[rows, column : column + width] = full_ref[first : first + small, :]


def finish_kernel(
    where_ref, flat_where_ref, own_ref, got_ref, own_more_ref, got_more_ref, *refs
):
    outs, full_ref = refs[:-1], refs[-1]
    width = own_ref.shape[1]
    place_blocks(where_ref, own_ref, got_ref, full_ref)
    place_blocks(flat_where_ref, own_more_ref, got_more_ref, full_ref, own_ref.shape[0] // 2)
    input_ref, table_ref, state_ref = outs[:3]
    unit_rows = input_ref.shape[0]
    for pair in range(PAIRS):
        parts = []
        for p in range(3):
            at = pair * GATE + p * LANES
            line, column = at // width * unit_rows, at % width
            parts.append(full_ref[line : line + unit_rows, column : column + LANES])
        input_ref[:, gates_of(pair)] = plain_row(jnp.concatenate(parts, 1))
    at = 3 * unit_rows
    table_ref[...] = full_ref[at : at + table_ref.shape[0], :]
    at += table_ref.shape[0]
    half = state_ref.shape[1]
    folded = full_ref[at : at + half, :]
    for e in range(2):
        state_ref[e] = jnp.concatenate(
            [folded[:, (2 * p + e) * half : (2 * p + e + 1) * half] for p in range(3)], 1
        )
    for ref in outs[3:14]:
        for line in range(ref.shape[0]):
            for column in range(0, ref.shape[1], LANES):
                ref[line : line + 1, column : column + LANES] = full_ref[at : at + 1, GATE:]
                at += 1


def struct(shape, dtype):
    return jax.ShapeDtypeStruct(shape, dtype)


class Incoming:
    def __init__(self, ref, copy, late):
        self.ref, self.copy, self.shape, self.started = ref, copy, ref.shape, False
        if not late:
            self.begin()

    def begin(self):
        if not self.started:
            self.copy.start()
            self.started = True

    def ready(self):
        if self.copy is not None:
            self.begin()
            self.copy.wait()
            self.copy = None

    def __getitem__(self, index):
        self.ready()
        return self.ref[index]


class Near:
    def __init__(self, ref):
        self.ref, self.shape = ref, ref.shape

    def __getitem__(self, index):
        return self.ref[index]

    def __setitem__(self, index, value):
        self.ref[index] = value

    def flush(self):
        pass


class Outgoing:
    def __init__(self, ref, target, marks):
        self.ref, self.target, self.marks = ref, target, marks
        self.shape, self.copies = ref.shape, []

    def __getitem__(self, index):
        return self.ref[index]

    def __setitem__(self, index, value):
        self.ref[index] = value

    def flush(self, part=None):
        source, target = self.ref, self.target
        if part is not None:
            source, target = source.at[part], target.at[part]
        elif self.copies:
            return
        copy = pltpu.make_async_copy(source, target, self.marks[len(self.copies)])
        copy.start()
        self.copies.append(copy)

    def finish(self):
        self.flush()
        for copy in self.copies:
            copy.wait()


def begin(*refs):
    for ref in refs:
        if isinstance(ref, Incoming):
            ref.begin()


def ready(*refs):
    for ref in refs:
        if isinstance(ref, Incoming):
            ref.ready()


def call(
    kernel,
    name,
    outs,
    ins,
    mib,
    scratch=(),
    scalars=0,
    after=(),
    near_in=(),
    near_out=(),
    parts=(),
    late=(),
):
    count, total = len(ins), len(ins) + len(after) + len(outs)
    far_in = [k for k in range(scalars, count) if k not in near_in]
    far_out = [k for k in range(len(outs)) if k not in near_out]
    pieces = {k: outs[k].shape[0] if k in parts else 1 for k in far_out}
    near = pl.BlockSpec(memory_space=pltpu.VMEM)
    far = pl.BlockSpec(memory_space=pltpu.HBM)

    def body(*refs):
        given, made = list(refs[:count]), list(refs[count + len(after) : total])
        places = refs[total : total + len(far_in) + len(far_out)]
        rest = refs[total + len(far_in) + len(far_out) : -1]
        marks = refs[-1]
        for at, k in enumerate(far_in):
            copy = pltpu.make_async_copy(given[k], places[at], marks.at[at])
            given[k] = Incoming(places[at], copy, k in late)
        at = len(far_in)
        for place, k in zip(places[at:], far_out, strict=True):
            own = [marks.at[at + part] for part in range(pieces[k])]
            made[k] = Outgoing(place, made[k], own)
            at += pieces[k]
        for k in near_out:
            made[k] = Near(made[k])
        kernel(*given, *made, *rest)
        ready(*given)
        for k in far_out:
            made[k].flush()
        for k in far_out:
            made[k].finish()

    return pl.pallas_call(
        body,
        out_shape=tuple(
            pltpu.HBM(out.shape, out.dtype) if k in far_out else out for k, out in enumerate(outs)
        ),
        in_specs=[pl.BlockSpec(memory_space=pltpu.SMEM)] * scalars
        + [far if k in far_in else near for k in range(scalars, count)]
        + [far] * len(after),
        out_specs=tuple(far if k in far_out else near for k in range(len(outs))),
        scratch_shapes=[pltpu.VMEM(ins[k].shape, ins[k].dtype) for k in far_in]
        + [pltpu.VMEM(outs[k].shape, outs[k].dtype) for k in far_out]
        + list(scratch)
        + [pltpu.SemaphoreType.DMA((len(far_in) + sum(pieces.values()),))],
        compiler_params=pltpu.CompilerParams(vmem_limit_bytes=mib * 1024 * 1024),
        name=name,
    )(
        *[
            pltpu.with_memory_space_constraint(member, pltpu.HBM) if k in far_in else member
            for k, member in enumerate(ins)
        ],
        *[pltpu.with_memory_space_constraint(member, pltpu.HBM) for member in after],
    )


def linear_bits(bits):
    own = bits[0]
    rep_count = lax.axis_size("rep")
    index = lax.axis_index("seq") * rep_count + lax.axis_index("rep")
    if bits[0] != bits[1]:
        own = jnp.where(index & 1 == 0, bits[0], bits[1])
    return (index >> own) & 1


def swap(values, bits):
    count = lax.axis_size("seq") * lax.axis_size("rep")
    return lax.ppermute(
        values, ("seq", "rep"), [(i, i ^ (1 << bits[i & 1])) for i in range(count)]
    )


class Terms:
    def __init__(self, member):
        self.members = [(member, [])]

    def add(self, member):
        self.members.append((member, []))

    def part(self, *sides):
        total = 0.0
        for member, path in self.members:
            path = path + list(sides)
            rows = member.shape[0] >> len(path)
            split = member.reshape((2,) * len(path) + (rows, member.shape[1]))
            one = (1,) * len(path) + split.shape[-2:]
            chosen = lax.dynamic_slice(split, path + [0, 0], one)
            total = total + chosen.reshape(split.shape[-2:]).astype(f32)
        return total.astype(bf16)

    def fold(self, arrived, bits):
        self.add(arrived)
        own = linear_bits(bits).astype(jnp.int32)
        send = self.part(1 - own)
        self.members = [(member, path + [own]) for member, path in self.members]
        return send


def added(left, right):
    return (left.astype(f32) + right.astype(f32)).astype(bf16)


def joined(values, got, bits):
    own = linear_bits(bits)
    return jnp.where(
        own == 0, jnp.concatenate([values, got], 0), jnp.concatenate([got, values], 0)
    )


class Chain:
    def __init__(self, keep, send, stages, last):
        self.terms, self.piece = Terms(keep), None
        self.folds, self.middle = list(stages[:-1]), stages[-1]
        self.joins = list(reversed(stages[2:-1])) + [last]
        self.begin(send, (0, 0))

    def begin(self, send, bits):
        self.sent, self.last = send, bits
        self.arrived = swap(send, bits)

    def advance(self, *after):
        if after:
            self.arrived = lax.optimization_barrier((self.arrived, *after))[0]
        if self.folds:
            bits = self.folds.pop(0)
            self.begin(self.terms.fold(self.arrived, bits), bits)
            return
        if self.piece is None:
            bits = self.middle
            self.terms.add(self.arrived)
            self.piece = self.terms.part()
        else:
            bits = self.joins.pop(0)
            if self.last == self.middle:
                self.piece = added(self.piece, self.arrived)
            else:
                self.piece = joined(self.piece, self.arrived, self.last)
        self.begin(self.piece, bits)


def on_device(
    start_deter,
    post_cat,
    embed,
    camera,
    start_order,
    imag_cat,
    imag_cot,
    stoch_table,
    stoch_gain,
    stoch_bias,
    state_weight,
    input_weight,
    cell_gain,
    cell_bias,
    prior_hidden,
    prior_gain,
    prior_bias,
    prior_out,
    prior_shift,
    post_deter,
    post_embed,
    post_gain,
    post_bias,
    post_out,
    post_shift,
    camera_scale,
):
    seq_count, length = post_cat.shape[:2]
    frames = seq_count * length
    count, horizon, width = imag_cot.shape
    features = embed.shape[-1]
    shares = lax.axis_size("rep")
    rep_bits = shares.bit_length() - 1
    seq_bits = lax.axis_size("seq").bit_length() - 1
    half = LANES // 2
    gate_count = 3 * width
    classes = GROUPS * CLASSES
    rows = horizon * count
    long = PAIRS * frames
    unit_rows = width // shares
    core = (lax.axis_index("rep") & 1).astype(jnp.int32).reshape(1)
    row = lambda vector: vector.reshape(1, -1)
    cat = jnp.swapaxes(post_cat, 1, 2)
    later_cat = jnp.transpose(imag_cat, (1, 2, 0))
    stoch_rows = (row(stoch_gain), row(stoch_bias))
    embed_rows = embed.reshape(frames, features)

    low_bit, next_bit = rep_bits, rep_bits + 1
    deeper = [rep_bits + bit for bit in range(2, seq_bits)]
    outer = (low_bit, next_bit)
    stages = list(
        zip([1, low_bit, next_bit] + deeper, [next_bit, 1] + deeper + [low_bit], strict=True)
    )

    (
        held,
        taken,
        obs_pre,
        imag_inputs,
        imag_pre,
        obs_gates,
        obs_states,
        sent,
        ordered,
        state,
        cell,
        scaled,
        embed_part,
    ) = call(
        observe_kernel,
        "observe",
        [
            struct((frames, width), bf16),
            struct((frames, width), bf16),
            struct((frames, width), f32),
            struct((rows - count, width), bf16),
            struct((rows - count, width), f32),
            struct((3 * long, LANES), f32),
            struct((long, LANES), f32),
            struct((count, 2 * width), bf16),
            struct((width, gate_count), bf16),
            struct((width, GATE), bf16),
            struct((2, gate_count), f32),
            struct((frames, features), bf16),
            struct((frames, width), f32),
        ],
        (
            row(camera),
            cat,
            stoch_table,
            *stoch_rows,
            input_weight,
            state_weight.reshape(width, 3 * half),
            cell_gain.reshape(-1, LANES),
            cell_bias.reshape(-1, LANES),
            start_deter,
            start_order,
            later_cat,
            embed_rows,
            camera_scale,
            post_embed,
        ),
        36,
        scratch=[pltpu.VMEM((3 * long, LANES), f32)],
        late=(12, 14),
    )
    got = lax.all_to_all(sent, "seq", split_axis=0, concat_axis=0, tiled=True)

    square = struct((frames, width), bf16)
    embed_rows_count = features // shares
    head_rows = embed_rows_count + 6 * unit_rows
    blocks = struct((2 * shares, head_rows // 4, width), bf16)
    post_low, prior_low, head_small, keep, send = call(
        heads_kernel,
        "heads",
        [square, square, struct((1, 4 * width + 2 * classes), f32), blocks, blocks],
        (
            core,
            held,
            prior_hidden,
            row(prior_gain),
            row(prior_bias),
            prior_out,
            row(prior_shift),
            post_deter,
            embed_part,
            row(post_gain),
            row(post_bias),
            post_out,
            row(post_shift),
            scaled,
        ),
        34,
        scratch=[pltpu.VMEM((frames, width), bf16), pltpu.VMEM((frames, width), bf16)],
        scalars=1,
        parts=(3, 4),
        late=(11, 13),
    )
    flat = (shares * head_rows // 2, width)
    send, got = lax.optimization_barrier((send, got))
    tail_stages = list(
        zip([1, low_bit, next_bit] + deeper, [next_bit, 1, low_bit] + deeper, strict=True)
    )
    more_stages = list(
        zip([low_bit, 1, next_bit] + deeper, [1, low_bit, next_bit] + deeper, strict=True)
    )
    head = Chain(keep.reshape(flat), send.reshape(flat), stages, outer)
    held_grad, embed_grad, camera_grad = call(
        embed_back_kernel,
        "embed_back",
        [
            struct((frames, width), f32),
            struct((frames, features), f32),
            struct(camera_scale.shape, f32),
        ],
        (
            camera,
            embed_rows,
            camera_scale,
            post_low,
            prior_low,
            post_embed,
            post_deter,
            prior_hidden,
        ),
        18,
        scalars=1,
        after=(head.sent,),
    )
    head.advance(camera_grad)

    states, back, gate_grads, cell_part, state_part = call(
        rollout_kernel,
        "rollout",
        [
            struct((horizon, count, width), f32),
            struct((count, 2 * width), bf16),
            struct((rows, gate_count), bf16),
            struct((2, gate_count), f32),
            struct((PAIRS, LANES, GATE), f32),
        ],
        (
            got,
            imag_inputs,
            ordered,
            state,
            cell,
            jnp.swapaxes(imag_cot, 0, 1),
        ),
        36,
        scratch=[
            pltpu.VMEM((rows, width), bf16),
            pltpu.VMEM((rows, gate_count), f32),
            pltpu.VMEM((rows, LANES), f32),
            pltpu.VMEM((count, gate_count), f32),
            pltpu.VMEM((8, gate_count), f32),
            pltpu.VMEM((8, gate_count), f32),
            pltpu.VMEM((GATE, PAIRS * LANES), bf16),
        ],
        after=(head.sent,),
    )
    imag_deter = jnp.swapaxes(states, 0, 1)
    returned = lax.all_to_all(back, "seq", split_axis=0, concat_axis=0, tiled=True)
    head.advance(cell_part)

    input_part, table_part, stoch_part = call(
        rollout_grads_kernel,
        "rollout_grads",
        [
            struct((width, gate_count), f32),
            struct(stoch_table.shape, f32),
            struct((1, 2 * width), f32),
        ],
        (gate_grads, got, imag_inputs, imag_pre, later_cat, ordered, *stoch_rows),
        30,
        late=(3, 5),
        scratch=[
            pltpu.VMEM((stoch_table.shape[0], rows - count), bf16),
            pltpu.VMEM((rows - count, width), bf16),
            pltpu.VMEM((rows, width), bf16),
        ],
        after=(head.sent,),
    )
    head.advance(stoch_part, returned)
    tail_rows = 5 * unit_rows + half
    less = tail_rows // 8 // 16 * 16
    blocks = struct((2 * shares, tail_rows // 4 - less, width), bf16)
    more = struct((2 * shares, less, width), bf16)
    start_grad, tail_keep, tail_send, more_keep, more_send = call(
        observe_back_kernel,
        "observe_back",
        [struct((seq_count, width), f32), blocks, blocks, more, more],
        (
            core,
            held_grad,
            returned,
            start_order,
            cat,
            taken,
            obs_pre,
            obs_gates,
            obs_states,
            start_deter,
            *stoch_rows,
            ordered,
            state,
            cell,
            input_part,
            state_part,
            table_part,
            stoch_part,
            cell_part,
            head_small,
            camera_grad,
        ),
        30,
        after=(head.sent,),
        scratch=[
            pltpu.VMEM((shares, tail_rows, width), bf16),
            pltpu.VMEM((GATE, PAIRS * LANES), bf16),
            pltpu.VMEM((long, LANES), f32),
            pltpu.VMEM((long, GATE), f32),
            pltpu.VMEM((3 * long, LANES), f32),
            pltpu.VMEM((long, GATE), f32),
        ]
        + [pltpu.VMEM((long, LANES), f32)] * 10,
        scalars=1,
        near_out=(1, 3),
        late=(12, 15, 16, 17),
    )
    tail_send, head.arrived = lax.optimization_barrier((tail_send, head.arrived))
    for _ in deeper:
        head.advance()
    tails = [
        Chain(keep.reshape(-1, width), send.reshape(-1, width), order, last)
        for keep, send, order, last in (
            (tail_keep, tail_send, tail_stages, outer),
            (more_keep, more_send, more_stages, (low_bit, low_bit)),
        )
    ]
    for step in range(2 * len(stages) - 2):
        if step in (1,4):
            head.advance(tails[0].sent)
        for tail in tails:
            tail.advance()
    while head.joins:
        head.advance(tails[0].sent)
    head_piece, head_other = head.piece, head.arrived
    where = jnp.concatenate([core, linear_bits(outer).astype(jnp.int32).reshape(1)])
    flat_where = jnp.stack([0, linear_bits((low_bit, low_bit)).astype(jnp.int32)])
    unit = struct((1, unit_rows), f32)
    logit = struct((1, classes // shares), f32)
    gate = struct((3, LANES), f32)
    small_rows = struct((unit_rows, width), f32)
    wide_rows = struct((unit_rows, classes), f32)
    post_embed_grad, post_deter_grad, prior_hidden_grad, post_out_grad, prior_out_grad = call(
        finish_heads_kernel,
        "finish_heads",
        [
            struct((embed_rows_count, width), f32),
            small_rows,
            small_rows,
            wide_rows,
            wide_rows,
        ],
        (where, head_piece, head_other),
        18,
        scratch=[pltpu.VMEM((head_rows, width), f32)],
        scalars=1,
        near_in=(1, 2),
    )
    finished = call(
        finish_kernel,
        "finish",
        [
            struct((unit_rows, gate_count), f32),
            struct((stoch_table.shape[0] // shares, width), f32),
            struct((2, half, 3 * half), f32),
            *[unit] * 6,
            logit,
            logit,
            gate,
            gate,
            struct((camera_scale.shape[0], features // shares), f32),
        ],
        (where, flat_where, *[member for tail in tails for member in (tail.piece, tail.arrived)]),
        12,
        scratch=[pltpu.VMEM((tail_rows, width), f32)],
        scalars=2,
        near_in=(2, 3, 4, 5),
        after=(post_embed_grad,),
    )
    input_weight_grad, stoch_table_grad, state_weight_grad = finished[:3]
    (
        stoch_gain_grad,
        stoch_bias_grad,
        post_gain_grad,
        post_bias_grad,
        prior_gain_grad,
        prior_bias_grad,
        post_shift_grad,
        prior_shift_grad,
        cell_gain_grad,
        cell_bias_grad,
    ) = [member.reshape(-1) for member in finished[3:13]]
    return (
        imag_deter,
        embed_grad.reshape(embed.shape),
        start_grad,
        stoch_table_grad,
        stoch_gain_grad,
        stoch_bias_grad,
        state_weight_grad,
        input_weight_grad,
        cell_gain_grad,
        cell_bias_grad,
        prior_hidden_grad,
        prior_gain_grad,
        prior_bias_grad,
        prior_out_grad,
        prior_shift_grad,
        post_deter_grad,
        post_embed_grad,
        post_gain_grad,
        post_bias_grad,
        post_out_grad,
        post_shift_grad,
        finished[13],
    )


def solution(mesh):
    both = ("seq", "rep")
    in_specs = (
        P(both, None),
        P(both, None, None),
        P(both, None, None),
        P(both),
        P(both, None),
        P(both, None, None),
        P(both, None, None),
    ) + (P(),) * 19
    rows, flat = P("rep", None), P("rep")
    out_specs = (
        P(both, None, None),
        P(both, None, None),
        P(both, None),
        rows,
        flat,
        flat,
        P("rep", None, None),
        rows,
        flat,
        flat,
        rows,
        flat,
        flat,
        rows,
        flat,
        rows,
        rows,
        flat,
        flat,
        rows,
        flat,
        P(None, "rep"),
    )
    return jax.shard_map(
        on_device, mesh=mesh, in_specs=in_specs, out_specs=out_specs, check_vma=False
    )
```
